512 devices in a mesh: row: 8 (over x, z_hi), col: 64 (over y, z_lo, core).
Axes of the slice: x: 4, y: 4, z: 16 (z_hi: 2, z_lo: 8; z = z_hi * 8 + z_lo), core: 2. Of those that a mesh axis runs over, the one named last changes fastest.
Arguments:
- features: bfloat16 [64, 1024, 128], P('col', 'row'), may hold values from -6 to 6
- weight: bfloat16 [128, 256], replicated, may hold values from -0.5 to 0.5
- upstream: bfloat16 [64, 1024, 256], P('col', 'row'), may hold values from -6 to 6
- tile_rows: int32 [8, 64, 64], P('row', 'col'), may hold values from 0 to 63
- tile_cols: int32 [8, 64, 64], P('row', 'col'), may hold values from 0 to 7
- tile_count: int32 [8, 64], P('row', 'col'), may hold values from 8 to 64, as said below
- edge_rows: int32 [8, 64, 64, 192], P('row', 'col'), may hold values from 0 to 127
- edge_cols: int32 [8, 64, 64, 192], P('row', 'col'), may hold values from 0 to 127
- edge_weight: bfloat16 [8, 64, 64, 192], P('row', 'col'), may hold values from 0.029907227 to 0.29882812
Outputs:
- out_act: bfloat16 [64, 1024, 256], P('col', 'row')
- grad_features: bfloat16 [64, 1024, 128], P('col', 'row')
- grad_weight: float32 [128, 256], replicated
The draws below stay inside these ranges and needn't reach their ends.
Inputs may be any that keep to these rules, and one draw needn't show every extreme that they name: `tile_count`: live slots of each block; exactly one block has all 64 slots live, the others at most half of them.
All inputs are finite; a program needn't handle non-finite values.
Results may differ from the reference program's by a relative error of at most 0.0061.
Values may be sent and summed in bfloat16 or wider, within the bound.
No kernel may reach another device: no remote copies, remote signals or barrier semaphores. Data moves between devices by JAX's collectives and lax.ppermute only.
A program may use at most 64 MiB of HBM per device.

```python
import math
import jax
import jax.numpy as jnp
from jax import lax

TILE = 128
F = 128
H = 256
NODE_DEV = 128
TILE_SLOTS = 64
TILE_EDGES = 192
COL_NODES = 1024
ROW_TILES = 64
COL_TILES = 8
NODES = 65536
N_ROW = 8
N_COL = 64


def draw_tile_count(key, part):
    key = jax.random.fold_in(key, 11)
    first_key, second_key = jax.random.split(key)
    counts = jax.random.randint(first_key, (N_ROW * N_COL,), TILE_SLOTS // 8, TILE_SLOTS // 2 + 1)
    chosen = jax.random.randint(second_key, (), 0, N_ROW * N_COL)
    counts = jnp.where(jnp.arange(N_ROW * N_COL) == chosen, TILE_SLOTS, counts)
    return counts.reshape(N_ROW, N_COL).astype(jnp.int32)


def set_ends(array, own_key, smallest, top_value):
    longest = array.shape.index(max(array.shape))
    spots = []
    for shift in (0, 1):
        where = [jax.random.randint(jax.random.fold_in(own_key, axis), (), 0, length) for axis, length in enumerate(array.shape)]
        where[longest] = (where[longest] + shift) % array.shape[longest]
        spots.append(tuple(where))
    return array.at[spots[0]].set(smallest).at[spots[1]].set(top_value)


def block_scale(rng, shape, pieces, least, high):
    loudness = 1.0
    for dim, blocks in pieces:
        steps = jax.random.uniform(jax.random.fold_in(jax.random.fold_in(rng, 6), dim), (blocks,), jnp.float32, least / len(pieces), high / len(pieces))
        loudness = loudness * jnp.repeat(jnp.exp(steps), shape[dim] // blocks).reshape((-1,) + (1,) * (len(shape) - 1 - dim))
    return loudness


def normal_values(own_key, extent, width, bound, cuts=(), kind=jnp.bfloat16):
    values = width * jax.random.normal(own_key, extent, jnp.float32)
    if cuts:
        values = values * block_scale(own_key, extent, cuts, -0.22, 0.18)
    return jnp.clip(values, -bound, bound).astype(kind)


def setup_inputs(seed: int = 0) -> dict:
    key_of = jax.random.split(jax.random.key(seed), 10)
    return {
        "features": normal_values(key_of[0], (N_COL, COL_NODES, F), 1.0, 6.0, ((0, 64), (1, 8))),
        "weight": normal_values(key_of[1], (F, H), F ** -0.5, 0.5),
        "upstream": normal_values(key_of[2], (N_COL, COL_NODES, H), 1.0, 6.0, ((0, 64), (1, 8))),
        "tile_rows": set_ends(jax.random.randint(key_of[3], (N_ROW, N_COL, TILE_SLOTS), 0, ROW_TILES), jax.random.fold_in(key_of[3], 1), 0, ROW_TILES - 1).astype(jnp.int32),
        "tile_cols": set_ends(jax.random.randint(key_of[4], (N_ROW, N_COL, TILE_SLOTS), 0, COL_TILES), jax.random.fold_in(key_of[4], 1), 0, COL_TILES - 1).astype(jnp.int32),
        "tile_count": draw_tile_count(jax.random.fold_in(key_of[9], 71), 0),
        "edge_rows": set_ends(jax.random.randint(key_of[6], (N_ROW, N_COL, TILE_SLOTS, TILE_EDGES), 0, TILE), jax.random.fold_in(key_of[6], 1), 0, TILE - 1).astype(jnp.int32),
        "edge_cols": set_ends(jax.random.randint(key_of[7], (N_ROW, N_COL, TILE_SLOTS, TILE_EDGES), 0, TILE), jax.random.fold_in(key_of[7], 1), 0, TILE - 1).astype(jnp.int32),
        "edge_weight": jnp.clip(jnp.exp(math.log(0.29882812) - 2.30176843 * jax.random.uniform(key_of[8], (N_ROW, N_COL, TILE_SLOTS, TILE_EDGES), jnp.float32) ** block_scale(key_of[8], (N_ROW, N_COL, TILE_SLOTS, TILE_EDGES), ((0, 8), (1, 64)), -0.2, 0.2)), 0.029907227, 0.29882812).astype(jnp.bfloat16),
    }


def densify(rows_now, cols_now, weights_now, live_count):
    slot_ids = jnp.arange(TILE_SLOTS, dtype=jnp.int32)
    is_live = (slot_ids < live_count).astype(jnp.float32)
    flat_index = (slot_ids[:, None] * (TILE * TILE) + rows_now * TILE + cols_now).reshape(-1)
    flat_values = (weights_now.astype(jnp.float32) * is_live[:, None]).reshape(-1)
    flat_tiles = jnp.zeros((TILE_SLOTS * TILE * TILE,), jnp.float32).at[flat_index].add(flat_values)
    return flat_tiles.reshape(TILE_SLOTS, TILE, TILE).astype(jnp.bfloat16).astype(jnp.float32)

def reference(features, weight, upstream, tile_rows, tile_cols, tile_count, edge_rows, edge_cols, edge_weight):
    feats = features.astype(jnp.float32)
    zero_index = jnp.int32(0)

    def forward_step(accum, device_id):
        row_id = device_id // N_COL
        col_id = device_id % N_COL
        dense_tiles = densify(edge_rows[row_id, col_id], edge_cols[row_id, col_id], edge_weight[row_id, col_id], tile_count[row_id, col_id])
        column = lax.dynamic_index_in_dim(feats, col_id, 0, keepdims=False).reshape(COL_TILES, TILE, F)
        picked = column[tile_cols[row_id, col_id]]
        products = jnp.einsum('kab,kbf->kaf', dense_tiles, picked)
        part_sum = jnp.zeros((ROW_TILES, TILE, F), jnp.float32).at[tile_rows[row_id, col_id]].add(products)
        part_sum = part_sum.reshape(N_COL, NODE_DEV, F)
        row_start = (row_id * NODE_DEV).astype(jnp.int32)
        before = lax.dynamic_slice(accum, (zero_index, row_start, zero_index), (N_COL, NODE_DEV, F))
        accum = lax.dynamic_update_slice(accum, before + part_sum, (zero_index, row_start, zero_index))
        return (accum, None)
    device_ids = jnp.arange(N_ROW * N_COL, dtype=jnp.int32)
    summed, _ = lax.scan(forward_step, jnp.zeros((N_COL, COL_NODES, F), jnp.float32), device_ids)
    aggregated = summed.astype(jnp.bfloat16)
    pre_act = jnp.einsum('jnf,fh->jnh', aggregated.astype(jnp.float32), weight.astype(jnp.float32))
    sigmoid_pre = jax.nn.sigmoid(pre_act)
    out_act = (pre_act * sigmoid_pre).astype(jnp.bfloat16)
    grad_pre = (upstream.astype(jnp.float32) * sigmoid_pre * (1.0 + pre_act * (1.0 - sigmoid_pre))).astype(jnp.bfloat16)
    grad_agg = jnp.einsum('jnh,fh->jnf', grad_pre.astype(jnp.float32), weight.astype(jnp.float32)).astype(jnp.bfloat16)
    grad_weight = jnp.einsum('jnf,jnh->fh', aggregated.astype(jnp.float32), grad_pre.astype(jnp.float32))
    grad_weight = grad_weight * jnp.float32(1.0 / math.sqrt(NODES))
    grad_rows = grad_agg.astype(jnp.float32)

    def backward_step(accum, device_id):
        row_id = device_id // N_COL
        col_id = device_id % N_COL
        dense_tiles = densify(edge_rows[row_id, col_id], edge_cols[row_id, col_id], edge_weight[row_id, col_id], tile_count[row_id, col_id])
        row_start = (row_id * NODE_DEV).astype(jnp.int32)
        row_block = lax.dynamic_slice(grad_rows, (zero_index, row_start, zero_index), (N_COL, NODE_DEV, F))
        row_block = row_block.reshape(ROW_TILES, TILE, F)
        picked = row_block[tile_rows[row_id, col_id]]
        products = jnp.einsum('kab,kaf->kbf', dense_tiles, picked)
        part_sum = jnp.zeros((COL_TILES, TILE, F), jnp.float32).at[tile_cols[row_id, col_id]].add(products)
        accum = accum.at[col_id].add(part_sum.reshape(COL_NODES, F))
        return (accum, None)
    back_sum, _ = lax.scan(backward_step, jnp.zeros((N_COL, COL_NODES, F), jnp.float32), device_ids)
    grad_features = back_sum.astype(jnp.bfloat16)
    return (out_act, grad_features, grad_weight)
```

```python
import math

import jax
import jax.numpy as jnp
from jax import lax
from jax.experimental import pallas as pl
from jax.experimental.pallas import tpu as pltpu
from jax.sharding import Mesh
from jax.sharding import PartitionSpec as P

TILE = 128
GROUP = 4
FINE = (("x", 4), ("zh", 2), ("y", 4), ("zl", 8), ("core", 2))
N_X, N_ZH, N_Y, N_ZL, N_CORE = (size for _, size in FINE)
ROW = ("x", "zh")
COL = ("y", "zl", "core")
W_ROWS = 32
VMEM_LIMIT = 48 * 1024 * 1024
BF16 = jnp.bfloat16
F32 = jnp.float32

vmem = pl.BlockSpec(memory_space=pltpu.VMEM)
smem = pl.BlockSpec(memory_space=pltpu.SMEM)
hbm = pl.BlockSpec(memory_space=pl.ANY)


def call(body, outs, in_specs, scratch=(), flops=0, moved=0):
    return pl.pallas_call(
        body,
        out_shape=outs,
        in_specs=in_specs,
        out_specs=jax.tree.map(lambda _: vmem, outs),
        scratch_shapes=list(scratch),
        compiler_params=pltpu.CompilerParams(vmem_limit_bytes=VMEM_LIMIT),
        cost_estimate=pl.CostEstimate(flops=flops, bytes_accessed=moved, transcendentals=0),
    )


def halves(value):
    high = value.astype(BF16)
    return high, (value - high.astype(F32)).astype(BF16)


def group_total(count_ref):
    return (count_ref[0, 0] + GROUP - 1) // GROUP


def build_body(count_ref, rows_ref, cols_ref, weight_ref, tiles_ref, live_ref):
    slots, edges = rows_ref.shape
    slot_ids = lax.broadcasted_iota(jnp.int32, (slots, edges), 0)
    live_ref[...] = jnp.where(slot_ids < count_ref[0, 0], weight_ref[...].astype(F32), 0.0)
    positions = lax.broadcasted_iota(jnp.int32, (TILE, edges), 0)

    def step(group, carry):
        for i in range(GROUP):
            slot = group * GROUP + i
            row_hot = jnp.where(positions == rows_ref[pl.ds(slot, 1), :], 1.0, 0.0).astype(BF16)
            col_hot = jnp.where(
                positions == cols_ref[pl.ds(slot, 1), :], live_ref[pl.ds(slot, 1), :], 0.0
            ).astype(BF16)
            built = lax.dot_general(
                row_hot, col_hot, (((1,), (1,)), ((), ())), preferred_element_type=F32
            )
            tiles_ref[slot] = built.astype(BF16)
        return carry

    lax.fori_loop(0, group_total(count_ref), step, 0)


def forward_body(count_ref, row_ref, col_ref, tiles_ref, feats_ref, out_ref, acc_ref):
    acc_ref[...] = jnp.zeros_like(acc_ref)
    half = acc_ref.shape[0] // N_CORE

    def step(group, carry):
        products = []
        for i in range(GROUP):
            slot = group * GROUP + i
            products.append(
                jnp.dot(tiles_ref[slot], feats_ref[col_ref[0, slot]], preferred_element_type=F32)
            )
        for i in range(GROUP):
            row = row_ref[0, group * GROUP + i]
            place = (row % N_CORE) * half + row // N_CORE
            acc_ref[place] += products[i]
        return carry

    lax.fori_loop(0, group_total(count_ref), step, 0)
    out_ref[...] = acc_ref[...].astype(BF16)


def dense_body(parts_ref, weight_ref, up_ref, act_ref, send_ref, *, scale):
    aggregated = jnp.sum(parts_ref[...].astype(F32), axis=0).astype(BF16)
    weight = weight_ref[...]
    pre_act = jnp.dot(aggregated, weight, preferred_element_type=F32)
    gate = jax.nn.sigmoid(pre_act)
    act_ref[...] = (pre_act * gate).astype(BF16)
    grad_pre = (up_ref[...].astype(F32) * gate * (1.0 + pre_act * (1.0 - gate))).astype(BF16)
    grad_agg = lax.dot_general(
        weight, grad_pre, (((1,), (1,)), ((), ())), preferred_element_type=F32
    ).astype(BF16)
    local_weight = (
        lax.dot_general(aggregated, grad_pre, (((0,), (0,)), ((), ())), preferred_element_type=F32)
        * scale
    )
    deep = TILE // N_ZL
    high, low = halves(local_weight)
    for peer in range(N_ZL):
        send_ref[peer, 0:TILE, :] = grad_agg
        here = slice(peer * deep, (peer + 1) * deep)
        for k, part in enumerate(
            (high[here, :TILE], high[here, TILE:], low[here, :TILE], low[here, TILE:])
        ):
            send_ref[peer, TILE + k * deep : TILE + (k + 1) * deep, :] = part


def spread_body(got_ref, send_ref):
    terms = jnp.sum(got_ref[:, TILE:, :].astype(F32), axis=0)
    high, low = halves(terms[:W_ROWS] + terms[W_ROWS:])
    for peer in range(N_Y):
        for k in range(N_ZL):
            send_ref[peer, k * TILE : (k + 1) * TILE, :] = got_ref[k, 0:TILE, :]
        send_ref[peer, N_ZL * TILE : N_ZL * TILE + W_ROWS, :] = high
        send_ref[peer, N_ZL * TILE + W_ROWS :, :] = low


def backward_body(
    count_ref, core_ref, row_ref, col_ref, tiles_ref, own_ref, other_ref, send_ref, grads_ref, acc_ref, sems
):
    core = core_ref[0]
    copies = [
        pltpu.make_async_copy(own_ref, grads_ref.at[core], sems.at[0]),
        pltpu.make_async_copy(other_ref, grads_ref.at[1 - core], sems.at[1]),
    ]
    for copy in copies:
        copy.start()
    acc_ref[...] = jnp.zeros_like(acc_ref)
    for copy in copies:
        copy.wait()

    def step(group, carry):
        products = []
        for i in range(GROUP):
            slot = group * GROUP + i
            row = row_ref[0, slot]
            start = pl.multiple_of(row // N_CORE % N_ZL * TILE, TILE)
            grad = grads_ref[row % N_CORE, row // (N_CORE * N_ZL), pl.ds(start, TILE), :]
            products.append(jnp.dot(grad, tiles_ref[slot], preferred_element_type=F32))
        for i in range(GROUP):
            acc_ref[col_ref[0, group * GROUP + i]] += products[i]
        return carry

    lax.fori_loop(0, group_total(count_ref), step, 0)
    terms = jnp.sum(grads_ref[:, :, N_ZL * TILE :, :].astype(F32), axis=(0, 1))
    high, low = halves(terms[:W_ROWS] + terms[W_ROWS:])
    for x in range(N_X):
        for zh in range(N_ZH):
            send_ref[x, zh * TILE : (zh + 1) * TILE, :] = acc_ref[x * N_ZH + zh].astype(BF16)
        send_ref[x, N_ZH * TILE : N_ZH * TILE + W_ROWS, :] = high
        send_ref[x, N_ZH * TILE + W_ROWS :, :] = low


def halfway_body(zh_ref, got_ref, send_ref, keep_ref, keep_weight_ref):
    zh = zh_ref[0]
    total = jnp.sum(got_ref[...].astype(F32), axis=0)
    first, second = total[:TILE], total[TILE : 2 * TILE]
    mine = zh == 0
    keep_ref[...] = jnp.where(mine, first, second)
    terms = total[2 * TILE :]
    weight_sum = terms[:W_ROWS] + terms[W_ROWS:]
    keep_weight_ref[...] = weight_sum
    high, low = halves(weight_sum)
    send_ref[0:TILE, :] = jnp.where(mine, second, first).astype(BF16)
    send_ref[TILE : TILE + W_ROWS, :] = high
    send_ref[TILE + W_ROWS :, :] = low


def finish_body(got_ref, keep_ref, keep_weight_ref, grad_ref, send_ref):
    grad_ref[...] = (keep_ref[...] + got_ref[0:TILE, :].astype(F32)).T.astype(BF16)
    terms = got_ref[TILE:, :].astype(F32)
    total = keep_weight_ref[...] + (terms[:W_ROWS] + terms[W_ROWS:])
    for peer in range(N_ZL):
        send_ref[peer] = total


def swap(value, axis):
    return lax.ppermute(value, axis, [(0, 1), (1, 0)])


def exchange(value, axis):
    return lax.all_to_all(value, axis, 0, 0, tiled=True)


def local(
    features, weight, upstream, tile_rows, tile_cols, tile_count, edge_rows, edge_cols, edge_weight
):
    width = features.shape[2]
    hidden = weight.shape[1]
    slots, edges = edge_rows.shape[2:]
    row_tiles, col_tiles = tile_rows[0], tile_cols[0]
    blocks = N_Y * N_ZL * N_CORE
    shape = jax.ShapeDtypeStruct

    zh = lax.axis_index("zh")
    own = features[0]
    other = swap(own, "zh")
    pair = jnp.where(zh == 0, jnp.stack([own, other]), jnp.stack([other, own]))
    column = lax.all_gather(pair, "x", axis=0, tiled=True)

    tiles = call(
        build_body,
        shape((slots, TILE, TILE), BF16),
        [smem, vmem, vmem, vmem],
        [pltpu.VMEM((slots, edges), F32)],
        flops=slots * TILE * TILE * edges * 8,
        moved=slots * TILE * TILE * 2,
    )(tile_count, edge_rows[0, 0], edge_cols[0, 0], edge_weight[0, 0])

    partial = call(
        forward_body,
        shape((blocks, TILE, width), BF16),
        [smem, smem, smem, vmem, vmem],
        [pltpu.VMEM((blocks, TILE, width), F32)],
        flops=slots * TILE * TILE * width * 2,
        moved=slots * TILE * TILE * 4,
    )(tile_count, row_tiles, col_tiles, tiles, column)

    for axis, size in (("core", N_CORE), ("y", N_Y)):
        got = exchange(partial, axis)
        got = got.reshape((size, -1) + got.shape[1:])
        partial = jnp.sum(got.astype(F32), axis=0).astype(BF16)
    parts = exchange(partial, "zl")

    node_total = features.shape[1] * N_X * N_ZH * blocks
    scale = 1.0 / math.sqrt(node_total)

    def dense(*refs):
        dense_body(*refs, scale=scale)

    out_act, send = call(
        dense,
        (shape((TILE, hidden), BF16), shape((N_ZL, TILE + 2 * W_ROWS, TILE), BF16)),
        [vmem] * 3,
    )(parts, weight, upstream[0])

    got = exchange(send, "zl")
    send = call(spread_body, shape((N_Y, N_ZL * TILE + 2 * W_ROWS, TILE), BF16), [vmem])(got)
    mine = exchange(send, "y")
    theirs = swap(mine, "core")
    send = call(
        backward_body,
        shape((N_X, N_ZH * TILE + 2 * W_ROWS, TILE), BF16),
        [smem, smem, smem, smem, vmem, hbm, hbm],
        [
            pltpu.VMEM((N_CORE,) + mine.shape, BF16),
            pltpu.VMEM((N_X * N_ZH, width, TILE), F32),
            pltpu.SemaphoreType.DMA((2,)),
        ],
    )(
        tile_count,
        lax.axis_index("core").astype(jnp.int32)[None],
        row_tiles,
        col_tiles,
        tiles,
        mine,
        theirs,
    )

    got = exchange(send, "x")
    send, keep, keep_weight = call(
        halfway_body,
        (
            shape((TILE + 2 * W_ROWS, TILE), BF16),
            shape((TILE, TILE), F32),
            shape((W_ROWS, TILE), F32),
        ),
        [smem, vmem],
    )(zh.astype(jnp.int32)[None], got)
    got = swap(send, "zh")
    grad_features, send = call(
        finish_body,
        (shape((TILE, width), BF16), shape((N_ZL, W_ROWS, TILE), F32)),
        [vmem] * 3,
    )(got, keep, keep_weight)
    got = exchange(send, "zl")
    grad_weight = got.reshape(N_ZL, hidden // TILE, -1, TILE).transpose(0, 2, 1, 3)
    grad_weight = grad_weight.reshape(width, hidden)
    return (out_act[None], grad_features[None], grad_weight)


def solution(mesh):
    fine = Mesh(mesh.devices.reshape([size for _, size in FINE]), [name for name, _ in FINE])
    in_specs = (
        P(COL, ROW, None),
        P(),
        P(COL, ROW, None),
        P(ROW, COL, None),
        P(ROW, COL, None),
        P(ROW, COL),
        P(ROW, COL, None, None),
        P(ROW, COL, None, None),
        P(ROW, COL, None, None),
    )
    out_specs = (P(COL, ROW, None), P(COL, ROW, None), P())
    return jax.shard_map(local, mesh=fine, in_specs=in_specs, out_specs=out_specs, check_vma=False)
```

```python
import math

import jax
import jax.numpy as jnp
from jax import lax
from jax.experimental import pallas as pl
from jax.experimental.pallas import tpu as pltpu
from jax.sharding import Mesh
from jax.sharding import PartitionSpec as P

TILE = 128
GROUP = 4
FINE = (("x", 4), ("zh", 2), ("y", 4), ("zl", 8), ("core", 2))
N_X, N_ZH, N_Y, N_ZL, N_CORE = (size for _, size in FINE)
ROW = ("x", "zh")
COL = ("y", "zl", "core")
W_ROWS = 32
VMEM_LIMIT = 48 * 1024 * 1024
BF16 = jnp.bfloat16
F32 = jnp.float32

vmem = pl.BlockSpec(memory_space=pltpu.VMEM)
smem = pl.BlockSpec(memory_space=pltpu.SMEM)
hbm = pl.BlockSpec(memory_space=pl.ANY)


def call(body, outs, in_specs, scratch=(), flops=0, moved=0):
    return pl.pallas_call(
        body,
        out_shape=outs,
        in_specs=in_specs,
        out_specs=jax.tree.map(lambda _: vmem, outs),
        scratch_shapes=list(scratch),
        compiler_params=pltpu.CompilerParams(vmem_limit_bytes=VMEM_LIMIT),
        cost_estimate=pl.CostEstimate(flops=flops, bytes_accessed=moved, transcendentals=0),
    )


def halves(value):
    high = value.astype(BF16)
    return high, (value - high.astype(F32)).astype(BF16)


def group_total(count_ref):
    return (count_ref[0, 0] + GROUP - 1) // GROUP


def build_body(count_ref, rows_ref, cols_ref, weight_ref, tiles_ref, live_ref):
    slots, edges = rows_ref.shape
    slot_ids = lax.broadcasted_iota(jnp.int32, (slots, edges), 0)
    live_ref[...] = jnp.where(slot_ids < count_ref[0, 0], weight_ref[...].astype(F32), 0.0)
    positions = lax.broadcasted_iota(jnp.int32, (TILE, edges), 0)

    def step(group, carry):
        for i in range(GROUP):
            slot = group * GROUP + i
            row_hot = jnp.where(positions == rows_ref[pl.ds(slot, 1), :], 1.0, 0.0).astype(BF16)
            col_hot = jnp.where(
                positions == cols_ref[pl.ds(slot, 1), :], live_ref[pl.ds(slot, 1), :], 0.0
            ).astype(BF16)
            built = lax.dot_general(
                row_hot, col_hot, (((1,), (1,)), ((), ())), preferred_element_type=F32
            )
            tiles_ref[slot] = built.astype(BF16)
        return carry

    lax.fori_loop(0, group_total(count_ref), step, 0)


def forward_body(
    count_ref, core_ref, row_ref, col_ref, tiles_ref, feats_ref, send_ref, keep_ref, acc_ref
):
    acc_ref[...] = jnp.zeros_like(acc_ref)
    core = core_ref[0]

    def step(group, carry):
        products = []
        for i in range(GROUP):
            slot = group * GROUP + i
            products.append(
                jnp.dot(tiles_ref[slot], feats_ref[col_ref[0, slot]], preferred_element_type=F32)
            )
        for i in range(GROUP):
            row = row_ref[0, group * GROUP + i]
            acc_ref[row % N_CORE, row // N_CORE] += products[i]
        return carry

    lax.fori_loop(0, group_total(count_ref), step, 0)
    send_ref[...] = acc_ref[1 - core].astype(BF16)
    keep_ref[...] = acc_ref[core]


def merge_body(got_ref, keep_ref, out_ref):
    out_ref[...] = (keep_ref[...] + got_ref[...].astype(F32)).astype(BF16)


def dense_body(parts_ref, weight_ref, up_ref, act_ref, send_ref, *, scale):
    aggregated = jnp.sum(parts_ref[...].astype(F32), axis=0).astype(BF16)
    weight = weight_ref[...]
    pre_act = jnp.dot(aggregated, weight, preferred_element_type=F32)
    gate = jax.nn.sigmoid(pre_act)
    act_ref[...] = (pre_act * gate).astype(BF16)
    grad_pre = (up_ref[...].astype(F32) * gate * (1.0 + pre_act * (1.0 - gate))).astype(BF16)
    grad_agg = lax.dot_general(
        weight, grad_pre, (((1,), (1,)), ((), ())), preferred_element_type=F32
    ).astype(BF16)
    local_weight = (
        lax.dot_general(aggregated, grad_pre, (((0,), (0,)), ((), ())), preferred_element_type=F32)
        * scale
    )
    deep = TILE // N_ZL
    local_weight = local_weight.astype(BF16)
    for peer in range(N_ZL):
        send_ref[peer, 0:TILE, :] = grad_agg
        here = slice(peer * deep, (peer + 1) * deep)
        send_ref[peer, TILE : TILE + deep, :] = local_weight[here, :TILE]
        send_ref[peer, TILE + deep :, :] = local_weight[here, TILE:]


def spread_body(got_ref, send_ref):
    high, low = halves(jnp.sum(got_ref[:, TILE:, :].astype(F32), axis=0))
    for peer in range(N_Y):
        for k in range(N_ZL):
            send_ref[peer, k * TILE : (k + 1) * TILE, :] = got_ref[k, 0:TILE, :]
        send_ref[peer, N_ZL * TILE : N_ZL * TILE + W_ROWS, :] = high
        send_ref[peer, N_ZL * TILE + W_ROWS :, :] = low


def backward_body(
    count_ref, core_ref, row_ref, col_ref, tiles_ref, own_ref, other_ref, send_ref, grads_ref, acc_ref, sems
):
    core = core_ref[0]
    copies = [
        pltpu.make_async_copy(own_ref, grads_ref.at[core], sems.at[0]),
        pltpu.make_async_copy(other_ref, grads_ref.at[1 - core], sems.at[1]),
    ]
    for copy in copies:
        copy.start()
    acc_ref[...] = jnp.zeros_like(acc_ref)
    for copy in copies:
        copy.wait()

    def step(group, carry):
        products = []
        for i in range(GROUP):
            slot = group * GROUP + i
            row = row_ref[0, slot]
            start = pl.multiple_of(row // N_CORE % N_ZL * TILE, TILE)
            grad = grads_ref[row % N_CORE, row // (N_CORE * N_ZL), pl.ds(start, TILE), :]
            products.append(jnp.dot(grad, tiles_ref[slot], preferred_element_type=F32))
        for i in range(GROUP):
            acc_ref[col_ref[0, group * GROUP + i]] += products[i]
        return carry

    lax.fori_loop(0, group_total(count_ref), step, 0)
    terms = jnp.sum(grads_ref[:, :, N_ZL * TILE :, :].astype(F32), axis=(0, 1))
    high, low = halves(terms[:W_ROWS] + terms[W_ROWS:])
    for x in range(N_X):
        for zh in range(N_ZH):
            send_ref[x, zh * TILE : (zh + 1) * TILE, :] = acc_ref[x * N_ZH + zh].astype(BF16)
        send_ref[x, N_ZH * TILE : N_ZH * TILE + W_ROWS, :] = high
        send_ref[x, N_ZH * TILE + W_ROWS :, :] = low


def halfway_body(zh_ref, got_ref, send_ref, keep_ref, send_weight_ref):
    zh = zh_ref[0]
    total = jnp.sum(got_ref[...].astype(F32), axis=0)
    first, second = total[:TILE], total[TILE : 2 * TILE]
    mine = zh == 0
    keep_ref[...] = jnp.where(mine, first, second)
    send_ref[...] = jnp.where(mine, second, first).astype(BF16)
    terms = total[2 * TILE :]
    weight_sum = (terms[:W_ROWS] + terms[W_ROWS:]).astype(BF16)
    for peer in range(N_ZH * N_ZL):
        send_weight_ref[peer] = weight_sum


def finish_body(got_ref, keep_ref, got_weight_ref, grad_ref, grad_weight_ref):
    grad_ref[...] = (keep_ref[...] + got_ref[...].astype(F32)).T.astype(BF16)
    deep = TILE // N_ZL
    for k in range(N_ZL):
        total = got_weight_ref[k].astype(F32) + got_weight_ref[N_ZL + k].astype(F32)
        grad_weight_ref[k * deep : (k + 1) * deep, :TILE] = total[:deep]
        grad_weight_ref[k * deep : (k + 1) * deep, TILE:] = total[deep:]


def swap(value, axis):
    return lax.ppermute(value, axis, [(0, 1), (1, 0)])


def exchange(value, axis):
    return lax.all_to_all(value, axis, 0, 0, tiled=True)


def local(
    features, weight, upstream, tile_rows, tile_cols, tile_count, edge_rows, edge_cols, edge_weight
):
    width = features.shape[2]
    hidden = weight.shape[1]
    slots, edges = edge_rows.shape[2:]
    row_tiles, col_tiles = tile_rows[0], tile_cols[0]
    blocks = N_Y * N_ZL * N_CORE
    shape = jax.ShapeDtypeStruct

    zh = lax.axis_index("zh")
    own = features[0]
    other = swap(own, "zh")
    pair = jnp.where(zh == 0, jnp.stack([own, other]), jnp.stack([other, own]))
    pair = jnp.broadcast_to(pair[None], (N_X,) + pair.shape)
    column = exchange(pair, "x").reshape(N_X * N_ZH, TILE, width)

    tiles = call(
        build_body,
        shape((slots, TILE, TILE), BF16),
        [smem, vmem, vmem, vmem],
        [pltpu.VMEM((slots, edges), F32)],
        flops=slots * TILE * TILE * edges * 8,
        moved=slots * TILE * TILE * 2,
    )(tile_count, edge_rows[0, 0], edge_cols[0, 0], edge_weight[0, 0])

    core = lax.axis_index("core").astype(jnp.int32)[None]
    half = (blocks // N_CORE, TILE, width)
    send, keep = call(
        forward_body,
        (shape(half, BF16), shape(half, F32)),
        [smem, smem, smem, smem, vmem, vmem],
        [pltpu.VMEM((N_CORE,) + half, F32)],
        flops=slots * TILE * TILE * width * 2,
        moved=slots * TILE * TILE * 4,
    )(tile_count, core, row_tiles, col_tiles, tiles, column)

    partial = call(merge_body, shape(half, BF16), [vmem, vmem])(swap(send, "core"), keep)
    got = exchange(partial, "y").reshape((N_Y, N_ZL, TILE, width))
    partial = jnp.sum(got.astype(F32), axis=0).astype(BF16)
    parts = exchange(partial, "zl")

    node_total = features.shape[1] * N_X * N_ZH * blocks
    scale = 1.0 / math.sqrt(node_total)

    def dense(*refs):
        dense_body(*refs, scale=scale)

    out_act, send = call(
        dense,
        (shape((TILE, hidden), BF16), shape((N_ZL, TILE + W_ROWS, TILE), BF16)),
        [vmem] * 3,
    )(parts, weight, upstream[0])

    got = exchange(send, "zl")
    send = call(spread_body, shape((N_Y, N_ZL * TILE + 2 * W_ROWS, TILE), BF16), [vmem])(got)
    mine = exchange(send, "y")
    theirs = swap(mine, "core")
    send = call(
        backward_body,
        shape((N_X, N_ZH * TILE + 2 * W_ROWS, TILE), BF16),
        [smem, smem, smem, smem, vmem, hbm, hbm],
        [
            pltpu.VMEM((N_CORE,) + mine.shape, BF16),
            pltpu.VMEM((N_X * N_ZH, width, TILE), F32),
            pltpu.SemaphoreType.DMA((2,)),
        ],
    )(
        tile_count,
        core,
        row_tiles,
        col_tiles,
        tiles,
        mine,
        theirs,
    )

    got = exchange(send, "x")
    send, keep, send_weight = call(
        halfway_body,
        (
            shape((TILE, TILE), BF16),
            shape((TILE, TILE), F32),
            shape((N_ZH * N_ZL, W_ROWS, TILE), BF16),
        ),
        [smem, vmem],
    )(zh.astype(jnp.int32)[None], got)
    got = swap(send, "zh")
    got_weight = exchange(send_weight, ("zh", "zl"))
    grad_features, grad_weight = call(
        finish_body,
        (shape((TILE, width), BF16), shape((width, hidden), F32)),
        [vmem] * 3,
    )(got, keep, got_weight)
    return (out_act[None], grad_features[None], grad_weight)


def solution(mesh):
    fine = Mesh(mesh.devices.reshape([size for _, size in FINE]), [name for name, _ in FINE])
    in_specs = (
        P(COL, ROW, None),
        P(),
        P(COL, ROW, None),
        P(ROW, COL, None),
        P(ROW, COL, None),
        P(ROW, COL),
        P(ROW, COL, None, None),
        P(ROW, COL, None, None),
        P(ROW, COL, None, None),
    )
    out_specs = (P(COL, ROW, None), P(COL, ROW, None), P())
    return jax.shard_map(local, mesh=fine, in_specs=in_specs, out_specs=out_specs, check_vma=False)
```

```python
import functools
import math

import jax
import jax.numpy as jnp
from jax import lax
from jax.experimental import pallas as pl
from jax.experimental.pallas import tpu as pltpu
from jax.sharding import Mesh
from jax.sharding import PartitionSpec as P

TILE = 128
GROUP = 4
FINE = (("x", 4), ("zh", 2), ("y", 4), ("zl", 8), ("core", 2))
N_X, N_ZH, N_Y, N_ZL, N_CORE = (size for _, size in FINE)
ROW = ("x", "zh")
COL = ("y", "zl", "core")
LISTS = N_Y * N_CORE
PLANE = N_X * N_Y
W_ROWS = 32
BF16 = jnp.bfloat16
F32 = jnp.float32
I32 = jnp.int32

vmem = pl.BlockSpec(memory_space=pltpu.VMEM)
smem = pl.BlockSpec(memory_space=pltpu.SMEM)
shape = jax.ShapeDtypeStruct


def call(body, outs, in_specs, out_specs=None, scratch=(), flops=0, moved=0, limit=24):
    return pl.pallas_call(
        body,
        out_shape=outs,
        in_specs=in_specs,
        out_specs=jax.tree.map(lambda _: vmem, outs) if out_specs is None else out_specs,
        scratch_shapes=list(scratch),
        compiler_params=pltpu.CompilerParams(vmem_limit_bytes=limit * 1024 * 1024),
        cost_estimate=pl.CostEstimate(flops=flops, bytes_accessed=moved, transcendentals=0),
    )


def halves(value):
    high = value.astype(BF16)
    return high, (value - high.astype(F32)).astype(BF16)


def pack_body(rows_ref, cols_ref, weight_ref, row_ref, col_ref, count_ref, send_ref):
    slots, edges = rows_ref.shape
    rows = rows_ref[...].astype(F32)
    cols = cols_ref[...].astype(F32)
    weight = weight_ref[...].astype(F32)
    line = lax.broadcasted_iota(I32, (slots, slots), 0)
    meta = jnp.where(line == 0, row_ref[...], jnp.where(line == 1, col_ref[...], count_ref[0, 0]))
    blocks = (
        rows[:, :TILE],
        cols[:, :TILE],
        weight[:, :TILE],
        jnp.concatenate([rows[:, TILE:], cols[:, TILE:]], axis=1),
        jnp.concatenate([weight[:, TILE:], meta.astype(F32)], axis=1),
    )
    for k, block in enumerate(blocks):
        block = block.astype(BF16)
        for peer in range(send_ref.shape[0]):
            send_ref[peer, k * slots : (k + 1) * slots, :] = block


def build_body(
    where_ref, got_ref, tiles_ref, zl_ref, src_ref, total_ref,
    slot_ref, edge_rows_ref, edge_cols_ref, weight_ref, meta_ref, slots_ref, sem,
):
    y, core = where_ref[0], where_ref[1]
    slots = got_ref.shape[1] // 5
    edges = edge_rows_ref.shape[1]
    rest = edges - TILE
    dummy = LISTS * slots
    for index in range(LISTS):
        meta = got_ref[index, 4 * slots : 4 * slots + 16, :].astype(F32)
        meta_ref[index * 8 : (index + 1) * 8, :] = meta[:8].astype(I32)
    copy = pltpu.make_async_copy(meta_ref, slots_ref, sem)
    copy.start()
    for index in range(LISTS):
        here = slice(index * slots, (index + 1) * slots)
        block = [got_ref[index, k * slots : (k + 1) * slots, :].astype(F32) for k in range(5)]
        edge_rows_ref[here, :TILE] = block[0]
        edge_cols_ref[here, :TILE] = block[1]
        weight_ref[here, :TILE] = block[2]
        edge_rows_ref[here, TILE:] = block[3][:, :rest]
        edge_cols_ref[here, TILE:] = block[3][:, rest:]
        weight_ref[here, TILE:] = block[4][:, :rest]
    for ref in (edge_rows_ref, edge_cols_ref, weight_ref):
        ref[dummy:, :] = jnp.zeros_like(ref[dummy:, :])
    copy.wait()

    used = jnp.int32(0)
    for part in range(N_CORE):
        column_core = core if part == 0 else 1 - core
        for column_y in range(N_Y):
            index = column_y * N_CORE + column_core

            def scan(slot, used, index=index, column_y=column_y):
                row, col = slots_ref[index * 8, rest + slot], slots_ref[index * 8 + 1, rest + slot]
                slot_ref[used] = index * slots + slot
                zl_ref[used] = row // N_CORE % N_ZL
                src_ref[used] = (col // N_ZH * N_Y + column_y) * N_ZH + col % N_ZH
                mine = (row // (N_CORE * N_ZL) == y) & (row % N_CORE == core)
                return used + mine.astype(I32)

            used = lax.fori_loop(0, slots_ref[index * 8 + 2, rest], scan, used)
        for extra in range(GROUP - 1):
            slot_ref[used + extra] = dummy
            zl_ref[used + extra] = 0
            src_ref[used + extra] = 0
        used = (used + GROUP - 1) // GROUP * GROUP
        total_ref[part] = used

    positions = lax.broadcasted_iota(I32, (TILE, edges), 0).astype(F32)

    def step(group, carry):
        for i in range(GROUP):
            entry = group * GROUP + i
            slot = slot_ref[entry]
            row_hot = jnp.where(positions == edge_rows_ref[pl.ds(slot, 1), :], 1.0, 0.0)
            col_hot = jnp.where(
                positions == edge_cols_ref[pl.ds(slot, 1), :], weight_ref[pl.ds(slot, 1), :], 0.0
            )
            built = lax.dot_general(
                row_hot.astype(BF16),
                col_hot.astype(BF16),
                (((1,), (1,)), ((), ())),
                preferred_element_type=F32,
            )
            tiles_ref[entry] = built.astype(BF16)
        return carry

    lax.fori_loop(0, used // GROUP, step, 0)


def forward_body(total_ref, zl_ref, src_ref, tiles_ref, own_ref, other_ref, send_ref, acc_ref):
    acc_ref[...] = jnp.zeros_like(acc_ref)

    def step(feats_ref, group, carry):
        products = []
        for i in range(GROUP):
            entry = group * GROUP + i
            products.append(
                jnp.dot(tiles_ref[entry], feats_ref[src_ref[entry]], preferred_element_type=F32)
            )
        for i in range(GROUP):
            acc_ref[zl_ref[group * GROUP + i]] += products[i]
        return carry

    middle, end = total_ref[0] // GROUP, total_ref[1] // GROUP
    lax.fori_loop(0, middle, functools.partial(step, own_ref), 0)
    lax.fori_loop(middle, end, functools.partial(step, other_ref), 0)
    send_ref[...] = acc_ref[...].astype(BF16)


def dense_body(parts_ref, weight_ref, up_ref, act_ref, send_ref, *, scale):
    aggregated = jnp.sum(parts_ref[...].astype(F32), axis=0).astype(BF16)
    weight = weight_ref[...]
    pre_act = jnp.dot(aggregated, weight, preferred_element_type=F32)
    gate = jax.nn.sigmoid(pre_act)
    act_ref[...] = (pre_act * gate).astype(BF16)
    grad_pre = (up_ref[...].astype(F32) * gate * (1.0 + pre_act * (1.0 - gate))).astype(BF16)
    grad_agg = lax.dot_general(
        weight, grad_pre, (((1,), (1,)), ((), ())), preferred_element_type=F32
    ).astype(BF16)
    local_weight = (
        lax.dot_general(aggregated, grad_pre, (((0,), (0,)), ((), ())), preferred_element_type=F32)
        * scale
    ).astype(BF16)
    deep = TILE // N_ZL
    for peer in range(N_ZL):
        send_ref[peer, 0:TILE, :] = grad_agg
        here = slice(peer * deep, (peer + 1) * deep)
        send_ref[peer, TILE : TILE + deep, :] = local_weight[here, :TILE]
        send_ref[peer, TILE + deep :, :] = local_weight[here, TILE:]


def backward_body(
    total_ref, zl_ref, src_ref, tiles_ref, got_ref, send_ref, keep_ref, keep_weight_ref, acc_ref
):
    acc_ref[...] = jnp.zeros_like(acc_ref)

    def step(part, group, carry):
        products = []
        for i in range(GROUP):
            entry = group * GROUP + i
            grad = got_ref[zl_ref[entry], 0:TILE, :]
            products.append(jnp.dot(grad, tiles_ref[entry], preferred_element_type=F32))
        for i in range(GROUP):
            acc_ref[part, src_ref[group * GROUP + i]] += products[i]
        return carry

    middle, end = total_ref[0] // GROUP, total_ref[1] // GROUP
    lax.fori_loop(0, middle, functools.partial(step, 0), 0)
    lax.fori_loop(middle, end, functools.partial(step, 1), 0)
    keep_ref[...] = acc_ref[0]
    tiles = acc_ref.shape[1]
    send_ref[0:tiles] = acc_ref[1].astype(BF16)
    weight_sum = jnp.sum(got_ref[:, TILE:, :].astype(F32), axis=0)
    keep_weight_ref[...] = weight_sum
    high, low = halves(weight_sum)
    send_ref[tiles, 0:W_ROWS, :] = high
    send_ref[tiles, W_ROWS : 2 * W_ROWS, :] = low
    send_ref[tiles, 2 * W_ROWS :, :] = jnp.zeros_like(send_ref[tiles, 2 * W_ROWS :, :])


def merge_body(got_ref, keep_ref, keep_weight_ref, send_ref):
    tiles = keep_ref.shape[0]
    terms = got_ref[tiles, 0 : 2 * W_ROWS, :].astype(F32)
    high, low = halves(keep_weight_ref[...] + (terms[:W_ROWS] + terms[W_ROWS:]))
    for peer in range(PLANE):
        for zh in range(N_ZH):
            tile = peer * N_ZH + zh
            send_ref[peer, zh * TILE : (zh + 1) * TILE, :] = (
                keep_ref[tile] + got_ref[tile].astype(F32)
            ).astype(BF16)
        send_ref[peer, N_ZH * TILE : N_ZH * TILE + W_ROWS, :] = high
        send_ref[peer, N_ZH * TILE + W_ROWS :, :] = low


def halfway_body(zh_ref, got_ref, send_ref, keep_ref, send_weight_ref):
    zh = zh_ref[0]
    total = jnp.sum(got_ref[...].astype(F32), axis=0)
    first, second = total[:TILE], total[TILE : 2 * TILE]
    mine = zh == 0
    keep_ref[...] = jnp.where(mine, first, second)
    send_ref[...] = jnp.where(mine, second, first).astype(BF16)
    terms = total[2 * TILE :]
    weight_sum = (terms[:W_ROWS] + terms[W_ROWS:]).astype(BF16)
    for peer in range(N_ZH * N_ZL):
        send_weight_ref[peer] = weight_sum


def finish_body(got_ref, keep_ref, got_weight_ref, grad_ref, grad_weight_ref):
    grad_ref[...] = (keep_ref[...] + got_ref[...].astype(F32)).T.astype(BF16)
    deep = TILE // N_ZL
    for k in range(N_ZL):
        total = got_weight_ref[k].astype(F32) + got_weight_ref[N_ZL + k].astype(F32)
        grad_weight_ref[k * deep : (k + 1) * deep, :TILE] = total[:deep]
        grad_weight_ref[k * deep : (k + 1) * deep, TILE:] = total[deep:]


def swap(value, axis):
    return lax.ppermute(value, axis, [(0, 1), (1, 0)])


def exchange(value, axis):
    return lax.all_to_all(value, axis, 0, 0, tiled=True)


def local(
    features, weight, upstream, tile_rows, tile_cols, tile_count, edge_rows, edge_cols, edge_weight
):
    width = features.shape[2]
    hidden = weight.shape[1]
    slots, edges = edge_rows.shape[2:]
    column_tiles = PLANE * N_ZH
    most = slots + (LISTS - 1) * slots // 2 + 2 * GROUP
    zh = lax.axis_index("zh")
    where = jnp.stack([lax.axis_index("y"), lax.axis_index("core")]).astype(I32)

    own = features[0]
    other = swap(own, "zh")

    send = call(pack_body, shape((LISTS, 5 * slots, TILE), BF16), [vmem] * 5 + [smem])(
        edge_rows[0, 0], edge_cols[0, 0], edge_weight[0, 0], tile_rows[0], tile_cols[0], tile_count
    )
    lists = exchange(send, ("y", "core"))
    other, lists = lax.optimization_barrier((other, lists))
    tiles, zl_list, src_list, total = call(
        build_body,
        (
            shape((most, TILE, TILE), BF16),
            shape((most,), I32),
            shape((most,), I32),
            shape((N_CORE,), I32),
        ),
        [smem, vmem],
        (vmem, smem, smem, smem),
        [pltpu.SMEM((most,), I32)]
        + [pltpu.VMEM((LISTS * slots + 8, edges), F32)] * 3
        + [
            pltpu.VMEM((LISTS * 8, TILE), I32),
            pltpu.SMEM((LISTS * 8, TILE), I32),
            pltpu.SemaphoreType.DMA,
        ],
        flops=slots * TILE * TILE * edges * 4,
        moved=slots * TILE * TILE * 2,
    )(where, lists)

    pair = jnp.where(zh == 0, jnp.stack([own, other]), jnp.stack([other, own]))
    pair = jnp.broadcast_to(pair[None], (PLANE,) + pair.shape)
    mine = exchange(pair, ("x", "y")).reshape(column_tiles, TILE, width)
    theirs = swap(mine, "core")

    partial = call(
        forward_body,
        shape((N_ZL, TILE, width), BF16),
        [smem] * 3 + [vmem] * 3,
        scratch=[pltpu.VMEM((N_ZL, TILE, width), F32)],
    )(total, zl_list, src_list, tiles, mine, theirs)

    parts = exchange(partial, "zl")

    node_total = features.shape[1] * N_X * N_ZH * N_Y * N_ZL * N_CORE
    out_act, send = call(
        functools.partial(dense_body, scale=1.0 / math.sqrt(node_total)),
        (shape((TILE, hidden), BF16), shape((N_ZL, TILE + W_ROWS, TILE), BF16)),
        [vmem] * 3,
    )(parts, weight, upstream[0])

    got = exchange(send, "zl")
    send, keep, keep_weight = call(
        backward_body,
        (
            shape((column_tiles + 1, width, TILE), BF16),
            shape((column_tiles, width, TILE), F32),
            shape((W_ROWS, TILE), F32),
        ),
        [smem] * 3 + [vmem] * 2,
        scratch=[pltpu.VMEM((N_CORE, column_tiles, width, TILE), F32)],
    )(total, zl_list, src_list, tiles, got)

    send = call(merge_body, shape((PLANE, N_ZH * TILE + 2 * W_ROWS, TILE), BF16), [vmem] * 3)(
        swap(send, "core"), keep, keep_weight
    )
    got = exchange(send, ("x", "y"))
    send, keep, send_weight = call(
        halfway_body,
        (
            shape((TILE, TILE), BF16),
            shape((TILE, TILE), F32),
            shape((N_ZH * N_ZL, W_ROWS, TILE), BF16),
        ),
        [smem, vmem],
    )(zh.astype(I32)[None], got)
    got = swap(send, "zh")
    got_weight = exchange(send_weight, ("zh", "zl"))
    grad_features, grad_weight = call(
        finish_body,
        (shape((TILE, width), BF16), shape((width, hidden), F32)),
        [vmem] * 3,
    )(got, keep, got_weight)
    return (out_act[None], grad_features[None], grad_weight)


def solution(mesh):
    fine = Mesh(mesh.devices.reshape([size for _, size in FINE]), [name for name, _ in FINE])
    in_specs = (
        P(COL, ROW, None),
        P(),
        P(COL, ROW, None),
        P(ROW, COL, None),
        P(ROW, COL, None),
        P(ROW, COL),
        P(ROW, COL, None, None),
        P(ROW, COL, None, None),
        P(ROW, COL, None, None),
    )
    out_specs = (P(COL, ROW, None), P(COL, ROW, None), P())
    return jax.shard_map(local, mesh=fine, in_specs=in_specs, out_specs=out_specs, check_vma=False)
```

```python
import functools
import math

import jax
import jax.numpy as jnp
from jax import lax
from jax.experimental import pallas as pl
from jax.experimental.pallas import tpu as pltpu
from jax.sharding import Mesh
from jax.sharding import PartitionSpec as P

TILE = 128
GROUP = 4
FINE = (("x", 4), ("zh", 2), ("y", 4), ("zl", 8), ("core", 2))
N_X, N_ZH, N_Y, N_ZL, N_CORE = (size for _, size in FINE)
ROW = ("x", "zh")
COL = ("y", "zl", "core")
LISTS = N_Y * N_CORE
PLANE = N_X * N_Y
W_ROWS = 16
BF16 = jnp.bfloat16
F32 = jnp.float32
I32 = jnp.int32

vmem = pl.BlockSpec(memory_space=pltpu.VMEM)
smem = pl.BlockSpec(memory_space=pltpu.SMEM)
shape = jax.ShapeDtypeStruct


def call(body, outs, in_specs, out_specs=None, scratch=(), flops=0, moved=0, limit=24):
    return pl.pallas_call(
        body,
        out_shape=outs,
        in_specs=in_specs,
        out_specs=jax.tree.map(lambda _: vmem, outs) if out_specs is None else out_specs,
        scratch_shapes=list(scratch),
        compiler_params=pltpu.CompilerParams(vmem_limit_bytes=limit * 1024 * 1024),
        cost_estimate=pl.CostEstimate(flops=flops, bytes_accessed=moved, transcendentals=0),
    )


def halves(value):
    high = value.astype(BF16)
    return high, (value - high.astype(F32)).astype(BF16)


def pack_body(rows_ref, cols_ref, weight_ref, row_ref, col_ref, count_ref, send_ref):
    slots, edges = rows_ref.shape
    rows = rows_ref[...].astype(F32)
    cols = cols_ref[...].astype(F32)
    weight = weight_ref[...].astype(F32)
    line = lax.broadcasted_iota(I32, (slots, slots), 0)
    meta = jnp.where(line == 0, row_ref[...], jnp.where(line == 1, col_ref[...], count_ref[0, 0]))
    blocks = (
        rows[:, :TILE],
        cols[:, :TILE],
        weight[:, :TILE],
        jnp.concatenate([rows[:, TILE:], cols[:, TILE:]], axis=1),
        jnp.concatenate([weight[:, TILE:], meta.astype(F32)], axis=1),
    )
    for k, block in enumerate(blocks):
        send_ref[k * slots : (k + 1) * slots, :] = block.astype(BF16)


def build_body(
    where_ref, own_ref, other_ref, tiles_ref, zl_ref, src_ref, total_ref,
    slot_ref, edge_rows_ref, edge_cols_ref, weight_ref, meta_ref, slots_ref, sem,
):
    y, core = where_ref[0], where_ref[1]
    slots = own_ref.shape[1] // 5
    edges = edge_rows_ref.shape[1]
    rest = edges - TILE
    dummy = LISTS * slots
    lists = [ref.at[k] for ref in (own_ref, other_ref) for k in range(N_Y)]
    for index in range(LISTS):
        meta = lists[index][4 * slots : 4 * slots + 16, :].astype(F32)
        meta_ref[index * 8 : (index + 1) * 8, :] = meta[:8].astype(I32)
    copy = pltpu.make_async_copy(meta_ref, slots_ref, sem)
    copy.start()
    for index in range(LISTS):
        here = slice(index * slots, (index + 1) * slots)
        block = [lists[index][k * slots : (k + 1) * slots, :].astype(F32) for k in range(5)]
        edge_rows_ref[here, :TILE] = block[0]
        edge_cols_ref[here, :TILE] = block[1]
        weight_ref[here, :TILE] = block[2]
        edge_rows_ref[here, TILE:] = block[3][:, :rest]
        edge_cols_ref[here, TILE:] = block[3][:, rest:]
        weight_ref[here, TILE:] = block[4][:, :rest]
    for ref in (edge_rows_ref, edge_cols_ref, weight_ref):
        ref[dummy:, :] = jnp.zeros_like(ref[dummy:, :])
    copy.wait()

    used = jnp.int32(0)
    for part in range(N_CORE):
        for shift in range(N_Y):
            index = part * N_Y + shift
            column_y = (y + N_Y - shift) % N_Y

            def scan(slot, used, index=index, column_y=column_y):
                row, col = slots_ref[index * 8, rest + slot], slots_ref[index * 8 + 1, rest + slot]
                slot_ref[used] = index * slots + slot
                zl_ref[used] = row // N_CORE % N_ZL
                src_ref[used] = (col // N_ZH * N_Y + column_y) * N_ZH + col % N_ZH
                mine = (row // (N_CORE * N_ZL) == y) & (row % N_CORE == core)
                return used + mine.astype(I32)

            used = lax.fori_loop(0, slots_ref[index * 8 + 2, rest], scan, used)
        for extra in range(GROUP - 1):
            slot_ref[used + extra] = dummy
            zl_ref[used + extra] = 0
            src_ref[used + extra] = 0
        used = (used + GROUP - 1) // GROUP * GROUP
        total_ref[part] = used

    positions = lax.broadcasted_iota(I32, (TILE, edges), 0).astype(F32)

    def step(group, carry):
        for i in range(GROUP):
            entry = group * GROUP + i
            slot = slot_ref[entry]
            row_hot = jnp.where(positions == edge_rows_ref[pl.ds(slot, 1), :], 1.0, 0.0)
            col_hot = jnp.where(
                positions == edge_cols_ref[pl.ds(slot, 1), :], weight_ref[pl.ds(slot, 1), :], 0.0
            )
            built = lax.dot_general(
                row_hot.astype(BF16),
                col_hot.astype(BF16),
                (((1,), (1,)), ((), ())),
                preferred_element_type=F32,
            )
            tiles_ref[entry] = built.astype(BF16)
        return carry

    lax.fori_loop(0, used // GROUP, step, 0)


def forward_body(total_ref, zl_ref, src_ref, tiles_ref, own_ref, other_ref, send_ref, acc_ref):
    acc_ref[...] = jnp.zeros_like(acc_ref)

    def step(feats_ref, group, carry):
        products = []
        for i in range(GROUP):
            entry = group * GROUP + i
            products.append(
                jnp.dot(tiles_ref[entry], feats_ref[src_ref[entry]], preferred_element_type=F32)
            )
        for i in range(GROUP):
            acc_ref[zl_ref[group * GROUP + i]] += products[i]
        return carry

    middle, end = total_ref[0] // GROUP, total_ref[1] // GROUP
    lax.fori_loop(0, middle, functools.partial(step, own_ref), 0)
    lax.fori_loop(middle, end, functools.partial(step, other_ref), 0)
    send_ref[...] = acc_ref[...].astype(BF16)


def dense_body(parts_ref, weight_ref, up_ref, act_ref, send_ref, send_weight_ref, *, scale):
    aggregated = jnp.sum(parts_ref[...].astype(F32), axis=0).astype(BF16)
    weight = weight_ref[...]
    pre_act = jnp.dot(aggregated, weight, preferred_element_type=F32)
    gate = jax.nn.sigmoid(pre_act)
    act_ref[...] = (pre_act * gate).astype(BF16)
    grad_pre = (up_ref[...].astype(F32) * gate * (1.0 + pre_act * (1.0 - gate))).astype(BF16)
    grad_agg = lax.dot_general(
        weight, grad_pre, (((1,), (1,)), ((), ())), preferred_element_type=F32
    ).astype(BF16)
    send_ref[...] = grad_agg
    local_weight = (
        lax.dot_general(aggregated, grad_pre, (((0,), (0,)), ((), ())), preferred_element_type=F32)
        * scale
    )
    deep = TILE // PLANE
    for peer in range(PLANE):
        here = slice(peer * deep, (peer + 1) * deep)
        part = jnp.concatenate([local_weight[here, :TILE], local_weight[here, TILE:]], axis=0)
        send_weight_ref[peer] = part.astype(BF16)


def spread_body(tile_ref, terms_ref, send_ref):
    part = jnp.sum(terms_ref[...].astype(F32), axis=0).astype(BF16)
    for peer in range(N_ZL):
        send_ref[peer, 0:TILE, :] = tile_ref[...]
        send_ref[peer, TILE:, :] = part


def backward_body(
    total_ref, zl_ref, src_ref, tiles_ref, got_ref, send_ref, keep_ref, keep_weight_ref, acc_ref
):
    acc_ref[...] = jnp.zeros_like(acc_ref)

    def step(part, group, carry):
        products = []
        for i in range(GROUP):
            entry = group * GROUP + i
            grad = got_ref[zl_ref[entry], 0:TILE, :]
            products.append(jnp.dot(grad, tiles_ref[entry], preferred_element_type=F32))
        for i in range(GROUP):
            acc_ref[part, src_ref[group * GROUP + i]] += products[i]
        return carry

    middle, end = total_ref[0] // GROUP, total_ref[1] // GROUP
    lax.fori_loop(0, middle, functools.partial(step, 0), 0)
    lax.fori_loop(middle, end, functools.partial(step, 1), 0)
    keep_ref[...] = acc_ref[0]
    tiles = acc_ref.shape[1]
    send_ref[0:tiles] = acc_ref[1].astype(BF16)
    weight_sum = jnp.sum(got_ref[:, TILE:, :].astype(F32), axis=0)
    keep_weight_ref[...] = weight_sum
    high, low = halves(weight_sum)
    send_ref[tiles, 0:W_ROWS, :] = high
    send_ref[tiles, W_ROWS : 2 * W_ROWS, :] = low
    send_ref[tiles, 2 * W_ROWS :, :] = jnp.zeros_like(send_ref[tiles, 2 * W_ROWS :, :])


def merge_body(got_ref, keep_ref, keep_weight_ref, send_ref):
    tiles = keep_ref.shape[0]
    terms = got_ref[tiles, 0 : 2 * W_ROWS, :].astype(F32)
    part = (keep_weight_ref[...] + (terms[:W_ROWS] + terms[W_ROWS:])).astype(BF16)
    for peer in range(PLANE):
        for zh in range(N_ZH):
            tile = peer * N_ZH + zh
            send_ref[peer, zh * TILE : (zh + 1) * TILE, :] = (
                keep_ref[tile] + got_ref[tile].astype(F32)
            ).astype(BF16)
        send_ref[peer, N_ZH * TILE :, :] = part


def halfway_body(zh_ref, got_ref, send_ref, keep_ref):
    zh = zh_ref[0]
    total = jnp.sum(got_ref[:, 0 : N_ZH * TILE, :].astype(F32), axis=0)
    first, second = total[:TILE], total[TILE:]
    mine = zh == 0
    keep_ref[...] = jnp.where(mine, first, second)
    send_ref[0:TILE, :] = jnp.where(mine, second, first).astype(BF16)
    for peer in range(PLANE):
        send_ref[TILE + peer * W_ROWS : TILE + (peer + 1) * W_ROWS, :] = got_ref[
            peer, N_ZH * TILE :, :
        ]


def finish_body(got_ref, keep_ref, sent_ref, grad_ref, grad_weight_ref):
    grad_ref[...] = (keep_ref[...] + got_ref[0:TILE, :].astype(F32)).T.astype(BF16)
    deep = TILE // PLANE
    total = got_ref[TILE:, :].astype(F32) + sent_ref[TILE:, :].astype(F32)
    for peer in range(PLANE):
        part = total[peer * W_ROWS : (peer + 1) * W_ROWS]
        grad_weight_ref[peer * deep : (peer + 1) * deep, :TILE] = part[:deep]
        grad_weight_ref[peer * deep : (peer + 1) * deep, TILE:] = part[deep:]


def swap(value, axis):
    return lax.ppermute(value, axis, [(0, 1), (1, 0)])


def exchange(value, axis):
    return lax.all_to_all(value, axis, 0, 0, tiled=True)


def local(
    features, weight, upstream, tile_rows, tile_cols, tile_count, edge_rows, edge_cols, edge_weight
):
    width = features.shape[2]
    hidden = weight.shape[1]
    slots, edges = edge_rows.shape[2:]
    column_tiles = PLANE * N_ZH
    most = slots + (LISTS - 1) * slots // 2 + 2 * GROUP
    zh = lax.axis_index("zh")
    where = jnp.stack([lax.axis_index("y"), lax.axis_index("core")]).astype(I32)

    own = jnp.broadcast_to(features, (N_ZH,) + features.shape[1:])
    pair = exchange(own, "zh")
    packed = call(pack_body, shape((5 * slots, TILE), BF16), [vmem] * 5 + [smem])(
        edge_rows[0, 0], edge_cols[0, 0], edge_weight[0, 0], tile_rows[0], tile_cols[0], tile_count
    )
    moved = [
        lax.ppermute(packed, "y", [(k, (k + shift) % N_Y) for k in range(N_Y)])
        for shift in range(1, N_Y)
    ]
    pair, moved = lax.optimization_barrier((pair, moved))
    mine = exchange(jnp.broadcast_to(pair[None], (PLANE,) + pair.shape), ("x", "y"))
    lists = jnp.stack([packed] + moved)
    built = call(
        build_body,
        (
            shape((most, TILE, TILE), BF16),
            shape((most,), I32),
            shape((most,), I32),
            shape((N_CORE,), I32),
        ),
        [smem, vmem, vmem],
        (vmem, smem, smem, smem),
        [pltpu.SMEM((most,), I32)]
        + [pltpu.VMEM((LISTS * slots + 8, edges), F32)] * 3
        + [
            pltpu.VMEM((LISTS * 8, TILE), I32),
            pltpu.SMEM((LISTS * 8, TILE), I32),
            pltpu.SemaphoreType.DMA,
        ],
        flops=slots * TILE * TILE * edges * 4,
        moved=slots * TILE * TILE * 2,
    )(where, lists, swap(lists, "core"))
    mine, (tiles, zl_list, src_list, total) = lax.optimization_barrier((mine, built))
    mine = mine.reshape(column_tiles, TILE, width)
    theirs = swap(mine, "core")

    partial = call(
        forward_body,
        shape((N_ZL, TILE, width), BF16),
        [smem] * 3 + [vmem] * 3,
        scratch=[pltpu.VMEM((N_ZL, TILE, width), F32)],
    )(total, zl_list, src_list, tiles, mine, theirs)

    parts = exchange(partial, "zl")

    node_total = features.shape[1] * N_X * N_ZH * N_Y * N_ZL * N_CORE
    out_act, tile, send_weight = call(
        functools.partial(dense_body, scale=1.0 / math.sqrt(node_total)),
        (
            shape((TILE, hidden), BF16),
            shape((width, TILE), BF16),
            shape((PLANE, W_ROWS, TILE), BF16),
        ),
        [vmem] * 3,
    )(parts, weight, upstream[0])

    send = call(spread_body, shape((N_ZL, TILE + W_ROWS, TILE), BF16), [vmem] * 2)(
        tile, exchange(send_weight, ("x", "y"))
    )
    got = exchange(send, "zl")
    send, keep, keep_weight = call(
        backward_body,
        (
            shape((column_tiles + 1, width, TILE), BF16),
            shape((column_tiles, width, TILE), F32),
            shape((W_ROWS, TILE), F32),
        ),
        [smem] * 3 + [vmem] * 2,
        scratch=[pltpu.VMEM((N_CORE, column_tiles, width, TILE), F32)],
    )(total, zl_list, src_list, tiles, got)

    send = call(merge_body, shape((PLANE, N_ZH * TILE + W_ROWS, TILE), BF16), [vmem] * 3)(
        swap(send, "core"), keep, keep_weight
    )
    got = exchange(send, ("x", "y"))
    send, keep = call(
        halfway_body,
        (shape((TILE + PLANE * W_ROWS, TILE), BF16), shape((TILE, TILE), F32)),
        [smem, vmem],
    )(zh.astype(I32)[None], got)
    grad_features, grad_weight = call(
        finish_body,
        (shape((TILE, width), BF16), shape((width, hidden), F32)),
        [vmem] * 3,
    )(swap(send, "zh"), keep, send)
    return (out_act[None], grad_features[None], grad_weight)


def solution(mesh):
    fine = Mesh(mesh.devices.reshape([size for _, size in FINE]), [name for name, _ in FINE])
    in_specs = (
        P(COL, ROW, None),
        P(),
        P(COL, ROW, None),
        P(ROW, COL, None),
        P(ROW, COL, None),
        P(ROW, COL),
        P(ROW, COL, None, None),
        P(ROW, COL, None, None),
        P(ROW, COL, None, None),
    )
    out_specs = (P(COL, ROW, None), P(COL, ROW, None), P())
    return jax.shard_map(local, mesh=fine, in_specs=in_specs, out_specs=out_specs, check_vma=False)
```

```python
import math

import jax
import jax.numpy as jnp
from jax import lax
from jax.experimental import pallas as pl
from jax.experimental.pallas import tpu as pltpu
from jax.sharding import Mesh
from jax.sharding import PartitionSpec as P

TILE = 128
GROUP = 4
FINE = (("x", 4), ("zh", 2), ("y", 4), ("z2", 2), ("z4", 4), ("core", 2))
N_X, N_ZH, N_Y, N_Z2, N_Z4, N_CORE = (size for _, size in FINE)
N_ZL = N_Z2 * N_Z4
ROW = ("x", "zh")
COL = ("y", "z2", "z4", "core")
W_ROWS = 64
VMEM_LIMIT = 48 * 1024 * 1024
BF16 = jnp.bfloat16
F32 = jnp.float32

vmem = pl.BlockSpec(memory_space=pltpu.VMEM)
smem = pl.BlockSpec(memory_space=pltpu.SMEM)
hbm = pl.BlockSpec(memory_space=pl.ANY)


def call(body, outs, in_specs, scratch=(), flops=0, moved=0):
    return pl.pallas_call(
        body,
        out_shape=outs,
        in_specs=in_specs,
        out_specs=jax.tree.map(lambda _: vmem, outs),
        scratch_shapes=list(scratch),
        compiler_params=pltpu.CompilerParams(vmem_limit_bytes=VMEM_LIMIT),
        cost_estimate=pl.CostEstimate(flops=flops, bytes_accessed=moved, transcendentals=0),
    )


def halves(value):
    high = value.astype(BF16)
    return high, (value - high.astype(F32)).astype(BF16)


def group_total(count_ref):
    return (count_ref[0, 0] + GROUP - 1) // GROUP


def tile_place(row):
    near = row // N_CORE
    return near // N_ZL * N_ZL + near % N_Z4 * N_Z2 + near // N_Z4 % N_Z2


def pair_body(zh_ref, own_ref, other_ref, send_ref):
    mine = zh_ref[0] == 0
    own, other = own_ref[...], other_ref[...]
    first, second = jnp.where(mine, own, other), jnp.where(mine, other, own)
    for peer in range(N_X):
        send_ref[peer, 0] = first
        send_ref[peer, 1] = second


def build_body(count_ref, rows_ref, cols_ref, weight_ref, tiles_ref, live_ref):
    slots, edges = rows_ref.shape
    slot_ids = lax.broadcasted_iota(jnp.int32, (slots, edges), 0)
    live_ref[...] = jnp.where(slot_ids < count_ref[0, 0], weight_ref[...].astype(F32), 0.0)
    positions = lax.broadcasted_iota(jnp.int32, (TILE, edges), 0)

    def step(group, carry):
        for i in range(GROUP):
            slot = group * GROUP + i
            row_hot = jnp.where(positions == rows_ref[pl.ds(slot, 1), :], 1.0, 0.0).astype(BF16)
            col_hot = jnp.where(
                positions == cols_ref[pl.ds(slot, 1), :], live_ref[pl.ds(slot, 1), :], 0.0
            ).astype(BF16)
            built = lax.dot_general(
                row_hot, col_hot, (((1,), (1,)), ((), ())), preferred_element_type=F32
            )
            tiles_ref[slot] = built.astype(BF16)
        return carry

    lax.fori_loop(0, group_total(count_ref), step, 0)


def forward_body(
    count_ref, core_ref, row_ref, col_ref, tiles_ref, feats_ref, send_ref, keep_ref, acc_ref
):
    acc_ref[...] = jnp.zeros_like(acc_ref)
    core = core_ref[0]

    def step(group, carry):
        products = []
        for i in range(GROUP):
            slot = group * GROUP + i
            products.append(
                jnp.dot(tiles_ref[slot], feats_ref[col_ref[0, slot]], preferred_element_type=F32)
            )
        for i in range(GROUP):
            row = row_ref[0, group * GROUP + i]
            acc_ref[row % N_CORE, tile_place(row)] += products[i]
        return carry

    lax.fori_loop(0, group_total(count_ref), step, 0)
    send_ref[...] = acc_ref[1 - core].astype(BF16)
    keep_ref[...] = acc_ref[core]


def merge_body(got_ref, keep_ref, out_ref):
    out_ref[...] = (keep_ref[...] + got_ref[...].astype(F32)).astype(BF16)


def dense_body(
    z2_ref, own_ref, other_ref, weight_ref, up_ref, other_up_ref, act_ref, send_ref, *, scale
):
    first = z2_ref[0] == 0
    total = own_ref[...].astype(F32) + other_ref[...].astype(F32)
    aggregated = total.reshape(N_Z2 * TILE, TILE).astype(BF16)
    weight = weight_ref[...]
    own_up, other_up = up_ref[...], other_up_ref[...]
    up = jnp.concatenate(
        [jnp.where(first, own_up, other_up), jnp.where(first, other_up, own_up)], axis=0
    )
    pre_act = jnp.dot(aggregated, weight, preferred_element_type=F32)
    gate = jax.nn.sigmoid(pre_act)
    act = (pre_act * gate).astype(BF16)
    act_ref[...] = jnp.where(first, act[:TILE], act[TILE:])
    grad_pre = (up.astype(F32) * gate * (1.0 + pre_act * (1.0 - gate))).astype(BF16)
    local_weight = (
        lax.dot_general(aggregated, grad_pre, (((0,), (0,)), ((), ())), preferred_element_type=F32)
        * scale
    ).astype(BF16)
    deep = TILE // N_Z4
    for z2 in range(N_Z2):
        grad_agg = lax.dot_general(
            weight,
            grad_pre[z2 * TILE : (z2 + 1) * TILE],
            (((1,), (1,)), ((), ())),
            preferred_element_type=F32,
        ).astype(BF16)
        for peer in range(N_Z4):
            send_ref[peer, z2 * TILE : (z2 + 1) * TILE, :] = grad_agg
    for peer in range(N_Z4):
        here = slice(peer * deep, (peer + 1) * deep)
        send_ref[peer, N_Z2 * TILE : N_Z2 * TILE + deep, :] = local_weight[here, :TILE]
        send_ref[peer, N_Z2 * TILE + deep :, :] = local_weight[here, TILE:]


def spread_body(got_ref, send_ref):
    high, low = halves(jnp.sum(got_ref[:, N_Z2 * TILE :, :].astype(F32), axis=0))
    for peer in range(N_Y):
        for z4 in range(N_Z4):
            here = slice(z4 * N_Z2 * TILE, (z4 + 1) * N_Z2 * TILE)
            send_ref[peer, here, :] = got_ref[z4, 0 : N_Z2 * TILE, :]
        send_ref[peer, N_ZL * TILE : N_ZL * TILE + W_ROWS, :] = high
        send_ref[peer, N_ZL * TILE + W_ROWS :, :] = low


def backward_body(
    count_ref, core_ref, row_ref, col_ref, tiles_ref, own_ref, other_ref, send_ref, grads_ref, acc_ref, sems
):
    core = core_ref[0]
    copies = [
        pltpu.make_async_copy(own_ref, grads_ref.at[core], sems.at[0]),
        pltpu.make_async_copy(other_ref, grads_ref.at[1 - core], sems.at[1]),
    ]
    for copy in copies:
        copy.start()
    acc_ref[...] = jnp.zeros_like(acc_ref)
    for copy in copies:
        copy.wait()

    def step(group, carry):
        products = []
        for i in range(GROUP):
            slot = group * GROUP + i
            row = row_ref[0, slot]
            place = tile_place(row)
            start = pl.multiple_of(place % N_ZL * TILE, TILE)
            grad = grads_ref[row % N_CORE, place // N_ZL, pl.ds(start, TILE), :]
            products.append(jnp.dot(grad, tiles_ref[slot], preferred_element_type=F32))
        for i in range(GROUP):
            acc_ref[col_ref[0, group * GROUP + i]] += products[i]
        return carry

    lax.fori_loop(0, group_total(count_ref), step, 0)
    terms = jnp.sum(grads_ref[:, :, N_ZL * TILE :, :].astype(F32), axis=(0, 1))
    weight_sum = (terms[:W_ROWS] + terms[W_ROWS:]).astype(BF16)
    for x in range(N_X):
        for zh in range(N_ZH):
            send_ref[x, zh * TILE : (zh + 1) * TILE, :] = acc_ref[x * N_ZH + zh].astype(BF16)
        send_ref[x, N_ZH * TILE :, :] = weight_sum


def halfway_body(zh_ref, got_ref, send_ref, keep_ref, send_weight_ref):
    zh = zh_ref[0]
    total = jnp.sum(got_ref[...].astype(F32), axis=0)
    first, second = total[:TILE], total[TILE : N_ZH * TILE]
    mine = zh == 0
    keep_ref[...] = jnp.where(mine, first, second)
    send_ref[...] = jnp.where(mine, second, first).astype(BF16)
    weight_sum = total[N_ZH * TILE :].astype(BF16)
    for peer in range(N_ZH * N_Z4):
        send_weight_ref[peer] = weight_sum


def finish_body(got_ref, keep_ref, got_weight_ref, grad_ref, grad_weight_ref):
    grad_ref[...] = (keep_ref[...] + got_ref[...].astype(F32)).T.astype(BF16)
    deep = TILE // N_Z4
    for k in range(N_Z4):
        total = got_weight_ref[k].astype(F32) + got_weight_ref[N_Z4 + k].astype(F32)
        grad_weight_ref[k * deep : (k + 1) * deep, :TILE] = total[:deep]
        grad_weight_ref[k * deep : (k + 1) * deep, TILE:] = total[deep:]


def swap(value, axis):
    return lax.ppermute(value, axis, [(0, 1), (1, 0)])


def exchange(value, axis):
    return lax.all_to_all(value, axis, 0, 0, tiled=True)


def local(
    features, weight, upstream, tile_rows, tile_cols, tile_count, edge_rows, edge_cols, edge_weight
):
    width = features.shape[2]
    hidden = weight.shape[1]
    slots, edges = edge_rows.shape[2:]
    row_tiles, col_tiles = tile_rows[0], tile_cols[0]
    blocks = N_Y * N_ZL * N_CORE
    shape = jax.ShapeDtypeStruct

    zh = lax.axis_index("zh")
    own = features[0]
    other = swap(own, "zh")
    zh_here = zh.astype(jnp.int32)[None]
    pair = call(pair_body, shape((N_X, N_ZH, TILE, width), BF16), [smem, vmem, vmem])(
        zh_here, own, other
    )
    column = exchange(pair, "x").reshape(N_X * N_ZH, TILE, width)

    tiles = call(
        build_body,
        shape((slots, TILE, TILE), BF16),
        [smem, vmem, vmem, vmem],
        [pltpu.VMEM((slots, edges), F32)],
        flops=slots * TILE * TILE * edges * 8,
        moved=slots * TILE * TILE * 2,
    )(tile_count, edge_rows[0, 0], edge_cols[0, 0], edge_weight[0, 0])

    core = lax.axis_index("core").astype(jnp.int32)[None]
    half = (blocks // N_CORE, TILE, width)
    send, keep = call(
        forward_body,
        (shape(half, BF16), shape(half, F32)),
        [smem, smem, smem, smem, vmem, vmem],
        [pltpu.VMEM((N_CORE,) + half, F32)],
        flops=slots * TILE * TILE * width * 2,
        moved=slots * TILE * TILE * 4,
    )(tile_count, core, row_tiles, col_tiles, tiles, column)

    partial = call(merge_body, shape(half, BF16), [vmem, vmem])(swap(send, "core"), keep)
    partial, up = lax.optimization_barrier((partial, upstream[0]))
    got, other_up = lax.optimization_barrier((exchange(partial, "y"), swap(up, "z2")))
    got = got.reshape((N_Y, N_ZL, TILE, width))
    partial = jnp.sum(got.astype(F32), axis=0).astype(BF16)
    got = exchange(partial, "z4").reshape((N_Z4, N_Z2, TILE, width))
    partial = jnp.sum(got.astype(F32), axis=0).astype(BF16)

    node_total = features.shape[1] * N_X * N_ZH * blocks
    scale = 1.0 / math.sqrt(node_total)

    def dense(*refs):
        dense_body(*refs, scale=scale)

    out_act, send = call(
        dense,
        (shape((TILE, hidden), BF16), shape((N_Z4, N_Z2 * TILE + W_ROWS, TILE), BF16)),
        [smem] + [vmem] * 5,
    )(
        lax.axis_index("z2").astype(jnp.int32)[None],
        partial,
        swap(partial, "z2"),
        weight,
        up,
        other_up,
    )

    got = exchange(send, "z4")
    send = call(spread_body, shape((N_Y, N_ZL * TILE + 2 * W_ROWS, TILE), BF16), [vmem])(got)
    mine = exchange(send, "y")
    theirs = swap(mine, "core")
    send = call(
        backward_body,
        shape((N_X, N_ZH * TILE + W_ROWS, TILE), BF16),
        [smem, smem, smem, smem, vmem, hbm, hbm],
        [
            pltpu.VMEM((N_CORE,) + mine.shape, BF16),
            pltpu.VMEM((N_X * N_ZH, width, TILE), F32),
            pltpu.SemaphoreType.DMA((2,)),
        ],
    )(
        tile_count,
        core,
        row_tiles,
        col_tiles,
        tiles,
        mine,
        theirs,
    )

    got = exchange(send, "x")
    send, keep, send_weight = call(
        halfway_body,
        (
            shape((TILE, TILE), BF16),
            shape((TILE, TILE), F32),
            shape((N_ZH * N_Z4, W_ROWS, TILE), BF16),
        ),
        [smem, vmem],
    )(zh_here, got)
    got = swap(send, "zh")
    got_weight = exchange(send_weight, ("zh", "z4"))
    grad_features, grad_weight = call(
        finish_body,
        (shape((TILE, width), BF16), shape((width, hidden), F32)),
        [vmem] * 3,
    )(got, keep, got_weight)
    return (out_act[None], grad_features[None], grad_weight)


def solution(mesh):
    fine = Mesh(mesh.devices.reshape([size for _, size in FINE]), [name for name, _ in FINE])
    in_specs = (
        P(COL, ROW, None),
        P(),
        P(COL, ROW, None),
        P(ROW, COL, None),
        P(ROW, COL, None),
        P(ROW, COL),
        P(ROW, COL, None, None),
        P(ROW, COL, None, None),
        P(ROW, COL, None, None),
    )
    out_specs = (P(COL, ROW, None), P(COL, ROW, None), P())
    return jax.shard_map(local, mesh=fine, in_specs=in_specs, out_specs=out_specs, check_vma=False)
```

```python
import math

import jax
import jax.numpy as jnp
from jax import lax
from jax.experimental import pallas as pl
from jax.experimental.pallas import tpu as pltpu
from jax.sharding import Mesh
from jax.sharding import PartitionSpec as P

TILE = 128
GROUP = 16
FINE = (("x", 4), ("zh", 2), ("y", 4), ("z2", 2), ("z4", 4), ("core", 2))
N_X, N_ZH, N_Y, N_Z2, N_Z4, N_CORE = (size for _, size in FINE)
N_ZL = N_Z2 * N_Z4
ROW = ("x", "zh")
COL = ("y", "z2", "z4", "core")
W_ROWS = 32
VMEM_LIMIT = 48 * 1024 * 1024
BF16 = jnp.bfloat16
F32 = jnp.float32

vmem = pl.BlockSpec(memory_space=pltpu.VMEM)
smem = pl.BlockSpec(memory_space=pltpu.SMEM)
hbm = pl.BlockSpec(memory_space=pl.ANY)


def call(body, outs, in_specs, scratch=(), flops=0, moved=0):
    return pl.pallas_call(
        body,
        out_shape=outs,
        in_specs=in_specs,
        out_specs=jax.tree.map(lambda _: vmem, outs),
        scratch_shapes=list(scratch),
        compiler_params=pltpu.CompilerParams(vmem_limit_bytes=VMEM_LIMIT),
        cost_estimate=pl.CostEstimate(flops=flops, bytes_accessed=moved, transcendentals=0),
    )


def halves(value):
    high = value.astype(BF16)
    return high, (value - high.astype(F32)).astype(BF16)


def group_total(count_ref):
    return (count_ref[0, 0] + GROUP - 1) // GROUP


def tile_place(row):
    near = row // N_CORE
    return near // N_ZL * N_ZL + near % N_Z4 * N_Z2 + near // N_Z4 % N_Z2


def pair_body(zh_ref, own_ref, other_ref, send_ref):
    mine = zh_ref[0] == 0
    own, other = own_ref[...], other_ref[...]
    first, second = jnp.where(mine, own, other), jnp.where(mine, other, own)
    for peer in range(N_X):
        send_ref[peer, 0] = first
        send_ref[peer, 1] = second


def build_body(count_ref, rows_ref, cols_ref, weight_ref, tiles_ref, live_ref):
    slots, edges = rows_ref.shape
    slot_ids = lax.broadcasted_iota(jnp.int32, (slots, edges), 0)
    live_ref[...] = jnp.where(slot_ids < count_ref[0, 0], weight_ref[...].astype(F32), 0.0)
    positions = lax.broadcasted_iota(jnp.int32, (TILE, edges), 0)

    def step(group, carry):
        for i in range(GROUP):
            slot = group * GROUP + i
            row_hot = jnp.where(positions == rows_ref[pl.ds(slot, 1), :], 1.0, 0.0).astype(BF16)
            col_hot = jnp.where(
                positions == cols_ref[pl.ds(slot, 1), :], live_ref[pl.ds(slot, 1), :], 0.0
            ).astype(BF16)
            built = lax.dot_general(
                row_hot, col_hot, (((1,), (1,)), ((), ())), preferred_element_type=F32
            )
            tiles_ref[slot] = built.astype(BF16)
        return carry

    lax.fori_loop(0, group_total(count_ref), step, 0)


def forward_body(
    count_ref, core_ref, row_ref, col_ref, tiles_ref, feats_ref, send_ref, keep_ref, acc_ref
):
    acc_ref[...] = jnp.zeros_like(acc_ref)
    core = core_ref[0]

    def step(group, carry):
        products = []
        for i in range(GROUP):
            slot = group * GROUP + i
            products.append(
                jnp.dot(tiles_ref[slot], feats_ref[col_ref[0, slot]], preferred_element_type=F32)
            )
        for i in range(GROUP):
            row = row_ref[0, group * GROUP + i]
            acc_ref[row % N_CORE, tile_place(row)] += products[i]
        return carry

    lax.fori_loop(0, group_total(count_ref), step, 0)
    send_ref[...] = acc_ref[1 - core].astype(BF16)
    keep_ref[...] = acc_ref[core]


def merge_body(got_ref, keep_ref, out_ref):
    out_ref[...] = (keep_ref[...] + got_ref[...].astype(F32)).astype(BF16)


def dense_body(
    z2_ref, own_ref, other_ref, weight_ref, up_ref, other_up_ref, act_ref, send_ref, *, scale
):
    first = z2_ref[0] == 0
    total = own_ref[...].astype(F32) + other_ref[...].astype(F32)
    aggregated = total.reshape(N_Z2 * TILE, TILE).astype(BF16)
    weight = weight_ref[...]
    own_up, other_up = up_ref[...], other_up_ref[...]
    up = jnp.concatenate(
        [jnp.where(first, own_up, other_up), jnp.where(first, other_up, own_up)], axis=0
    )
    pre_act = jnp.dot(aggregated, weight, preferred_element_type=F32)
    gate = jax.nn.sigmoid(pre_act)
    act = (pre_act * gate).astype(BF16)
    act_ref[...] = jnp.where(first, act[:TILE], act[TILE:])
    grad_pre = (up.astype(F32) * gate * (1.0 + pre_act * (1.0 - gate))).astype(BF16)
    local_weight = (
        lax.dot_general(aggregated, grad_pre, (((0,), (0,)), ((), ())), preferred_element_type=F32)
        * scale
    ).astype(BF16)
    deep = TILE // N_Z4
    for z2 in range(N_Z2):
        grad_agg = lax.dot_general(
            weight,
            grad_pre[z2 * TILE : (z2 + 1) * TILE],
            (((1,), (1,)), ((), ())),
            preferred_element_type=F32,
        ).astype(BF16)
        for peer in range(N_Z4):
            send_ref[peer, z2 * TILE : (z2 + 1) * TILE, :] = grad_agg
    for peer in range(N_Z4):
        here = slice(peer * deep, (peer + 1) * deep)
        send_ref[peer, N_Z2 * TILE : N_Z2 * TILE + deep, :] = local_weight[here, :TILE]
        send_ref[peer, N_Z2 * TILE + deep :, :] = local_weight[here, TILE:]


def spread_body(z2_ref, got_ref, send_ref):
    terms = jnp.sum(got_ref[:, N_Z2 * TILE :, :].astype(F32), axis=0)
    high, low = halves(jnp.where(z2_ref[0] == 0, terms[:W_ROWS], terms[W_ROWS:]))
    for peer in range(N_Y):
        for z4 in range(N_Z4):
            here = slice(z4 * N_Z2 * TILE, (z4 + 1) * N_Z2 * TILE)
            send_ref[peer, here, :] = got_ref[z4, 0 : N_Z2 * TILE, :]
        send_ref[peer, N_ZL * TILE : N_ZL * TILE + W_ROWS, :] = high
        send_ref[peer, N_ZL * TILE + W_ROWS :, :] = low


def backward_body(
    count_ref, core_ref, row_ref, col_ref, tiles_ref, own_ref, other_ref, send_ref, grads_ref, acc_ref, sems
):
    core = core_ref[0]
    copies = [
        pltpu.make_async_copy(own_ref, grads_ref.at[core], sems.at[0]),
        pltpu.make_async_copy(other_ref, grads_ref.at[1 - core], sems.at[1]),
    ]
    for copy in copies:
        copy.start()
    acc_ref[...] = jnp.zeros_like(acc_ref)
    for copy in copies:
        copy.wait()

    def step(group, carry):
        products = []
        for i in range(GROUP):
            slot = group * GROUP + i
            row = row_ref[0, slot]
            place = tile_place(row)
            start = pl.multiple_of(place % N_ZL * TILE, TILE)
            grad = grads_ref[row % N_CORE, place // N_ZL, pl.ds(start, TILE), :]
            products.append(jnp.dot(grad, tiles_ref[slot], preferred_element_type=F32))
        for i in range(GROUP):
            acc_ref[col_ref[0, group * GROUP + i]] += products[i]
        return carry

    lax.fori_loop(0, group_total(count_ref), step, 0)
    terms = jnp.sum(grads_ref[:, :, N_ZL * TILE :, :].astype(F32), axis=(0, 1))
    high, low = halves(terms[:W_ROWS] + terms[W_ROWS:])
    for x in range(N_X):
        for zh in range(N_ZH):
            send_ref[x, zh * TILE : (zh + 1) * TILE, :] = acc_ref[x * N_ZH + zh].astype(BF16)
        send_ref[x, N_ZH * TILE : N_ZH * TILE + W_ROWS, :] = high
        send_ref[x, N_ZH * TILE + W_ROWS :, :] = low


def halfway_body(zh_ref, got_ref, send_ref, keep_ref, send_weight_ref):
    zh = zh_ref[0]
    total = jnp.sum(got_ref[...].astype(F32), axis=0)
    first, second = total[:TILE], total[TILE : N_ZH * TILE]
    mine = zh == 0
    keep_ref[...] = jnp.where(mine, first, second)
    send_ref[...] = jnp.where(mine, second, first).astype(BF16)
    terms = total[N_ZH * TILE :]
    weight_sum = (terms[:W_ROWS] + terms[W_ROWS:]).astype(BF16)
    for peer in range(N_ZH * N_ZL):
        send_weight_ref[peer] = weight_sum


def finish_body(got_ref, keep_ref, got_weight_ref, grad_ref, grad_weight_ref):
    grad_ref[...] = (keep_ref[...] + got_ref[...].astype(F32)).T.astype(BF16)
    deep = TILE // N_Z4
    for z2 in range(N_Z2):
        for z4 in range(N_Z4):
            k = z2 * N_Z4 + z4
            total = got_weight_ref[k].astype(F32) + got_weight_ref[N_ZL + k].astype(F32)
            grad_weight_ref[z4 * deep : (z4 + 1) * deep, z2 * TILE : (z2 + 1) * TILE] = total


def swap(value, axis):
    return lax.ppermute(value, axis, [(0, 1), (1, 0)])


def exchange(value, axis):
    return lax.all_to_all(value, axis, 0, 0, tiled=True)


def local(
    features, weight, upstream, tile_rows, tile_cols, tile_count, edge_rows, edge_cols, edge_weight
):
    width = features.shape[2]
    hidden = weight.shape[1]
    slots, edges = edge_rows.shape[2:]
    row_tiles, col_tiles = tile_rows[0], tile_cols[0]
    blocks = N_Y * N_ZL * N_CORE
    shape = jax.ShapeDtypeStruct

    zh = lax.axis_index("zh")
    own = features[0]
    other = swap(own, "zh")
    zh_here = zh.astype(jnp.int32)[None]
    z2 = lax.axis_index("z2").astype(jnp.int32)[None]
    pair = call(pair_body, shape((N_X, N_ZH, TILE, width), BF16), [smem, vmem, vmem])(
        zh_here, own, other
    )
    column = exchange(pair, "x").reshape(N_X * N_ZH, TILE, width)

    tiles = call(
        build_body,
        shape((slots, TILE, TILE), BF16),
        [smem, vmem, vmem, vmem],
        [pltpu.VMEM((slots, edges), F32)],
        flops=slots * TILE * TILE * edges * 8,
        moved=slots * TILE * TILE * 2,
    )(tile_count, edge_rows[0, 0], edge_cols[0, 0], edge_weight[0, 0])

    core = lax.axis_index("core").astype(jnp.int32)[None]
    half = (blocks // N_CORE, TILE, width)
    send, keep = call(
        forward_body,
        (shape(half, BF16), shape(half, F32)),
        [smem, smem, smem, smem, vmem, vmem],
        [pltpu.VMEM((N_CORE,) + half, F32)],
        flops=slots * TILE * TILE * width * 2,
        moved=slots * TILE * TILE * 4,
    )(tile_count, core, row_tiles, col_tiles, tiles, column)

    partial = call(merge_body, shape(half, BF16), [vmem, vmem])(swap(send, "core"), keep)
    partial, up = lax.optimization_barrier((partial, upstream[0]))
    got, other_up = lax.optimization_barrier((exchange(partial, "y"), swap(up, "z2")))
    got = got.reshape((N_Y, N_ZL, TILE, width))
    partial = jnp.sum(got.astype(F32), axis=0).astype(BF16)
    got = exchange(partial, "z4").reshape((N_Z4, N_Z2, TILE, width))
    partial = jnp.sum(got.astype(F32), axis=0).astype(BF16)

    node_total = features.shape[1] * N_X * N_ZH * blocks
    scale = 1.0 / math.sqrt(node_total)

    def dense(*refs):
        dense_body(*refs, scale=scale)

    out_act, send = call(
        dense,
        (shape((TILE, hidden), BF16), shape((N_Z4, N_Z2 * (TILE + W_ROWS), TILE), BF16)),
        [smem] + [vmem] * 5,
    )(
        z2,
        partial,
        swap(partial, "z2"),
        weight,
        up,
        other_up,
    )

    got = exchange(send, "z4")
    send = call(spread_body, shape((N_Y, N_ZL * TILE + 2 * W_ROWS, TILE), BF16), [smem, vmem])(
        z2, got
    )
    mine = exchange(send, "y")
    theirs = swap(mine, "core")
    send = call(
        backward_body,
        shape((N_X, N_ZH * TILE + 2 * W_ROWS, TILE), BF16),
        [smem, smem, smem, smem, vmem, hbm, hbm],
        [
            pltpu.VMEM((N_CORE,) + mine.shape, BF16),
            pltpu.VMEM((N_X * N_ZH, width, TILE), F32),
            pltpu.SemaphoreType.DMA((2,)),
        ],
    )(
        tile_count,
        core,
        row_tiles,
        col_tiles,
        tiles,
        mine,
        theirs,
    )

    got = exchange(send, "x")
    send, keep, send_weight = call(
        halfway_body,
        (
            shape((TILE, TILE), BF16),
            shape((TILE, TILE), F32),
            shape((N_ZH * N_ZL, W_ROWS, TILE), BF16),
        ),
        [smem, vmem],
    )(zh_here, got)
    got = swap(send, "zh")
    got_weight = exchange(send_weight, ("zh", "z2", "z4"))
    grad_features, grad_weight = call(
        finish_body,
        (shape((TILE, width), BF16), shape((width, hidden), F32)),
        [vmem] * 3,
    )(got, keep, got_weight)
    return (out_act[None], grad_features[None], grad_weight)


def solution(mesh):
    fine = Mesh(mesh.devices.reshape([size for _, size in FINE]), [name for name, _ in FINE])
    in_specs = (
        P(COL, ROW, None),
        P(),
        P(COL, ROW, None),
        P(ROW, COL, None),
        P(ROW, COL, None),
        P(ROW, COL),
        P(ROW, COL, None, None),
        P(ROW, COL, None, None),
        P(ROW, COL, None, None),
    )
    out_specs = (P(COL, ROW, None), P(COL, ROW, None), P())
    return jax.shard_map(local, mesh=fine, in_specs=in_specs, out_specs=out_specs, check_vma=False)
```

```python
import math

import jax
import jax.numpy as jnp
from jax import lax
from jax.experimental import pallas as pl
from jax.experimental.pallas import tpu as pltpu
from jax.sharding import Mesh
from jax.sharding import PartitionSpec as P

TILE = 128
GROUP = 16
FINE = (("x", 4), ("zh", 2), ("y", 4), ("z2", 2), ("z4", 4), ("core", 2))
N_X, N_ZH, N_Y, N_Z2, N_Z4, N_CORE = (size for _, size in FINE)
N_ZL = N_Z2 * N_Z4
ROW = ("x", "zh")
COL = ("y", "z2", "z4", "core")
W_ROWS = 64
VMEM_LIMIT = 48 * 1024 * 1024
BF16 = jnp.bfloat16
F32 = jnp.float32

vmem = pl.BlockSpec(memory_space=pltpu.VMEM)
smem = pl.BlockSpec(memory_space=pltpu.SMEM)
hbm = pl.BlockSpec(memory_space=pl.ANY)


def call(body, outs, in_specs, scratch=(), flops=0, moved=0):
    return pl.pallas_call(
        body,
        out_shape=outs,
        in_specs=in_specs,
        out_specs=jax.tree.map(lambda _: vmem, outs),
        scratch_shapes=list(scratch),
        compiler_params=pltpu.CompilerParams(vmem_limit_bytes=VMEM_LIMIT),
        cost_estimate=pl.CostEstimate(flops=flops, bytes_accessed=moved, transcendentals=0),
    )


def halves(value):
    high = value.astype(BF16)
    return high, (value - high.astype(F32)).astype(BF16)


def group_total(count_ref):
    return (count_ref[0, 0] + GROUP - 1) // GROUP


def tile_place(row):
    near = row // N_CORE
    return near // N_ZL * N_ZL + near % N_Z4 * N_Z2 + near // N_Z4 % N_Z2


def pair_body(zh_ref, own_ref, other_ref, send_ref):
    mine = zh_ref[0] == 0
    own, other = own_ref[...], other_ref[...]
    first, second = jnp.where(mine, own, other), jnp.where(mine, other, own)
    for peer in range(N_X):
        send_ref[peer, 0] = first
        send_ref[peer, 1] = second


def build_body(count_ref, rows_ref, cols_ref, weight_ref, tiles_ref, live_ref):
    slots, edges = rows_ref.shape
    slot_ids = lax.broadcasted_iota(jnp.int32, (slots, edges), 0)
    live_ref[...] = jnp.where(slot_ids < count_ref[0, 0], weight_ref[...].astype(F32), 0.0)
    positions = lax.broadcasted_iota(jnp.int32, (TILE, edges), 0)

    def step(group, carry):
        for i in range(GROUP):
            slot = group * GROUP + i
            row_hot = jnp.where(positions == rows_ref[pl.ds(slot, 1), :], 1.0, 0.0).astype(BF16)
            col_hot = jnp.where(
                positions == cols_ref[pl.ds(slot, 1), :], live_ref[pl.ds(slot, 1), :], 0.0
            ).astype(BF16)
            built = lax.dot_general(
                row_hot, col_hot, (((1,), (1,)), ((), ())), preferred_element_type=F32
            )
            tiles_ref[slot] = built.astype(BF16)
        return carry

    lax.fori_loop(0, group_total(count_ref), step, 0)


def forward_body(
    count_ref, core_ref, row_ref, col_ref, tiles_ref, feats_ref, send_ref, keep_ref, acc_ref
):
    acc_ref[...] = jnp.zeros_like(acc_ref)
    core = core_ref[0]

    def step(group, carry):
        products = []
        for i in range(GROUP):
            slot = group * GROUP + i
            products.append(
                jnp.dot(tiles_ref[slot], feats_ref[col_ref[0, slot]], preferred_element_type=F32)
            )
        for i in range(GROUP):
            row = row_ref[0, group * GROUP + i]
            acc_ref[row % N_CORE, tile_place(row)] += products[i]
        return carry

    lax.fori_loop(0, group_total(count_ref), step, 0)
    send_ref[...] = acc_ref[1 - core].astype(BF16)
    keep_ref[...] = acc_ref[core]


def merge_body(got_ref, keep_ref, out_ref):
    out_ref[...] = (keep_ref[...] + got_ref[...].astype(F32)).astype(BF16)


def dense_body(
    z2_ref, own_ref, other_ref, weight_ref, up_ref, other_up_ref, act_ref, send_ref, *, scale
):
    first = z2_ref[0] == 0
    total = own_ref[...].astype(F32) + other_ref[...].astype(F32)
    aggregated = total.reshape(N_Z2 * TILE, TILE).astype(BF16)
    weight = weight_ref[...]
    own_up, other_up = up_ref[...], other_up_ref[...]
    up = jnp.concatenate(
        [jnp.where(first, own_up, other_up), jnp.where(first, other_up, own_up)], axis=0
    )
    pre_act = jnp.dot(aggregated, weight, preferred_element_type=F32)
    gate = jax.nn.sigmoid(pre_act)
    act = (pre_act * gate).astype(BF16)
    act_ref[...] = jnp.where(first, act[:TILE], act[TILE:])
    grad_pre = (up.astype(F32) * gate * (1.0 + pre_act * (1.0 - gate))).astype(BF16)
    local_weight = (
        lax.dot_general(aggregated, grad_pre, (((0,), (0,)), ((), ())), preferred_element_type=F32)
        * scale
    )
    high, low = halves(local_weight)
    deep = TILE // N_Z4
    for z2 in range(N_Z2):
        grad_agg = lax.dot_general(
            weight,
            grad_pre[z2 * TILE : (z2 + 1) * TILE],
            (((1,), (1,)), ((), ())),
            preferred_element_type=F32,
        ).astype(BF16)
        for peer in range(N_Z4):
            send_ref[peer, z2 * TILE : (z2 + 1) * TILE, :] = grad_agg
    for peer in range(N_Z4):
        here = slice(peer * deep, (peer + 1) * deep)
        for k, part in enumerate(
            (high[here, :TILE], high[here, TILE:], low[here, :TILE], low[here, TILE:])
        ):
            start = N_Z2 * TILE + k * deep
            send_ref[peer, start : start + deep, :] = part


def spread_body(got_ref, send_ref):
    terms = jnp.sum(got_ref[:, N_Z2 * TILE :, :].astype(F32), axis=0)
    high, low = halves(terms[:W_ROWS] + terms[W_ROWS:])
    for peer in range(N_Y):
        for z4 in range(N_Z4):
            here = slice(z4 * N_Z2 * TILE, (z4 + 1) * N_Z2 * TILE)
            send_ref[peer, here, :] = got_ref[z4, 0 : N_Z2 * TILE, :]
        send_ref[peer, N_ZL * TILE : N_ZL * TILE + W_ROWS, :] = high
        send_ref[peer, N_ZL * TILE + W_ROWS :, :] = low


def backward_body(
    count_ref, core_ref, x_ref, row_ref, col_ref, tiles_ref, own_ref, other_ref, *refs
):
    send_refs, (send_weight_ref, keep_ref, grads_ref, acc_ref, sems) = refs[: N_X - 1], refs[N_X - 1 :]
    core = core_ref[0]
    copies = [
        pltpu.make_async_copy(own_ref, grads_ref.at[core], sems.at[0]),
        pltpu.make_async_copy(other_ref, grads_ref.at[1 - core], sems.at[1]),
    ]
    for copy in copies:
        copy.start()
    acc_ref[...] = jnp.zeros_like(acc_ref)
    for copy in copies:
        copy.wait()

    def step(group, carry):
        products = []
        for i in range(GROUP):
            slot = group * GROUP + i
            row = row_ref[0, slot]
            place = tile_place(row)
            start = pl.multiple_of(place % N_ZL * TILE, TILE)
            grad = grads_ref[row % N_CORE, place // N_ZL, pl.ds(start, TILE), :]
            products.append(jnp.dot(grad, tiles_ref[slot], preferred_element_type=F32))
        for i in range(GROUP):
            acc_ref[col_ref[0, group * GROUP + i]] += products[i]
        return carry

    lax.fori_loop(0, group_total(count_ref), step, 0)
    terms = jnp.sum(grads_ref[:, :, N_ZL * TILE :, :].astype(F32), axis=(0, 1))
    weight_sum = (terms[:W_ROWS] + terms[W_ROWS:]).astype(BF16)
    for peer in range(N_X * N_Z4):
        send_weight_ref[peer] = weight_sum
    for shift in range(N_X):
        peer = (x_ref[0] + shift) % N_X
        part = acc_ref[pl.ds(peer * N_ZH, N_ZH)].reshape(N_ZH * TILE, TILE)
        if shift == 0:
            keep_ref[...] = part.astype(BF16)
        else:
            send_refs[shift - 1][...] = part.astype(BF16)


def halfway_body(zh_ref, own_ref, *refs):
    got_refs, (got_weight_ref, send_ref, keep_ref) = refs[: N_X - 1], refs[N_X - 1 :]
    total = own_ref[...].astype(F32)
    for got_ref in got_refs:
        total += got_ref[...].astype(F32)
    first, second = total[:TILE], total[TILE:]
    mine = zh_ref[0] == 0
    keep_ref[...] = jnp.where(mine, first, second)
    send_ref[0:TILE, :] = jnp.where(mine, second, first).astype(BF16)
    for z4 in range(N_Z4):
        terms = got_weight_ref[z4].astype(F32)
        for x in range(1, N_X):
            terms += got_weight_ref[x * N_Z4 + z4].astype(F32)
        send_ref[TILE + z4 * W_ROWS : TILE + (z4 + 1) * W_ROWS, :] = terms.astype(BF16)


def finish_body(got_ref, keep_ref, sent_ref, grad_ref, grad_weight_ref):
    grad_ref[...] = (keep_ref[...] + got_ref[0:TILE, :].astype(F32)).T.astype(BF16)
    deep = TILE // N_Z4
    total = got_ref[TILE:, :].astype(F32) + sent_ref[TILE:, :].astype(F32)
    for z4 in range(N_Z4):
        part = total[z4 * W_ROWS : (z4 + 1) * W_ROWS]
        grad_weight_ref[z4 * deep : (z4 + 1) * deep, :TILE] = part[:deep]
        grad_weight_ref[z4 * deep : (z4 + 1) * deep, TILE:] = part[deep:]


def swap(value, axis):
    return lax.ppermute(value, axis, [(0, 1), (1, 0)])


def exchange(value, axis):
    return lax.all_to_all(value, axis, 0, 0, tiled=True)


def local(
    features, weight, upstream, tile_rows, tile_cols, tile_count, edge_rows, edge_cols, edge_weight
):
    width = features.shape[2]
    hidden = weight.shape[1]
    slots, edges = edge_rows.shape[2:]
    row_tiles, col_tiles = tile_rows[0], tile_cols[0]
    blocks = N_Y * N_ZL * N_CORE
    shape = jax.ShapeDtypeStruct

    zh = lax.axis_index("zh")
    own = features[0]
    other = swap(own, "zh")
    zh_here = zh.astype(jnp.int32)[None]
    pair = call(pair_body, shape((N_X, N_ZH, TILE, width), BF16), [smem, vmem, vmem])(
        zh_here, own, other
    )
    column = exchange(pair, "x").reshape(N_X * N_ZH, TILE, width)

    tiles = call(
        build_body,
        shape((slots, TILE, TILE), BF16),
        [smem, vmem, vmem, vmem],
        [pltpu.VMEM((slots, edges), F32)],
        flops=slots * TILE * TILE * edges * 8,
        moved=slots * TILE * TILE * 2,
    )(tile_count, edge_rows[0, 0], edge_cols[0, 0], edge_weight[0, 0])

    core = lax.axis_index("core").astype(jnp.int32)[None]
    half = (blocks // N_CORE, TILE, width)
    send, keep = call(
        forward_body,
        (shape(half, BF16), shape(half, F32)),
        [smem, smem, smem, smem, vmem, vmem],
        [pltpu.VMEM((N_CORE,) + half, F32)],
        flops=slots * TILE * TILE * width * 2,
        moved=slots * TILE * TILE * 4,
    )(tile_count, core, row_tiles, col_tiles, tiles, column)

    partial = call(merge_body, shape(half, BF16), [vmem, vmem])(swap(send, "core"), keep)
    partial, up = lax.optimization_barrier((partial, upstream[0]))
    got, other_up = lax.optimization_barrier((exchange(partial, "y"), swap(up, "z2")))
    got = got.reshape((N_Y, N_ZL, TILE, width))
    partial = jnp.sum(got.astype(F32), axis=0).astype(BF16)
    got = exchange(partial, "z4").reshape((N_Z4, N_Z2, TILE, width))
    partial = jnp.sum(got.astype(F32), axis=0).astype(BF16)

    node_total = features.shape[1] * N_X * N_ZH * blocks
    scale = 1.0 / math.sqrt(node_total)

    def dense(*refs):
        dense_body(*refs, scale=scale)

    out_act, send = call(
        dense,
        (shape((TILE, hidden), BF16), shape((N_Z4, N_Z2 * TILE + 2 * W_ROWS, TILE), BF16)),
        [smem] + [vmem] * 5,
    )(
        lax.axis_index("z2").astype(jnp.int32)[None],
        partial,
        swap(partial, "z2"),
        weight,
        up,
        other_up,
    )

    got = exchange(send, "z4")
    send = call(spread_body, shape((N_Y, N_ZL * TILE + 2 * W_ROWS, TILE), BF16), [vmem])(got)
    mine = exchange(send, "y")
    theirs = swap(mine, "core")
    part = (N_ZH * TILE, TILE)
    *sends, send_weight, keep = call(
        backward_body,
        (shape(part, BF16),) * (N_X - 1)
        + (shape((N_X * N_Z4, W_ROWS, TILE), BF16), shape(part, BF16)),
        [smem] * 5 + [vmem, hbm, hbm],
        [
            pltpu.VMEM((N_CORE,) + mine.shape, BF16),
            pltpu.VMEM((N_X * N_ZH, width, TILE), F32),
            pltpu.SemaphoreType.DMA((2,)),
        ],
    )(
        tile_count,
        core,
        lax.axis_index("x").astype(jnp.int32)[None],
        row_tiles,
        col_tiles,
        tiles,
        mine,
        theirs,
    )

    gots = [
        lax.ppermute(send, "x", [(k, (k + shift + 1) % N_X) for k in range(N_X)])
        for shift, send in enumerate(sends)
    ]
    got_weight = exchange(send_weight, ("x", "z4"))
    send, keep = call(
        halfway_body,
        (shape((TILE + N_Z4 * W_ROWS, TILE), BF16), shape((TILE, TILE), F32)),
        [smem] + [vmem] * (N_X + 1),
    )(zh_here, keep, *gots, got_weight)
    grad_features, grad_weight = call(
        finish_body,
        (shape((TILE, width), BF16), shape((width, hidden), F32)),
        [vmem] * 3,
    )(swap(send, "zh"), keep, send)
    return (out_act[None], grad_features[None], grad_weight)


def solution(mesh):
    fine = Mesh(mesh.devices.reshape([size for _, size in FINE]), [name for name, _ in FINE])
    in_specs = (
        P(COL, ROW, None),
        P(),
        P(COL, ROW, None),
        P(ROW, COL, None),
        P(ROW, COL, None),
        P(ROW, COL),
        P(ROW, COL, None, None),
        P(ROW, COL, None, None),
        P(ROW, COL, None, None),
    )
    out_specs = (P(COL, ROW, None), P(COL, ROW, None), P())
    return jax.shard_map(local, mesh=fine, in_specs=in_specs, out_specs=out_specs, check_vma=False)
```

```python
import functools
import math

import jax
import jax.numpy as jnp
from jax import lax
from jax.experimental import pallas as pl
from jax.experimental.pallas import tpu as pltpu
from jax.sharding import Mesh
from jax.sharding import PartitionSpec as P

TILE = 128
GROUP = 16
FINE = (("x", 4), ("zh", 2), ("y", 4), ("z2", 2), ("z4", 4), ("core", 2))
N_X, N_ZH, N_Y, N_Z2, N_Z4, N_CORE = (size for _, size in FINE)
N_ZL = N_Z2 * N_Z4
ROW = ("x", "zh")
COL = ("y", "z2", "z4", "core")
LISTS = N_Y * N_CORE
PLANE = N_X * N_Y
LARGE = 50
W_ROWS = 64
BF16 = jnp.bfloat16
F32 = jnp.float32
I32 = jnp.int32

vmem = pl.BlockSpec(memory_space=pltpu.VMEM)
smem = pl.BlockSpec(memory_space=pltpu.SMEM)
hbm = pl.BlockSpec(memory_space=pltpu.HBM)
shape = jax.ShapeDtypeStruct


def call(body, outs, in_specs, out_specs=None, scratch=(), flops=0, moved=0, limit=24):
    return pl.pallas_call(
        body,
        out_shape=outs,
        in_specs=in_specs,
        out_specs=jax.tree.map(lambda _: vmem, outs) if out_specs is None else out_specs,
        scratch_shapes=list(scratch),
        compiler_params=pltpu.CompilerParams(vmem_limit_bytes=limit * 1024 * 1024),
        cost_estimate=pl.CostEstimate(flops=flops, bytes_accessed=moved, transcendentals=0),
    )


def halves(value):
    high = value.astype(BF16)
    return high, (value - high.astype(F32)).astype(BF16)


def pair_body(zh_ref, own_ref, other_ref, send_ref):
    mine = zh_ref[0] == 0
    own, other = own_ref[...], other_ref[...]
    first, second = jnp.where(mine, own, other), jnp.where(mine, other, own)
    for peer in range(PLANE):
        send_ref[peer, 0] = first
        send_ref[peer, 1] = second


def pack_body(
    rows_hbm, cols_hbm, weight_hbm, row_hbm, col_hbm, count_ref, send_ref,
    rows_ref, cols_ref, weight_ref, row_ref, col_ref, sems,
):
    copies = [
        pltpu.make_async_copy(source, target, sems.at[k])
        for k, (source, target) in enumerate(
            (
                (rows_hbm, rows_ref),
                (cols_hbm, cols_ref),
                (weight_hbm, weight_ref),
                (row_hbm, row_ref),
                (col_hbm, col_ref),
            )
        )
    ]
    for copy in copies:
        copy.start()
    for copy in copies:
        copy.wait()
    slots, edges = rows_ref.shape
    rows = rows_ref[...].astype(F32)
    cols = cols_ref[...].astype(F32)
    weight = weight_ref[...].astype(F32)
    line = lax.broadcasted_iota(I32, (slots, slots), 0)
    meta = jnp.where(line == 0, row_ref[...], jnp.where(line == 1, col_ref[...], count_ref[0, 0]))
    blocks = (
        rows[:, :TILE],
        cols[:, :TILE],
        weight[:, :TILE],
        jnp.concatenate([rows[:, TILE:], cols[:, TILE:]], axis=1),
        jnp.concatenate([weight[:, TILE:], meta.astype(F32)], axis=1),
    )
    for k, block in enumerate(blocks):
        block = block.astype(BF16)
        for peer in range(send_ref.shape[0]):
            send_ref[peer, k * slots : (k + 1) * slots, :] = block


def fetch(tiles_hbm, tiles_ref, sems, group):
    here = pl.ds(group * GROUP, GROUP)
    return pltpu.make_async_copy(tiles_hbm.at[here], tiles_ref.at[here], sems.at[group])


def fetch_all(total_ref, tiles_hbm, tiles_ref, sems):
    def start(group, carry):
        fetch(tiles_hbm, tiles_ref, sems, group).start()
        return carry

    lax.fori_loop(0, total_ref[1] // GROUP, start, 0)


def build_body(
    where_ref, got_ref, tiles_hbm, zl_ref, src_ref, total_ref,
    slot_ref, edge_rows_ref, edge_cols_ref, weight_ref, meta_ref, slots_ref, sem, stage_ref, sems,
):
    y, core = where_ref[0], where_ref[1]
    slots = got_ref.shape[1] // 5
    edges = edge_rows_ref.shape[1]
    rest = edges - TILE
    dummy = LISTS * slots
    for index in range(LISTS):
        meta = got_ref[index, 4 * slots : 4 * slots + 16, :].astype(F32)
        meta_ref[index * 8 : (index + 1) * 8, :] = meta[:8].astype(I32)
    copy = pltpu.make_async_copy(meta_ref, slots_ref, sem)
    copy.start()
    for index in range(LISTS):
        here = slice(index * slots, (index + 1) * slots)
        block = [got_ref[index, k * slots : (k + 1) * slots, :].astype(F32) for k in range(5)]
        edge_rows_ref[here, :TILE] = block[0]
        edge_cols_ref[here, :TILE] = block[1]
        weight_ref[here, :TILE] = block[2]
        edge_rows_ref[here, TILE:] = block[3][:, :rest]
        edge_cols_ref[here, TILE:] = block[3][:, rest:]
        weight_ref[here, TILE:] = block[4][:, :rest]
    for ref in (edge_rows_ref, edge_cols_ref, weight_ref):
        ref[dummy:, :] = jnp.zeros_like(ref[dummy:, :])
    copy.wait()

    used = jnp.int32(0)
    for part in range(N_CORE):
        column_core = core if part == 0 else 1 - core
        for column_y in range(N_Y):
            index = column_y * N_CORE + column_core

            def scan(slot, used, index=index, column_y=column_y):
                row, col = slots_ref[index * 8, rest + slot], slots_ref[index * 8 + 1, rest + slot]
                slot_ref[used] = index * slots + slot
                near = row // N_CORE
                zl_ref[used] = near % N_Z4 * N_Z2 + near // N_Z4 % N_Z2
                src_ref[used] = (col // N_ZH * N_Y + column_y) * N_ZH + col % N_ZH
                mine = (row // (N_CORE * N_ZL) == y) & (row % N_CORE == core)
                return used + mine.astype(I32)

            used = lax.fori_loop(0, slots_ref[index * 8 + 2, rest], scan, used)
        for extra in range(GROUP - 1):
            slot_ref[used + extra] = dummy
            zl_ref[used + extra] = 0
            src_ref[used + extra] = 0
        used = (used + GROUP - 1) // GROUP * GROUP
        total_ref[part] = used

    positions = lax.broadcasted_iota(I32, (TILE, edges), 0).astype(F32)

    def store(group):
        place = group % 2
        here = pl.ds(group * GROUP, GROUP)
        return pltpu.make_async_copy(stage_ref.at[place], tiles_hbm.at[here], sems.at[place])

    def step(group, carry):
        @pl.when(group >= 2)
        def _():
            store(group - 2).wait()

        for i in range(GROUP):
            entry = group * GROUP + i
            slot = slot_ref[entry]
            row_hot = jnp.where(positions == edge_rows_ref[pl.ds(slot, 1), :], 1.0, 0.0)
            col_hot = jnp.where(
                positions == edge_cols_ref[pl.ds(slot, 1), :], weight_ref[pl.ds(slot, 1), :], 0.0
            )
            built = lax.dot_general(
                row_hot.astype(BF16),
                col_hot.astype(BF16),
                (((1,), (1,)), ((), ())),
                preferred_element_type=F32,
            )
            stage_ref[group % 2, i] = built.astype(BF16)
        store(group).start()
        return carry

    groups = used // GROUP
    lax.fori_loop(0, groups, step, 0)
    for back in (2, 1):

        @pl.when(groups >= back)
        def _(back=back):
            store(groups - back).wait()


def forward_body(
    total_ref, zl_ref, src_ref, tiles_hbm, own_ref, other_ref, send_ref, acc_ref, tiles_ref, sems
):
    fetch_all(total_ref, tiles_hbm, tiles_ref, sems)
    acc_ref[...] = jnp.zeros_like(acc_ref)

    def step(feats_ref, group, carry):
        fetch(tiles_hbm, tiles_ref, sems, group).wait()
        products = []
        for i in range(GROUP):
            entry = group * GROUP + i
            products.append(
                jnp.dot(tiles_ref[entry], feats_ref[src_ref[entry]], preferred_element_type=F32)
            )
        for i in range(GROUP):
            acc_ref[zl_ref[group * GROUP + i]] += products[i]
        return carry

    middle, end = total_ref[0] // GROUP, total_ref[1] // GROUP
    lax.fori_loop(0, middle, functools.partial(step, own_ref), 0)
    lax.fori_loop(middle, end, functools.partial(step, other_ref), 0)
    send_ref[...] = acc_ref[...].astype(BF16)


def dense_body(
    z2_ref, own_ref, other_ref, weight_ref, up_ref, other_up_ref, act_ref, send_ref, *, scale
):
    first = z2_ref[0] == 0
    total = own_ref[...].astype(F32) + other_ref[...].astype(F32)
    aggregated = total.reshape(N_Z2 * TILE, TILE).astype(BF16)
    weight = weight_ref[...]
    own_up, other_up = up_ref[...], other_up_ref[...]
    up = jnp.concatenate(
        [jnp.where(first, own_up, other_up), jnp.where(first, other_up, own_up)], axis=0
    )
    pre_act = jnp.dot(aggregated, weight, preferred_element_type=F32)
    gate = jax.nn.sigmoid(pre_act)
    act = (pre_act * gate).astype(BF16)
    act_ref[...] = jnp.where(first, act[:TILE], act[TILE:])
    grad_pre = (up.astype(F32) * gate * (1.0 + pre_act * (1.0 - gate))).astype(BF16)
    local_weight = (
        lax.dot_general(aggregated, grad_pre, (((0,), (0,)), ((), ())), preferred_element_type=F32)
        * scale
    ).astype(BF16)
    deep = TILE // N_Z4
    for z2 in range(N_Z2):
        grad_agg = lax.dot_general(
            weight,
            grad_pre[z2 * TILE : (z2 + 1) * TILE],
            (((1,), (1,)), ((), ())),
            preferred_element_type=F32,
        ).astype(BF16)
        for peer in range(N_Z4):
            send_ref[peer, z2 * TILE : (z2 + 1) * TILE, :] = grad_agg
    for peer in range(N_Z4):
        here = slice(peer * deep, (peer + 1) * deep)
        send_ref[peer, N_Z2 * TILE : N_Z2 * TILE + deep, :] = local_weight[here, :TILE]
        send_ref[peer, N_Z2 * TILE + deep :, :] = local_weight[here, TILE:]


def backward_body(
    total_ref, zl_ref, src_ref, tiles_hbm, got_ref, send_ref, keep_ref, keep_weight_ref,
    acc_ref, tiles_ref, sems,
):
    fetch_all(total_ref, tiles_hbm, tiles_ref, sems)
    acc_ref[...] = jnp.zeros_like(acc_ref)

    def step(part, group, carry):
        fetch(tiles_hbm, tiles_ref, sems, group).wait()
        products = []
        for i in range(GROUP):
            entry = group * GROUP + i
            place = zl_ref[entry]
            start = pl.multiple_of(place % N_Z2 * TILE, TILE)
            grad = got_ref[place // N_Z2, pl.ds(start, TILE), :]
            products.append(jnp.dot(grad, tiles_ref[entry], preferred_element_type=F32))
        for i in range(GROUP):
            acc_ref[part, src_ref[group * GROUP + i]] += products[i]
        return carry

    middle, end = total_ref[0] // GROUP, total_ref[1] // GROUP
    lax.fori_loop(0, middle, functools.partial(step, 0), 0)
    lax.fori_loop(middle, end, functools.partial(step, 1), 0)
    keep_ref[...] = acc_ref[0]
    tiles = acc_ref.shape[1]
    send_ref[0:tiles] = acc_ref[1].astype(BF16)
    high, low = halves(jnp.sum(got_ref[:, N_Z2 * TILE :, :].astype(F32), axis=0))
    keep_weight_ref[...] = high.astype(F32) + low.astype(F32)
    send_ref[tiles, 0:W_ROWS, :] = high
    send_ref[tiles, W_ROWS : 2 * W_ROWS, :] = low


def merge_body(got_ref, keep_ref, keep_weight_ref, send_ref):
    tiles = keep_ref.shape[0]
    terms = got_ref[tiles, 0 : 2 * W_ROWS, :].astype(F32)
    part = (keep_weight_ref[...] + (terms[:W_ROWS] + terms[W_ROWS:])).astype(BF16)
    for peer in range(PLANE):
        for zh in range(N_ZH):
            tile = peer * N_ZH + zh
            send_ref[peer, zh * TILE : (zh + 1) * TILE, :] = (
                keep_ref[tile] + got_ref[tile].astype(F32)
            ).astype(BF16)
        send_ref[peer, N_ZH * TILE :, :] = part


def halfway_body(zh_ref, got_ref, send_ref, keep_ref, send_weight_ref):
    zh = zh_ref[0]
    total = jnp.sum(got_ref[...].astype(F32), axis=0)
    first, second = total[:TILE], total[TILE : N_ZH * TILE]
    mine = zh == 0
    keep_ref[...] = jnp.where(mine, first, second)
    send_ref[...] = jnp.where(mine, second, first).astype(BF16)
    weight_sum = total[N_ZH * TILE :].astype(BF16)
    for peer in range(N_ZH * N_Z4):
        send_weight_ref[peer] = weight_sum


def finish_body(got_ref, keep_ref, got_weight_ref, grad_ref, grad_weight_ref):
    grad_ref[...] = (keep_ref[...] + got_ref[...].astype(F32)).T.astype(BF16)
    deep = TILE // N_Z4
    for k in range(N_Z4):
        total = got_weight_ref[k].astype(F32) + got_weight_ref[N_Z4 + k].astype(F32)
        grad_weight_ref[k * deep : (k + 1) * deep, :TILE] = total[:deep]
        grad_weight_ref[k * deep : (k + 1) * deep, TILE:] = total[deep:]


def swap(value, axis):
    return lax.ppermute(value, axis, [(0, 1), (1, 0)])


def exchange(value, axis):
    return lax.all_to_all(value, axis, 0, 0, tiled=True)


def local(
    features, weight, upstream, tile_rows, tile_cols, tile_count, edge_rows, edge_cols, edge_weight
):
    width = features.shape[2]
    hidden = weight.shape[1]
    slots, edges = edge_rows.shape[2:]
    column_tiles = PLANE * N_ZH
    most = slots + (LISTS - 1) * slots // 2 + 2 * GROUP
    tile_room = [pltpu.VMEM((most, TILE, TILE), BF16), pltpu.SemaphoreType.DMA((most // GROUP,))]
    zh = lax.axis_index("zh")
    where = jnp.stack([lax.axis_index("y"), lax.axis_index("core")]).astype(I32)

    own = features[0]
    other = swap(own, "zh")

    send = call(
        pack_body,
        shape((LISTS, 5 * slots, TILE), BF16),
        [hbm] * 5 + [smem],
        scratch=[
            pltpu.VMEM((slots, edges), I32),
            pltpu.VMEM((slots, edges), I32),
            pltpu.VMEM((slots, edges), BF16),
            pltpu.VMEM((1, slots), I32),
            pltpu.VMEM((1, slots), I32),
            pltpu.SemaphoreType.DMA((5,)),
        ],
    )(edge_rows[0, 0], edge_cols[0, 0], edge_weight[0, 0], tile_rows[0], tile_cols[0], tile_count)
    lists = exchange(send, ("y", "core"))
    other, lists = lax.optimization_barrier((other, lists))
    tiles, zl_list, src_list, total = call(
        build_body,
        (
            shape((most, TILE, TILE), BF16),
            shape((most,), I32),
            shape((most,), I32),
            shape((N_CORE,), I32),
        ),
        [smem, vmem],
        (hbm, smem, smem, smem),
        [pltpu.SMEM((most,), I32)]
        + [pltpu.VMEM((LISTS * slots + 8, edges), F32)] * 3
        + [
            pltpu.VMEM((LISTS * 8, TILE), I32),
            pltpu.SMEM((LISTS * 8, TILE), I32),
            pltpu.SemaphoreType.DMA,
            pltpu.VMEM((2, GROUP, TILE, TILE), BF16),
            pltpu.SemaphoreType.DMA((2,)),
        ],
        flops=slots * TILE * TILE * edges * 4,
        moved=slots * TILE * TILE * 2,
        limit=LARGE,
    )(where, lists)

    zh_here = zh.astype(I32)[None]
    pair = call(pair_body, shape((PLANE, N_ZH, TILE, width), BF16), [smem, vmem, vmem])(
        zh_here, own, other
    )
    pair, up = lax.optimization_barrier((pair, upstream[0]))
    mine = exchange(pair, ("x", "y")).reshape(column_tiles, TILE, width)
    mine, total, other_up = lax.optimization_barrier((mine, total, swap(up, "z2")))
    theirs = swap(mine, "core")

    partial = call(
        forward_body,
        shape((N_ZL, TILE, width), BF16),
        [smem] * 3 + [hbm, vmem, vmem],
        scratch=[pltpu.VMEM((N_ZL, TILE, width), F32)] + tile_room,
        limit=LARGE,
    )(total, zl_list, src_list, tiles, mine, theirs)

    got = exchange(partial, "z4").reshape((N_Z4, N_Z2, TILE, width))
    partial = jnp.sum(got.astype(F32), axis=0).astype(BF16)

    node_total = features.shape[1] * N_X * N_ZH * N_Y * N_ZL * N_CORE
    out_act, send = call(
        functools.partial(dense_body, scale=1.0 / math.sqrt(node_total)),
        (shape((TILE, hidden), BF16), shape((N_Z4, N_Z2 * TILE + W_ROWS, TILE), BF16)),
        [smem] + [vmem] * 5,
    )(
        lax.axis_index("z2").astype(I32)[None],
        partial,
        swap(partial, "z2"),
        weight,
        up,
        other_up,
    )

    got = exchange(send, "z4")
    send, keep, keep_weight = call(
        backward_body,
        (
            shape((column_tiles + 1, width, TILE), BF16),
            shape((column_tiles, width, TILE), F32),
            shape((W_ROWS, TILE), F32),
        ),
        [smem] * 3 + [hbm, vmem],
        scratch=[pltpu.VMEM((N_CORE, column_tiles, width, TILE), F32)] + tile_room,
        limit=LARGE,
    )(total, zl_list, src_list, tiles, got)

    send = call(merge_body, shape((PLANE, N_ZH * TILE + W_ROWS, TILE), BF16), [vmem] * 3)(
        swap(send, "core"), keep, keep_weight
    )
    got = exchange(send, ("x", "y"))
    send, keep, send_weight = call(
        halfway_body,
        (
            shape((TILE, TILE), BF16),
            shape((TILE, TILE), F32),
            shape((N_ZH * N_Z4, W_ROWS, TILE), BF16),
        ),
        [smem, vmem],
    )(zh_here, got)
    got = swap(send, "zh")
    got_weight = exchange(send_weight, ("zh", "z4"))
    grad_features, grad_weight = call(
        finish_body,
        (shape((TILE, width), BF16), shape((width, hidden), F32)),
        [vmem] * 3,
    )(got, keep, got_weight)
    return (out_act[None], grad_features[None], grad_weight)


def solution(mesh):
    fine = Mesh(mesh.devices.reshape([size for _, size in FINE]), [name for name, _ in FINE])
    in_specs = (
        P(COL, ROW, None),
        P(),
        P(COL, ROW, None),
        P(ROW, COL, None),
        P(ROW, COL, None),
        P(ROW, COL),
        P(ROW, COL, None, None),
        P(ROW, COL, None, None),
        P(ROW, COL, None, None),
    )
    out_specs = (P(COL, ROW, None), P(COL, ROW, None), P())
    return jax.shard_map(local, mesh=fine, in_specs=in_specs, out_specs=out_specs, check_vma=False)
```

```python
import functools
import math

import jax
import jax.numpy as jnp
from jax import lax
from jax.experimental import pallas as pl
from jax.experimental.pallas import tpu as pltpu
from jax.sharding import Mesh
from jax.sharding import PartitionSpec as P

TILE = 128
GROUP = 16
BLOCK = 8
FINE = (("x", 4), ("zh", 2), ("y", 4), ("z2", 2), ("z4", 4), ("core", 2))
N_X, N_ZH, N_Y, N_Z2, N_Z4, N_CORE = (size for _, size in FINE)
N_ZL = N_Z2 * N_Z4
ROW = ("x", "zh")
COL = ("y", "z2", "z4", "core")
LISTS = N_Y * N_CORE
PLANE = N_X * N_Y
PACK = 62
LARGE = 50
W_ROWS = 64
BF16 = jnp.bfloat16
F32 = jnp.float32
I32 = jnp.int32

vmem = pl.BlockSpec(memory_space=pltpu.VMEM)
smem = pl.BlockSpec(memory_space=pltpu.SMEM)
hbm = pl.BlockSpec(memory_space=pltpu.HBM)
shape = jax.ShapeDtypeStruct


def call(body, outs, in_specs, out_specs=None, scratch=(), flops=0, moved=0, limit=24):
    return pl.pallas_call(
        body,
        out_shape=outs,
        in_specs=in_specs,
        out_specs=jax.tree.map(lambda _: vmem, outs) if out_specs is None else out_specs,
        scratch_shapes=list(scratch),
        compiler_params=pltpu.CompilerParams(vmem_limit_bytes=limit * 1024 * 1024),
        cost_estimate=pl.CostEstimate(flops=flops, bytes_accessed=moved, transcendentals=0),
    )


def halves(value):
    high = value.astype(BF16)
    return high, (value - high.astype(F32)).astype(BF16)


def pair_body(zh_ref, own_ref, other_ref, send_ref):
    mine = zh_ref[0] == 0
    own, other = own_ref[...], other_ref[...]
    first, second = jnp.where(mine, own, other), jnp.where(mine, other, own)
    for peer in range(PLANE):
        send_ref[peer, 0] = first
        send_ref[peer, 1] = second


def pack_body(
    rows_hbm, cols_hbm, weight_hbm, row_hbm, col_hbm, count_ref, send_ref,
    rows_ref, cols_ref, weight_ref, row_ref, col_ref, sems,
):
    copies = [
        pltpu.make_async_copy(source, target, sems.at[k])
        for k, (source, target) in enumerate(
            (
                (rows_hbm, rows_ref),
                (cols_hbm, cols_ref),
                (weight_hbm, weight_ref),
                (row_hbm, row_ref),
                (col_hbm, col_ref),
            )
        )
    ]
    for copy in copies:
        copy.start()
    for copy in copies:
        copy.wait()
    slots, edges = rows_ref.shape
    rows = rows_ref[...].astype(F32)
    cols = cols_ref[...].astype(F32)
    weight = weight_ref[...].astype(F32)
    line = lax.broadcasted_iota(I32, (slots, slots), 0)
    meta = jnp.where(line == 0, row_ref[...], jnp.where(line == 1, col_ref[...], count_ref[0, 0]))
    blocks = (
        rows[:, :TILE],
        cols[:, :TILE],
        weight[:, :TILE],
        jnp.concatenate([rows[:, TILE:], cols[:, TILE:]], axis=1),
        jnp.concatenate([weight[:, TILE:], meta.astype(F32)], axis=1),
    )
    for k, block in enumerate(blocks):
        block = block.astype(BF16)
        for peer in range(send_ref.shape[0]):
            send_ref[peer, k * slots : (k + 1) * slots, :] = block


def fetch(tiles_hbm, tiles_ref, sems, group):
    here = pl.ds(group * GROUP, GROUP)
    return pltpu.make_async_copy(tiles_hbm.at[here], tiles_ref.at[here], sems.at[group])


def fetch_all(total_ref, tiles_hbm, tiles_ref, sems):
    def start(group, carry):
        fetch(tiles_hbm, tiles_ref, sems, group).start()
        return carry

    lax.fori_loop(0, total_ref[1] // GROUP, start, 0)


def build_body(
    where_ref, got_ref, tiles_hbm, zl_ref, src_ref, total_ref,
    slot_ref, edge_rows_ref, edge_cols_ref, weight_ref, meta_ref, slots_ref, sem, stage_ref, sems,
):
    y, core = where_ref[0], where_ref[1]
    slots = got_ref.shape[1] // 5
    edges = edge_rows_ref.shape[1]
    rest = edges - TILE
    dummy = LISTS * slots
    for index in range(LISTS):
        meta = got_ref[index, 4 * slots : 4 * slots + 16, :].astype(F32)
        meta_ref[index * 8 : (index + 1) * 8, :] = meta[:8].astype(I32)
    copy = pltpu.make_async_copy(meta_ref, slots_ref, sem)
    copy.start()
    for index in range(LISTS):
        here = slice(index * slots, (index + 1) * slots)
        block = [got_ref[index, k * slots : (k + 1) * slots, :].astype(F32) for k in range(5)]
        edge_rows_ref[here, :TILE] = block[0]
        edge_cols_ref[here, :TILE] = block[1]
        weight_ref[here, :TILE] = block[2]
        edge_rows_ref[here, TILE:] = block[3][:, :rest]
        edge_cols_ref[here, TILE:] = block[3][:, rest:]
        weight_ref[here, TILE:] = block[4][:, :rest]
    for ref in (edge_rows_ref, edge_cols_ref, weight_ref):
        ref[dummy:, :] = jnp.zeros_like(ref[dummy:, :])
    copy.wait()

    used = jnp.int32(0)
    for part in range(N_CORE):
        column_core = core if part == 0 else 1 - core
        for column_y in range(N_Y):
            index = column_y * N_CORE + column_core

            count = slots_ref[index * 8 + 2, rest]

            def scan(block, used, index=index, column_y=column_y, count=count):
                for i in range(BLOCK):
                    slot = block * BLOCK + i
                    row = slots_ref[index * 8, rest + slot]
                    col = slots_ref[index * 8 + 1, rest + slot]
                    slot_ref[used] = index * slots + slot
                    near = row // N_CORE
                    zl_ref[used] = near % N_Z4 * N_Z2 + near // N_Z4 % N_Z2
                    src_ref[used] = (col // N_ZH * N_Y + column_y) * N_ZH + col % N_ZH
                    mine = (near // N_ZL == y) & (row % N_CORE == core) & (slot < count)
                    used = used + mine.astype(I32)
                return used

            used = lax.fori_loop(0, (count + BLOCK - 1) // BLOCK, scan, used)
        for extra in range(GROUP - 1):
            slot_ref[used + extra] = dummy
            zl_ref[used + extra] = 0
            src_ref[used + extra] = 0
        used = (used + GROUP - 1) // GROUP * GROUP
        total_ref[part] = used

    positions = lax.broadcasted_iota(I32, (TILE, edges), 0).astype(F32)

    def store(group):
        place = group % 2
        here = pl.ds(group * GROUP, GROUP)
        return pltpu.make_async_copy(stage_ref.at[place], tiles_hbm.at[here], sems.at[place])

    def step(group, carry):
        @pl.when(group >= 2)
        def _():
            store(group - 2).wait()

        for i in range(GROUP):
            entry = group * GROUP + i
            slot = slot_ref[entry]
            row_hot = jnp.where(positions == edge_rows_ref[pl.ds(slot, 1), :], 1.0, 0.0)
            col_hot = jnp.where(
                positions == edge_cols_ref[pl.ds(slot, 1), :], weight_ref[pl.ds(slot, 1), :], 0.0
            )
            built = lax.dot_general(
                row_hot.astype(BF16),
                col_hot.astype(BF16),
                (((1,), (1,)), ((), ())),
                preferred_element_type=F32,
            )
            stage_ref[group % 2, i] = built.astype(BF16)
        store(group).start()
        return carry

    groups = used // GROUP
    lax.fori_loop(0, groups, step, 0)
    for back in (2, 1):

        @pl.when(groups >= back)
        def _(back=back):
            store(groups - back).wait()


def forward_body(
    total_ref, zl_ref, src_ref, tiles_hbm, own_ref, other_ref, send_ref, acc_ref, tiles_ref, sems
):
    fetch_all(total_ref, tiles_hbm, tiles_ref, sems)
    acc_ref[...] = jnp.zeros_like(acc_ref)

    def step(feats_ref, group, carry):
        fetch(tiles_hbm, tiles_ref, sems, group).wait()
        products = []
        for i in range(GROUP):
            entry = group * GROUP + i
            products.append(
                jnp.dot(tiles_ref[entry], feats_ref[src_ref[entry]], preferred_element_type=F32)
            )
        for i in range(GROUP):
            acc_ref[zl_ref[group * GROUP + i]] += products[i]
        return carry

    middle, end = total_ref[0] // GROUP, total_ref[1] // GROUP
    lax.fori_loop(0, middle, functools.partial(step, own_ref), 0)
    lax.fori_loop(middle, end, functools.partial(step, other_ref), 0)
    send_ref[...] = acc_ref[...].astype(BF16)


def dense_body(
    z2_ref, own_ref, other_ref, weight_ref, up_ref, other_up_ref, act_ref, send_ref, *, scale
):
    first = z2_ref[0] == 0
    total = own_ref[...].astype(F32) + other_ref[...].astype(F32)
    aggregated = total.reshape(N_Z2 * TILE, TILE).astype(BF16)
    weight = weight_ref[...]
    own_up, other_up = up_ref[...], other_up_ref[...]
    up = jnp.concatenate(
        [jnp.where(first, own_up, other_up), jnp.where(first, other_up, own_up)], axis=0
    )
    pre_act = jnp.dot(aggregated, weight, preferred_element_type=F32)
    gate = jax.nn.sigmoid(pre_act)
    act = (pre_act * gate).astype(BF16)
    act_ref[...] = jnp.where(first, act[:TILE], act[TILE:])
    grad_pre = (up.astype(F32) * gate * (1.0 + pre_act * (1.0 - gate))).astype(BF16)
    local_weight = (
        lax.dot_general(aggregated, grad_pre, (((0,), (0,)), ((), ())), preferred_element_type=F32)
        * scale
    ).astype(BF16)
    deep = TILE // N_Z4
    for z2 in range(N_Z2):
        grad_agg = lax.dot_general(
            weight,
            grad_pre[z2 * TILE : (z2 + 1) * TILE],
            (((1,), (1,)), ((), ())),
            preferred_element_type=F32,
        ).astype(BF16)
        for peer in range(N_Z4):
            send_ref[peer, z2 * TILE : (z2 + 1) * TILE, :] = grad_agg
    for peer in range(N_Z4):
        here = slice(peer * deep, (peer + 1) * deep)
        send_ref[peer, N_Z2 * TILE : N_Z2 * TILE + deep, :] = local_weight[here, :TILE]
        send_ref[peer, N_Z2 * TILE + deep :, :] = local_weight[here, TILE:]


def backward_body(
    total_ref, zl_ref, src_ref, tiles_hbm, got_ref, send_ref, keep_ref, keep_weight_ref,
    acc_ref, tiles_ref, sems,
):
    fetch_all(total_ref, tiles_hbm, tiles_ref, sems)
    acc_ref[...] = jnp.zeros_like(acc_ref)

    def step(part, group, carry):
        fetch(tiles_hbm, tiles_ref, sems, group).wait()
        products = []
        for i in range(GROUP):
            entry = group * GROUP + i
            place = zl_ref[entry]
            start = pl.multiple_of(place % N_Z2 * TILE, TILE)
            grad = got_ref[place // N_Z2, pl.ds(start, TILE), :]
            products.append(jnp.dot(grad, tiles_ref[entry], preferred_element_type=F32))
        for i in range(GROUP):
            acc_ref[part, src_ref[group * GROUP + i]] += products[i]
        return carry

    middle, end = total_ref[0] // GROUP, total_ref[1] // GROUP
    lax.fori_loop(0, middle, functools.partial(step, 0), 0)
    lax.fori_loop(middle, end, functools.partial(step, 1), 0)
    keep_ref[...] = acc_ref[0]
    tiles = acc_ref.shape[1]
    send_ref[0:tiles] = acc_ref[1].astype(BF16)
    high, low = halves(jnp.sum(got_ref[:, N_Z2 * TILE :, :].astype(F32), axis=0))
    keep_weight_ref[...] = high.astype(F32) + low.astype(F32)
    send_ref[tiles, 0:W_ROWS, :] = high
    send_ref[tiles, W_ROWS : 2 * W_ROWS, :] = low


def merge_body(got_ref, keep_ref, keep_weight_ref, send_ref):
    tiles = keep_ref.shape[0]
    terms = got_ref[tiles, 0 : 2 * W_ROWS, :].astype(F32)
    part = (keep_weight_ref[...] + (terms[:W_ROWS] + terms[W_ROWS:])).astype(BF16)
    for peer in range(PLANE):
        for zh in range(N_ZH):
            tile = peer * N_ZH + zh
            send_ref[peer, zh * TILE : (zh + 1) * TILE, :] = (
                keep_ref[tile] + got_ref[tile].astype(F32)
            ).astype(BF16)
        send_ref[peer, N_ZH * TILE :, :] = part


def halfway_body(zh_ref, got_ref, send_ref, keep_ref, send_weight_ref):
    zh = zh_ref[0]
    total = jnp.sum(got_ref[...].astype(F32), axis=0)
    first, second = total[:TILE], total[TILE : N_ZH * TILE]
    mine = zh == 0
    keep_ref[...] = jnp.where(mine, first, second)
    send_ref[...] = jnp.where(mine, second, first).astype(BF16)
    weight_sum = total[N_ZH * TILE :].astype(BF16)
    for peer in range(N_ZH * N_Z4):
        send_weight_ref[peer] = weight_sum


def finish_body(got_ref, keep_ref, got_weight_ref, grad_ref, grad_weight_ref):
    grad_ref[...] = (keep_ref[...] + got_ref[...].astype(F32)).T.astype(BF16)
    deep = TILE // N_Z4
    for k in range(N_Z4):
        total = got_weight_ref[k].astype(F32) + got_weight_ref[N_Z4 + k].astype(F32)
        grad_weight_ref[k * deep : (k + 1) * deep, :TILE] = total[:deep]
        grad_weight_ref[k * deep : (k + 1) * deep, TILE:] = total[deep:]


def swap(value, axis):
    return lax.ppermute(value, axis, [(0, 1), (1, 0)])


def exchange(value, axis):
    return lax.all_to_all(value, axis, 0, 0, tiled=True)


def local(
    features, weight, upstream, tile_rows, tile_cols, tile_count, edge_rows, edge_cols, edge_weight
):
    width = features.shape[2]
    hidden = weight.shape[1]
    slots, edges = edge_rows.shape[2:]
    column_tiles = PLANE * N_ZH
    most = slots + (LISTS - 1) * slots // 2 + 2 * GROUP
    tile_room = [pltpu.VMEM((most, TILE, TILE), BF16), pltpu.SemaphoreType.DMA((most // GROUP,))]
    zh = lax.axis_index("zh")
    where = jnp.stack([lax.axis_index("y"), lax.axis_index("core")]).astype(I32)

    own = features[0]
    other = swap(own, "zh")

    send = call(
        pack_body,
        shape((LISTS, 5 * slots, TILE), BF16),
        [hbm] * 5 + [smem],
        scratch=[
            pltpu.VMEM((slots, edges), I32),
            pltpu.VMEM((slots, edges), I32),
            pltpu.VMEM((slots, edges), BF16),
            pltpu.VMEM((1, slots), I32),
            pltpu.VMEM((1, slots), I32),
            pltpu.SemaphoreType.DMA((5,)),
        ],
        limit=PACK,
    )(edge_rows[0, 0], edge_cols[0, 0], edge_weight[0, 0], tile_rows[0], tile_cols[0], tile_count)
    lists = exchange(send, ("y", "core"))
    other, lists = lax.optimization_barrier((other, lists))
    tiles, zl_list, src_list, total = call(
        build_body,
        (
            shape((most, TILE, TILE), BF16),
            shape((most,), I32),
            shape((most,), I32),
            shape((N_CORE,), I32),
        ),
        [smem, vmem],
        (hbm, smem, smem, smem),
        [pltpu.SMEM((most,), I32)]
        + [pltpu.VMEM((LISTS * slots + 8, edges), F32)] * 3
        + [
            pltpu.VMEM((LISTS * 8, TILE), I32),
            pltpu.SMEM((LISTS * 8, TILE), I32),
            pltpu.SemaphoreType.DMA,
            pltpu.VMEM((2, GROUP, TILE, TILE), BF16),
            pltpu.SemaphoreType.DMA((2,)),
        ],
        flops=slots * TILE * TILE * edges * 4,
        moved=slots * TILE * TILE * 2,
        limit=LARGE,
    )(where, lists)

    zh_here = zh.astype(I32)[None]
    pair = call(pair_body, shape((PLANE, N_ZH, TILE, width), BF16), [smem, vmem, vmem])(
        zh_here, own, other
    )
    pair, up = lax.optimization_barrier((pair, upstream[0]))
    mine = exchange(pair, ("x", "y")).reshape(column_tiles, TILE, width)
    mine, total, other_up = lax.optimization_barrier((mine, total, swap(up, "z2")))
    theirs = swap(mine, "core")

    partial = call(
        forward_body,
        shape((N_ZL, TILE, width), BF16),
        [smem] * 3 + [hbm, vmem, vmem],
        scratch=[pltpu.VMEM((N_ZL, TILE, width), F32)] + tile_room,
        limit=LARGE,
    )(total, zl_list, src_list, tiles, mine, theirs)

    got = exchange(partial, "z4").reshape((N_Z4, N_Z2, TILE, width))
    partial = jnp.sum(got.astype(F32), axis=0).astype(BF16)

    node_total = features.shape[1] * N_X * N_ZH * N_Y * N_ZL * N_CORE
    out_act, send = call(
        functools.partial(dense_body, scale=1.0 / math.sqrt(node_total)),
        (shape((TILE, hidden), BF16), shape((N_Z4, N_Z2 * TILE + W_ROWS, TILE), BF16)),
        [smem] + [vmem] * 5,
    )(
        lax.axis_index("z2").astype(I32)[None],
        partial,
        swap(partial, "z2"),
        weight,
        up,
        other_up,
    )

    got = exchange(send, "z4")
    send, keep, keep_weight = call(
        backward_body,
        (
            shape((column_tiles + 1, width, TILE), BF16),
            shape((column_tiles, width, TILE), F32),
            shape((W_ROWS, TILE), F32),
        ),
        [smem] * 3 + [hbm, vmem],
        scratch=[pltpu.VMEM((N_CORE, column_tiles, width, TILE), F32)] + tile_room,
        limit=LARGE,
    )(total, zl_list, src_list, tiles, got)

    send = call(merge_body, shape((PLANE, N_ZH * TILE + W_ROWS, TILE), BF16), [vmem] * 3)(
        swap(send, "core"), keep, keep_weight
    )
    got = exchange(send, ("x", "y"))
    send, keep, send_weight = call(
        halfway_body,
        (
            shape((TILE, TILE), BF16),
            shape((TILE, TILE), F32),
            shape((N_ZH * N_Z4, W_ROWS, TILE), BF16),
        ),
        [smem, vmem],
    )(zh_here, got)
    got = swap(send, "zh")
    got_weight = exchange(send_weight, ("zh", "z4"))
    grad_features, grad_weight = call(
        finish_body,
        (shape((TILE, width), BF16), shape((width, hidden), F32)),
        [vmem] * 3,
    )(got, keep, got_weight)
    return (out_act[None], grad_features[None], grad_weight)


def solution(mesh):
    fine = Mesh(mesh.devices.reshape([size for _, size in FINE]), [name for name, _ in FINE])
    in_specs = (
        P(COL, ROW, None),
        P(),
        P(COL, ROW, None),
        P(ROW, COL, None),
        P(ROW, COL, None),
        P(ROW, COL),
        P(ROW, COL, None, None),
        P(ROW, COL, None, None),
        P(ROW, COL, None, None),
    )
    out_specs = (P(COL, ROW, None), P(COL, ROW, None), P())
    return jax.shard_map(local, mesh=fine, in_specs=in_specs, out_specs=out_specs, check_vma=False)
```

```python
import functools
import math

import jax
import jax.numpy as jnp
from jax import lax
from jax.experimental import pallas as pl
from jax.experimental.pallas import tpu as pltpu
from jax.sharding import Mesh
from jax.sharding import PartitionSpec as P

TILE = 128
GROUP = 16
BLOCK = 8
SRC_AT, ZL_AT, FLAG_AT = 10, 15, 18
FINE = (("x", 4), ("zh", 2), ("y", 4), ("z2", 2), ("z4", 4), ("core", 2))
N_X, N_ZH, N_Y, N_Z2, N_Z4, N_CORE = (size for _, size in FINE)
N_ZL = N_Z2 * N_Z4
ROW = ("x", "zh")
COL = ("y", "z2", "z4", "core")
LISTS = N_Y * N_CORE
PLANE = N_X * N_Y
PACK = 62
LARGE = 50
W_ROWS = 64
BF16 = jnp.bfloat16
F32 = jnp.float32
I32 = jnp.int32

vmem = pl.BlockSpec(memory_space=pltpu.VMEM)
smem = pl.BlockSpec(memory_space=pltpu.SMEM)
hbm = pl.BlockSpec(memory_space=pltpu.HBM)
shape = jax.ShapeDtypeStruct


def call(body, outs, in_specs, out_specs=None, scratch=(), flops=0, moved=0, limit=24):
    return pl.pallas_call(
        body,
        out_shape=outs,
        in_specs=in_specs,
        out_specs=jax.tree.map(lambda _: vmem, outs) if out_specs is None else out_specs,
        scratch_shapes=list(scratch),
        compiler_params=pltpu.CompilerParams(vmem_limit_bytes=limit * 1024 * 1024),
        cost_estimate=pl.CostEstimate(flops=flops, bytes_accessed=moved, transcendentals=0),
    )


def halves(value):
    high = value.astype(BF16)
    return high, (value - high.astype(F32)).astype(BF16)


def pair_body(zh_ref, own_ref, other_ref, send_ref):
    mine = zh_ref[0] == 0
    own, other = own_ref[...], other_ref[...]
    first, second = jnp.where(mine, own, other), jnp.where(mine, other, own)
    for peer in range(PLANE):
        send_ref[peer, 0] = first
        send_ref[peer, 1] = second


def pack_body(
    rows_hbm, cols_hbm, weight_hbm, row_hbm, col_hbm, count_ref, send_ref,
    rows_ref, cols_ref, weight_ref, row_ref, col_ref, sems,
):
    copies = [
        pltpu.make_async_copy(source, target, sems.at[k])
        for k, (source, target) in enumerate(
            (
                (rows_hbm, rows_ref),
                (cols_hbm, cols_ref),
                (weight_hbm, weight_ref),
                (row_hbm, row_ref),
                (col_hbm, col_ref),
            )
        )
    ]
    for copy in copies:
        copy.start()
    for copy in copies:
        copy.wait()
    slots, edges = rows_ref.shape
    rows = rows_ref[...].astype(F32)
    cols = cols_ref[...].astype(F32)
    weight = weight_ref[...].astype(F32)
    line = lax.broadcasted_iota(I32, (slots, slots), 0)
    meta = jnp.where(line == 0, row_ref[...], jnp.where(line == 1, col_ref[...], count_ref[0, 0]))
    blocks = (
        rows[:, :TILE],
        cols[:, :TILE],
        weight[:, :TILE],
        jnp.concatenate([rows[:, TILE:], cols[:, TILE:]], axis=1),
        jnp.concatenate([weight[:, TILE:], meta.astype(F32)], axis=1),
    )
    for k, block in enumerate(blocks):
        block = block.astype(BF16)
        for peer in range(send_ref.shape[0]):
            send_ref[peer, k * slots : (k + 1) * slots, :] = block


def field(code, at, until):
    return (code >> at) & ((1 << (until - at)) - 1)


def fetch(tiles_hbm, tiles_ref, sems, group):
    here = pl.ds(group * GROUP, GROUP)
    return pltpu.make_async_copy(tiles_hbm.at[here], tiles_ref.at[here], sems.at[group])


def part_groups(total_ref, part):
    first = 0 if part == 0 else total_ref[0] // GROUP
    return first, total_ref[part] // GROUP


def fetch_part(total_ref, part, tiles_hbm, tiles_ref, sems):
    def start(group, carry):
        fetch(tiles_hbm, tiles_ref, sems, group).start()
        return carry

    lax.fori_loop(*part_groups(total_ref, part), start, 0)


def build_body(
    where_ref, got_ref, tiles_hbm, code_ref, total_ref,
    edge_rows_ref, edge_cols_ref, weight_ref, meta_ref, slots_ref, sem, stage_ref, sems,
):
    y, core = where_ref[0], where_ref[1]
    slots = got_ref.shape[1] // 5
    edges = edge_rows_ref.shape[1]
    rest = edges - TILE
    dummy = LISTS * slots
    lane = lax.broadcasted_iota(I32, (1, TILE), 1) - rest
    for index in range(LISTS):
        meta = got_ref[index, 4 * slots : 4 * slots + 16, :].astype(F32).astype(I32)
        row, col, count = meta[0:1], meta[1:2], meta[2:3]
        near = row >> 1
        place = (near & (N_Z4 - 1)) * N_Z2 + (near >> 2 & 1)
        source = ((col >> 1) * N_Y + index // N_CORE) * N_ZH + (col & 1)
        mine = (near >> 3 == y) & (row & 1 == core) & (lane < count)
        code = (index * slots + lane) + (source << SRC_AT) + (place << ZL_AT)
        meta_ref[index * 8 : index * 8 + 1, :] = code + jnp.where(mine, 1 << FLAG_AT, 0)
        meta_ref[index * 8 + 1 : index * 8 + 2, :] = count
    copy = pltpu.make_async_copy(meta_ref, slots_ref, sem)
    copy.start()
    for index in range(LISTS):
        here = slice(index * slots, (index + 1) * slots)
        block = [got_ref[index, k * slots : (k + 1) * slots, :].astype(F32) for k in range(5)]
        edge_rows_ref[here, :TILE] = block[0]
        edge_cols_ref[here, :TILE] = block[1]
        weight_ref[here, :TILE] = block[2]
        edge_rows_ref[here, TILE:] = block[3][:, :rest]
        edge_cols_ref[here, TILE:] = block[3][:, rest:]
        weight_ref[here, TILE:] = block[4][:, :rest]
    for ref in (edge_rows_ref, edge_cols_ref, weight_ref):
        ref[dummy:, :] = jnp.zeros_like(ref[dummy:, :])
    copy.wait()

    used = jnp.int32(0)
    for part in range(N_CORE):
        column_core = core if part == 0 else 1 - core
        for column_y in range(N_Y):
            index = column_y * N_CORE + column_core

            count = slots_ref[index * 8 + 1, rest]

            def scan(block, used, index=index):
                for i in range(BLOCK):
                    code = slots_ref[index * 8, rest + block * BLOCK + i]
                    code_ref[used] = code
                    used = used + (code >> FLAG_AT)
                return used

            used = lax.fori_loop(0, (count + BLOCK - 1) // BLOCK, scan, used)
        for extra in range(GROUP - 1):
            code_ref[used + extra] = dummy
        used = (used + GROUP - 1) // GROUP * GROUP
        total_ref[part] = used

    positions = lax.broadcasted_iota(I32, (TILE, edges), 0).astype(F32)

    def store(group):
        place = group % 2
        here = pl.ds(group * GROUP, GROUP)
        return pltpu.make_async_copy(stage_ref.at[place], tiles_hbm.at[here], sems.at[place])

    def step(group, carry):
        @pl.when(group >= 2)
        def _():
            store(group - 2).wait()

        for i in range(GROUP):
            entry = group * GROUP + i
            slot = field(code_ref[entry], 0, SRC_AT)
            row_hot = jnp.where(positions == edge_rows_ref[pl.ds(slot, 1), :], 1.0, 0.0)
            col_hot = jnp.where(
                positions == edge_cols_ref[pl.ds(slot, 1), :], weight_ref[pl.ds(slot, 1), :], 0.0
            )
            built = lax.dot_general(
                row_hot.astype(BF16),
                col_hot.astype(BF16),
                (((1,), (1,)), ((), ())),
                preferred_element_type=F32,
            )
            stage_ref[group % 2, i] = built.astype(BF16)
        store(group).start()
        return carry

    groups = used // GROUP
    lax.fori_loop(0, groups, step, 0)
    for back in (2, 1):

        @pl.when(groups >= back)
        def _(back=back):
            store(groups - back).wait()


def forward_body(part, total_ref, code_ref, tiles_hbm, feats_ref, *refs):
    *start_refs, out_ref, acc_ref, tiles_ref, sems = refs
    fetch_part(total_ref, part, tiles_hbm, tiles_ref, sems)
    acc_ref[...] = start_refs[0][...] if start_refs else jnp.zeros_like(acc_ref)

    def step(group, carry):
        fetch(tiles_hbm, tiles_ref, sems, group).wait()
        products = []
        for i in range(GROUP):
            entry = group * GROUP + i
            source = field(code_ref[entry], SRC_AT, ZL_AT)
            products.append(
                jnp.dot(tiles_ref[entry], feats_ref[source], preferred_element_type=F32)
            )
        for i in range(GROUP):
            acc_ref[field(code_ref[group * GROUP + i], ZL_AT, FLAG_AT)] += products[i]
        return carry

    lax.fori_loop(*part_groups(total_ref, part), step, 0)
    out_ref[...] = acc_ref[...].astype(out_ref.dtype)


def dense_body(
    z2_ref, own_ref, other_ref, weight_ref, up_ref, other_up_ref, act_ref, send_ref, *, scale
):
    first = z2_ref[0] == 0
    total = own_ref[...].astype(F32) + other_ref[...].astype(F32)
    aggregated = total.reshape(N_Z2 * TILE, TILE).astype(BF16)
    weight = weight_ref[...]
    own_up, other_up = up_ref[...], other_up_ref[...]
    up = jnp.concatenate(
        [jnp.where(first, own_up, other_up), jnp.where(first, other_up, own_up)], axis=0
    )
    pre_act = jnp.dot(aggregated, weight, preferred_element_type=F32)
    gate = jax.nn.sigmoid(pre_act)
    act = (pre_act * gate).astype(BF16)
    act_ref[...] = jnp.where(first, act[:TILE], act[TILE:])
    grad_pre = (up.astype(F32) * gate * (1.0 + pre_act * (1.0 - gate))).astype(BF16)
    local_weight = (
        lax.dot_general(aggregated, grad_pre, (((0,), (0,)), ((), ())), preferred_element_type=F32)
        * scale
    ).astype(BF16)
    deep = TILE // N_Z4
    for z2 in range(N_Z2):
        grad_agg = lax.dot_general(
            weight,
            grad_pre[z2 * TILE : (z2 + 1) * TILE],
            (((1,), (1,)), ((), ())),
            preferred_element_type=F32,
        ).astype(BF16)
        for peer in range(N_Z4):
            send_ref[peer, z2 * TILE : (z2 + 1) * TILE, :] = grad_agg
    for peer in range(N_Z4):
        here = slice(peer * deep, (peer + 1) * deep)
        send_ref[peer, N_Z2 * TILE : N_Z2 * TILE + deep, :] = local_weight[here, :TILE]
        send_ref[peer, N_Z2 * TILE + deep :, :] = local_weight[here, TILE:]


def backward_tiles(part, total_ref, code_ref, tiles_hbm, got_ref, acc_ref, tiles_ref, sems):
    fetch_part(total_ref, part, tiles_hbm, tiles_ref, sems)
    acc_ref[...] = jnp.zeros_like(acc_ref)

    def step(group, carry):
        fetch(tiles_hbm, tiles_ref, sems, group).wait()
        products = []
        for i in range(GROUP):
            entry = group * GROUP + i
            place = field(code_ref[entry], ZL_AT, FLAG_AT)
            start = pl.multiple_of(place % N_Z2 * TILE, TILE)
            grad = got_ref[place // N_Z2, pl.ds(start, TILE), :]
            products.append(jnp.dot(grad, tiles_ref[entry], preferred_element_type=F32))
        for i in range(GROUP):
            acc_ref[field(code_ref[group * GROUP + i], SRC_AT, ZL_AT)] += products[i]
        return carry

    lax.fori_loop(*part_groups(total_ref, part), step, 0)


def weight_terms(got_ref):
    return halves(jnp.sum(got_ref[:, N_Z2 * TILE :, :].astype(F32), axis=0))


def backward_other_body(
    total_ref, code_ref, tiles_hbm, got_ref, send_ref, acc_ref, tiles_ref, sems
):
    backward_tiles(1, total_ref, code_ref, tiles_hbm, got_ref, acc_ref, tiles_ref, sems)
    tiles = acc_ref.shape[0]
    send_ref[0:tiles] = acc_ref[...].astype(BF16)
    high, low = weight_terms(got_ref)
    send_ref[tiles, 0:W_ROWS, :] = high
    send_ref[tiles, W_ROWS:, :] = low


def backward_own_body(
    total_ref, code_ref, tiles_hbm, got_ref, keep_ref, keep_weight_ref, tiles_ref, sems
):
    backward_tiles(0, total_ref, code_ref, tiles_hbm, got_ref, keep_ref, tiles_ref, sems)
    high, low = weight_terms(got_ref)
    keep_weight_ref[...] = high.astype(F32) + low.astype(F32)


def merge_body(got_ref, keep_ref, keep_weight_ref, send_ref):
    tiles = keep_ref.shape[0]
    terms = got_ref[tiles, 0 : 2 * W_ROWS, :].astype(F32)
    part = (keep_weight_ref[...] + (terms[:W_ROWS] + terms[W_ROWS:])).astype(BF16)
    for peer in range(PLANE):
        for zh in range(N_ZH):
            tile = peer * N_ZH + zh
            send_ref[peer, zh * TILE : (zh + 1) * TILE, :] = (
                keep_ref[tile] + got_ref[tile].astype(F32)
            ).astype(BF16)
        send_ref[peer, N_ZH * TILE :, :] = part


def halfway_body(zh_ref, got_ref, send_ref, keep_ref, send_weight_ref):
    zh = zh_ref[0]
    total = jnp.sum(got_ref[...].astype(F32), axis=0)
    first, second = total[:TILE], total[TILE : N_ZH * TILE]
    mine = zh == 0
    keep_ref[...] = jnp.where(mine, first, second)
    send_ref[...] = jnp.where(mine, second, first).astype(BF16)
    weight_sum = total[N_ZH * TILE :].astype(BF16)
    for peer in range(N_ZH * N_Z4):
        send_weight_ref[peer] = weight_sum


def finish_body(got_ref, keep_ref, got_weight_ref, grad_ref, grad_weight_ref):
    grad_ref[...] = (keep_ref[...] + got_ref[...].astype(F32)).T.astype(BF16)
    deep = TILE // N_Z4
    for k in range(N_Z4):
        total = got_weight_ref[k].astype(F32) + got_weight_ref[N_Z4 + k].astype(F32)
        grad_weight_ref[k * deep : (k + 1) * deep, :TILE] = total[:deep]
        grad_weight_ref[k * deep : (k + 1) * deep, TILE:] = total[deep:]


def swap(value, axis):
    return lax.ppermute(value, axis, [(0, 1), (1, 0)])


def exchange(value, axis):
    return lax.all_to_all(value, axis, 0, 0, tiled=True)


def local(
    features, weight, upstream, tile_rows, tile_cols, tile_count, edge_rows, edge_cols, edge_weight
):
    width = features.shape[2]
    hidden = weight.shape[1]
    slots, edges = edge_rows.shape[2:]
    column_tiles = PLANE * N_ZH
    most = slots + (LISTS - 1) * slots // 2 + 2 * GROUP
    tile_room = [pltpu.VMEM((most, TILE, TILE), BF16), pltpu.SemaphoreType.DMA((most // GROUP,))]
    zh = lax.axis_index("zh")
    where = jnp.stack([lax.axis_index("y"), lax.axis_index("core")]).astype(I32)

    own = features[0]
    other = swap(own, "zh")

    send = call(
        pack_body,
        shape((LISTS, 5 * slots, TILE), BF16),
        [hbm] * 5 + [smem],
        scratch=[
            pltpu.VMEM((slots, edges), I32),
            pltpu.VMEM((slots, edges), I32),
            pltpu.VMEM((slots, edges), BF16),
            pltpu.VMEM((1, slots), I32),
            pltpu.VMEM((1, slots), I32),
            pltpu.SemaphoreType.DMA((5,)),
        ],
        limit=PACK,
    )(edge_rows[0, 0], edge_cols[0, 0], edge_weight[0, 0], tile_rows[0], tile_cols[0], tile_count)
    lists = exchange(send, ("y", "core"))
    other, lists = lax.optimization_barrier((other, lists))
    tiles, codes, total = call(
        build_body,
        (shape((most, TILE, TILE), BF16), shape((most,), I32), shape((N_CORE,), I32)),
        [smem, vmem],
        (hbm, smem, smem),
        [pltpu.VMEM((LISTS * slots + 8, edges), F32)] * 3
        + [
            pltpu.VMEM((LISTS * 8, TILE), I32),
            pltpu.SMEM((LISTS * 8, TILE), I32),
            pltpu.SemaphoreType.DMA,
            pltpu.VMEM((2, GROUP, TILE, TILE), BF16),
            pltpu.SemaphoreType.DMA((2,)),
        ],
        flops=slots * TILE * TILE * edges * 4,
        moved=slots * TILE * TILE * 2,
        limit=LARGE,
    )(where, lists)

    zh_here = zh.astype(I32)[None]
    pair = call(pair_body, shape((PLANE, N_ZH, TILE, width), BF16), [smem, vmem, vmem])(
        zh_here, own, other
    )
    pair, up = lax.optimization_barrier((pair, upstream[0]))
    mine = exchange(pair, ("x", "y")).reshape(column_tiles, TILE, width)
    mine, total, other_up = lax.optimization_barrier((mine, total, swap(up, "z2")))
    theirs = swap(mine, "core")

    work = dict(flops=slots * TILE * TILE * width, moved=slots * TILE * TILE, limit=LARGE)
    sums = (N_ZL, TILE, width)
    partial = call(
        functools.partial(forward_body, 0),
        shape(sums, F32),
        [smem] * 2 + [hbm, vmem],
        scratch=[pltpu.VMEM(sums, F32)] + tile_room,
        **work,
    )(total, codes, tiles, mine)
    partial = call(
        functools.partial(forward_body, 1),
        shape(sums, BF16),
        [smem] * 2 + [hbm, vmem, vmem],
        scratch=[pltpu.VMEM(sums, F32)] + tile_room,
        **work,
    )(total, codes, tiles, theirs, partial)

    got = exchange(partial, "z4").reshape((N_Z4, N_Z2, TILE, width))
    partial = jnp.sum(got.astype(F32), axis=0).astype(BF16)

    node_total = features.shape[1] * N_X * N_ZH * N_Y * N_ZL * N_CORE
    out_act, send = call(
        functools.partial(dense_body, scale=1.0 / math.sqrt(node_total)),
        (shape((TILE, hidden), BF16), shape((N_Z4, N_Z2 * TILE + W_ROWS, TILE), BF16)),
        [smem] + [vmem] * 5,
    )(
        lax.axis_index("z2").astype(I32)[None],
        partial,
        swap(partial, "z2"),
        weight,
        up,
        other_up,
    )

    got = exchange(send, "z4")
    sums = (column_tiles, width, TILE)
    send = call(
        backward_other_body,
        shape((column_tiles + 1, width, TILE), BF16),
        [smem] * 2 + [hbm, vmem],
        scratch=[pltpu.VMEM(sums, F32)] + tile_room,
        **work,
    )(total, codes, tiles, got)
    keep, keep_weight = call(
        backward_own_body,
        (shape(sums, F32), shape((W_ROWS, TILE), F32)),
        [smem] * 2 + [hbm, vmem],
        scratch=tile_room,
        **work,
    )(total, codes, tiles, got)

    send = call(merge_body, shape((PLANE, N_ZH * TILE + W_ROWS, TILE), BF16), [vmem] * 3)(
        swap(send, "core"), keep, keep_weight
    )
    got = exchange(send, ("x", "y"))
    send, keep, send_weight = call(
        halfway_body,
        (
            shape((TILE, TILE), BF16),
            shape((TILE, TILE), F32),
            shape((N_ZH * N_Z4, W_ROWS, TILE), BF16),
        ),
        [smem, vmem],
    )(zh_here, got)
    got = swap(send, "zh")
    got_weight = exchange(send_weight, ("zh", "z4"))
    grad_features, grad_weight = call(
        finish_body,
        (shape((TILE, width), BF16), shape((width, hidden), F32)),
        [vmem] * 3,
    )(got, keep, got_weight)
    return (out_act[None], grad_features[None], grad_weight)


def solution(mesh):
    fine = Mesh(mesh.devices.reshape([size for _, size in FINE]), [name for name, _ in FINE])
    in_specs = (
        P(COL, ROW, None),
        P(),
        P(COL, ROW, None),
        P(ROW, COL, None),
        P(ROW, COL, None),
        P(ROW, COL),
        P(ROW, COL, None, None),
        P(ROW, COL, None, None),
        P(ROW, COL, None, None),
    )
    out_specs = (P(COL, ROW, None), P(COL, ROW, None), P())
    return jax.shard_map(local, mesh=fine, in_specs=in_specs, out_specs=out_specs, check_vma=False)
```

```python
import functools
import math

import jax
import jax.numpy as jnp
from jax import lax
from jax.experimental import pallas as pl
from jax.experimental.pallas import tpu as pltpu
from jax.sharding import Mesh
from jax.sharding import PartitionSpec as P

TILE = 128
GROUP = 16
BLOCK = 8
SRC_AT, ZL_AT, FLAG_AT = 10, 15, 18
FINE = (("x", 4), ("zh", 2), ("y", 4), ("z2", 2), ("z4", 4), ("core", 2))
N_X, N_ZH, N_Y, N_Z2, N_Z4, N_CORE = (size for _, size in FINE)
N_ZL = N_Z2 * N_Z4
ROW = ("x", "zh")
COL = ("y", "z2", "z4", "core")
LISTS = N_Y * N_CORE
PLANE = N_X * N_Y
PACK = 62
LARGE = 50
W_ROWS = 64
W_HALF = W_ROWS // N_CORE
BF16 = jnp.bfloat16
F32 = jnp.float32
I32 = jnp.int32

vmem = pl.BlockSpec(memory_space=pltpu.VMEM)
smem = pl.BlockSpec(memory_space=pltpu.SMEM)
hbm = pl.BlockSpec(memory_space=pltpu.HBM)
shape = jax.ShapeDtypeStruct


def call(body, outs, in_specs, out_specs=None, scratch=(), flops=0, moved=0, limit=24):
    return pl.pallas_call(
        body,
        out_shape=outs,
        in_specs=in_specs,
        out_specs=jax.tree.map(lambda _: vmem, outs) if out_specs is None else out_specs,
        scratch_shapes=list(scratch),
        compiler_params=pltpu.CompilerParams(vmem_limit_bytes=limit * 1024 * 1024),
        cost_estimate=pl.CostEstimate(flops=flops, bytes_accessed=moved, transcendentals=0),
    )


def halves(value):
    high = value.astype(BF16)
    return high, (value - high.astype(F32)).astype(BF16)


def pair_body(zh_ref, own_ref, other_ref, send_ref):
    mine = zh_ref[0] == 0
    own, other = own_ref[...], other_ref[...]
    first, second = jnp.where(mine, own, other), jnp.where(mine, other, own)
    for peer in range(PLANE):
        send_ref[peer, 0] = first
        send_ref[peer, 1] = second


def pack_body(
    rows_hbm, cols_hbm, weight_hbm, row_hbm, col_hbm, count_ref, send_ref,
    rows_ref, cols_ref, weight_ref, row_ref, col_ref, sems,
):
    copies = [
        pltpu.make_async_copy(source, target, sems.at[k])
        for k, (source, target) in enumerate(
            (
                (rows_hbm, rows_ref),
                (cols_hbm, cols_ref),
                (weight_hbm, weight_ref),
                (row_hbm, row_ref),
                (col_hbm, col_ref),
            )
        )
    ]
    for copy in copies:
        copy.start()
    for copy in copies:
        copy.wait()
    slots, edges = rows_ref.shape
    rows = rows_ref[...].astype(F32)
    cols = cols_ref[...].astype(F32)
    weight = weight_ref[...].astype(F32)
    line = lax.broadcasted_iota(I32, (slots, slots), 0)
    meta = jnp.where(line == 0, row_ref[...], jnp.where(line == 1, col_ref[...], count_ref[0, 0]))
    blocks = (
        rows[:, :TILE],
        cols[:, :TILE],
        weight[:, :TILE],
        jnp.concatenate([rows[:, TILE:], cols[:, TILE:]], axis=1),
        jnp.concatenate([weight[:, TILE:], meta.astype(F32)], axis=1),
    )
    for k, block in enumerate(blocks):
        block = block.astype(BF16)
        for peer in range(send_ref.shape[0]):
            send_ref[peer, k * slots : (k + 1) * slots, :] = block


def field(code, at, until):
    return (code >> at) & ((1 << (until - at)) - 1)


def fetch(tiles_hbm, tiles_ref, sems, group):
    here = pl.ds(group * GROUP, GROUP)
    return pltpu.make_async_copy(tiles_hbm.at[here], tiles_ref.at[here], sems.at[group])


def part_groups(total_ref, part):
    first = 0 if part == 0 else total_ref[0] // GROUP
    return first, total_ref[part] // GROUP


def fetch_part(total_ref, part, tiles_hbm, tiles_ref, sems):
    def start(group, carry):
        fetch(tiles_hbm, tiles_ref, sems, group).start()
        return carry

    lax.fori_loop(*part_groups(total_ref, part), start, 0)


def build_body(
    where_ref, got_ref, tiles_hbm, code_ref, total_ref,
    edge_rows_ref, edge_cols_ref, weight_ref, meta_ref, slots_ref, sem, stage_ref, sems,
):
    y, core = where_ref[0], where_ref[1]
    slots = got_ref.shape[1] // 5
    edges = edge_rows_ref.shape[1]
    rest = edges - TILE
    dummy = LISTS * slots
    lane = lax.broadcasted_iota(I32, (1, TILE), 1) - rest
    for index in range(LISTS):
        meta = got_ref[index, 4 * slots : 4 * slots + 16, :].astype(F32).astype(I32)
        row, col, count = meta[0:1], meta[1:2], meta[2:3]
        near = row >> 1
        place = (near & (N_Z4 - 1)) * N_Z2 + (near >> 2 & 1)
        source = ((col >> 1) * N_Y + index // N_CORE) * N_ZH + (col & 1)
        mine = (near >> 3 == y) & (row & 1 == core) & (lane < count)
        code = (index * slots + lane) + (source << SRC_AT) + (place << ZL_AT)
        meta_ref[index * 8 : index * 8 + 1, :] = code + jnp.where(mine, 1 << FLAG_AT, 0)
        meta_ref[index * 8 + 1 : index * 8 + 2, :] = count
    copy = pltpu.make_async_copy(meta_ref, slots_ref, sem)
    copy.start()
    for index in range(LISTS):
        here = slice(index * slots, (index + 1) * slots)
        block = [got_ref[index, k * slots : (k + 1) * slots, :].astype(F32) for k in range(5)]
        edge_rows_ref[here, :TILE] = block[0]
        edge_cols_ref[here, :TILE] = block[1]
        weight_ref[here, :TILE] = block[2]
        edge_rows_ref[here, TILE:] = block[3][:, :rest]
        edge_cols_ref[here, TILE:] = block[3][:, rest:]
        weight_ref[here, TILE:] = block[4][:, :rest]
    for ref in (edge_rows_ref, edge_cols_ref, weight_ref):
        ref[dummy:, :] = jnp.zeros_like(ref[dummy:, :])
    copy.wait()

    used = jnp.int32(0)
    for part in range(N_CORE):
        column_core = core if part == 0 else 1 - core
        for column_y in range(N_Y):
            index = column_y * N_CORE + column_core

            count = slots_ref[index * 8 + 1, rest]

            def scan(block, used, index=index):
                for i in range(BLOCK):
                    code = slots_ref[index * 8, rest + block * BLOCK + i]
                    code_ref[used] = code
                    used = used + (code >> FLAG_AT)
                return used

            used = lax.fori_loop(0, (count + BLOCK - 1) // BLOCK, scan, used)
        for extra in range(GROUP - 1):
            code_ref[used + extra] = dummy
        used = (used + GROUP - 1) // GROUP * GROUP
        total_ref[part] = used

    positions = lax.broadcasted_iota(I32, (TILE, edges), 0).astype(F32)

    def store(group):
        place = group % 2
        here = pl.ds(group * GROUP, GROUP)
        return pltpu.make_async_copy(stage_ref.at[place], tiles_hbm.at[here], sems.at[place])

    def step(group, carry):
        @pl.when(group >= 2)
        def _():
            store(group - 2).wait()

        for i in range(GROUP):
            entry = group * GROUP + i
            slot = field(code_ref[entry], 0, SRC_AT)
            row_hot = jnp.where(positions == edge_rows_ref[pl.ds(slot, 1), :], 1.0, 0.0)
            col_hot = jnp.where(
                positions == edge_cols_ref[pl.ds(slot, 1), :], weight_ref[pl.ds(slot, 1), :], 0.0
            )
            built = lax.dot_general(
                row_hot.astype(BF16),
                col_hot.astype(BF16),
                (((1,), (1,)), ((), ())),
                preferred_element_type=F32,
            )
            stage_ref[group % 2, i] = built.astype(BF16)
        store(group).start()
        return carry

    groups = used // GROUP
    lax.fori_loop(0, groups, step, 0)
    for back in (2, 1):

        @pl.when(groups >= back)
        def _(back=back):
            store(groups - back).wait()


def forward_body(part, total_ref, code_ref, tiles_hbm, feats_ref, *refs):
    *start_refs, out_ref, acc_ref, tiles_ref, sems = refs
    fetch_part(total_ref, part, tiles_hbm, tiles_ref, sems)
    acc_ref[...] = start_refs[0][...] if start_refs else jnp.zeros_like(acc_ref)

    def step(group, carry):
        fetch(tiles_hbm, tiles_ref, sems, group).wait()
        products = []
        for i in range(GROUP):
            entry = group * GROUP + i
            source = field(code_ref[entry], SRC_AT, ZL_AT)
            products.append(
                jnp.dot(tiles_ref[entry], feats_ref[source], preferred_element_type=F32)
            )
        for i in range(GROUP):
            acc_ref[field(code_ref[group * GROUP + i], ZL_AT, FLAG_AT)] += products[i]
        return carry

    lax.fori_loop(*part_groups(total_ref, part), step, 0)
    out_ref[...] = acc_ref[...].astype(out_ref.dtype)


def dense_body(
    z2_ref, own_ref, other_ref, weight_ref, up_ref, other_up_ref, act_ref, send_ref, *, scale
):
    first = z2_ref[0] == 0
    total = own_ref[...].astype(F32) + other_ref[...].astype(F32)
    aggregated = total.reshape(N_Z2 * TILE, TILE).astype(BF16)
    weight = weight_ref[...]
    own_up, other_up = up_ref[...], other_up_ref[...]
    up = jnp.concatenate(
        [jnp.where(first, own_up, other_up), jnp.where(first, other_up, own_up)], axis=0
    )
    pre_act = jnp.dot(aggregated, weight, preferred_element_type=F32)
    gate = jax.nn.sigmoid(pre_act)
    act = (pre_act * gate).astype(BF16)
    act_ref[...] = jnp.where(first, act[:TILE], act[TILE:])
    grad_pre = (up.astype(F32) * gate * (1.0 + pre_act * (1.0 - gate))).astype(BF16)
    local_weight = (
        lax.dot_general(aggregated, grad_pre, (((0,), (0,)), ((), ())), preferred_element_type=F32)
        * scale
    ).astype(BF16)
    deep = TILE // N_Z4
    for z2 in range(N_Z2):
        grad_agg = lax.dot_general(
            weight,
            grad_pre[z2 * TILE : (z2 + 1) * TILE],
            (((1,), (1,)), ((), ())),
            preferred_element_type=F32,
        ).astype(BF16)
        for peer in range(N_Z4):
            send_ref[peer, z2 * TILE : (z2 + 1) * TILE, :] = grad_agg
    for peer in range(N_Z4):
        here = slice(peer * deep, (peer + 1) * deep)
        send_ref[peer, N_Z2 * TILE : N_Z2 * TILE + deep, :] = local_weight[here, :TILE]
        send_ref[peer, N_Z2 * TILE + deep :, :] = local_weight[here, TILE:]


def backward_tiles(part, total_ref, code_ref, tiles_hbm, got_ref, acc_ref, tiles_ref, sems):
    fetch_part(total_ref, part, tiles_hbm, tiles_ref, sems)
    acc_ref[...] = jnp.zeros_like(acc_ref)

    def step(group, carry):
        fetch(tiles_hbm, tiles_ref, sems, group).wait()
        products = []
        for i in range(GROUP):
            entry = group * GROUP + i
            place = field(code_ref[entry], ZL_AT, FLAG_AT)
            start = pl.multiple_of(place % N_Z2 * TILE, TILE)
            grad = got_ref[place // N_Z2, pl.ds(start, TILE), :]
            products.append(jnp.dot(grad, tiles_ref[entry], preferred_element_type=F32))
        for i in range(GROUP):
            acc_ref[field(code_ref[group * GROUP + i], SRC_AT, ZL_AT)] += products[i]
        return carry

    lax.fori_loop(*part_groups(total_ref, part), step, 0)


def weight_half(got_ref, core):
    terms = jnp.sum(got_ref[:, N_Z2 * TILE :, :].astype(F32), axis=0)
    return jnp.where(core == 0, terms[:W_HALF], terms[W_HALF:])


def backward_other_body(
    core_ref, total_ref, code_ref, tiles_hbm, got_ref, send_ref, acc_ref, tiles_ref, sems
):
    backward_tiles(1, total_ref, code_ref, tiles_hbm, got_ref, acc_ref, tiles_ref, sems)
    tiles = acc_ref.shape[0]
    send_ref[0:tiles] = acc_ref[...].astype(BF16)
    high, low = halves(weight_half(got_ref, 1 - core_ref[0]))
    send_ref[tiles, 0:W_HALF, :] = high
    send_ref[tiles, W_HALF : 2 * W_HALF, :] = low
    send_ref[tiles, 2 * W_HALF :, :] = jnp.zeros_like(send_ref[tiles, 2 * W_HALF :, :])


def backward_own_body(
    core_ref, total_ref, code_ref, tiles_hbm, got_ref, keep_ref, keep_weight_ref, tiles_ref, sems
):
    backward_tiles(0, total_ref, code_ref, tiles_hbm, got_ref, keep_ref, tiles_ref, sems)
    keep_weight_ref[...] = weight_half(got_ref, core_ref[0])


def merge_body(got_ref, keep_ref, keep_weight_ref, send_ref):
    tiles = keep_ref.shape[0]
    terms = got_ref[tiles, 0 : 2 * W_HALF, :].astype(F32)
    part = (keep_weight_ref[...] + (terms[:W_HALF] + terms[W_HALF:])).astype(BF16)
    for peer in range(PLANE):
        for zh in range(N_ZH):
            tile = peer * N_ZH + zh
            send_ref[peer, zh * TILE : (zh + 1) * TILE, :] = (
                keep_ref[tile] + got_ref[tile].astype(F32)
            ).astype(BF16)
        send_ref[peer, N_ZH * TILE :, :] = part


def halfway_body(zh_ref, got_ref, send_ref, keep_ref):
    zh = zh_ref[0]
    total = jnp.sum(got_ref[...].astype(F32), axis=0)
    first, second = total[:TILE], total[TILE : N_ZH * TILE]
    mine = zh == 0
    keep_ref[...] = jnp.where(mine, first, second)
    send_ref[0:TILE, :] = jnp.where(mine, second, first).astype(BF16)
    high, low = halves(total[N_ZH * TILE :])
    send_ref[TILE : TILE + W_HALF, :] = high
    send_ref[TILE + W_HALF :, :] = low


def last_sum_body(got_ref, sent_ref, send_ref):
    terms = got_ref[TILE:, :].astype(F32), sent_ref[TILE:, :].astype(F32)
    total = (terms[0][:W_HALF] + terms[0][W_HALF:]) + (terms[1][:W_HALF] + terms[1][W_HALF:])
    for peer in range(N_Z4 * N_CORE):
        send_ref[peer] = total


def finish_body(got_ref, keep_ref, grad_ref):
    grad_ref[...] = (keep_ref[...] + got_ref[0:TILE, :].astype(F32)).T.astype(BF16)


def place_body(got_ref, grad_weight_ref):
    for z4 in range(N_Z4):
        for core in range(N_CORE):
            grad_weight_ref[
                z4 * W_HALF : (z4 + 1) * W_HALF, core * TILE : (core + 1) * TILE
            ] = got_ref[z4 * N_CORE + core]


def swap(value, axis):
    return lax.ppermute(value, axis, [(0, 1), (1, 0)])


def exchange(value, axis):
    return lax.all_to_all(value, axis, 0, 0, tiled=True)


def local(
    features, weight, upstream, tile_rows, tile_cols, tile_count, edge_rows, edge_cols, edge_weight
):
    width = features.shape[2]
    hidden = weight.shape[1]
    slots, edges = edge_rows.shape[2:]
    column_tiles = PLANE * N_ZH
    most = slots + (LISTS - 1) * slots // 2 + 2 * GROUP
    tile_room = [pltpu.VMEM((most, TILE, TILE), BF16), pltpu.SemaphoreType.DMA((most // GROUP,))]
    zh = lax.axis_index("zh")
    where = jnp.stack([lax.axis_index("y"), lax.axis_index("core")]).astype(I32)

    own = features[0]
    other = swap(own, "zh")

    send = call(
        pack_body,
        shape((LISTS, 5 * slots, TILE), BF16),
        [hbm] * 5 + [smem],
        scratch=[
            pltpu.VMEM((slots, edges), I32),
            pltpu.VMEM((slots, edges), I32),
            pltpu.VMEM((slots, edges), BF16),
            pltpu.VMEM((1, slots), I32),
            pltpu.VMEM((1, slots), I32),
            pltpu.SemaphoreType.DMA((5,)),
        ],
        limit=PACK,
    )(edge_rows[0, 0], edge_cols[0, 0], edge_weight[0, 0], tile_rows[0], tile_cols[0], tile_count)
    lists = exchange(send, ("y", "core"))
    other, lists = lax.optimization_barrier((other, lists))
    tiles, codes, total = call(
        build_body,
        (shape((most, TILE, TILE), BF16), shape((most,), I32), shape((N_CORE,), I32)),
        [smem, vmem],
        (hbm, smem, smem),
        [pltpu.VMEM((LISTS * slots + 8, edges), F32)] * 3
        + [
            pltpu.VMEM((LISTS * 8, TILE), I32),
            pltpu.SMEM((LISTS * 8, TILE), I32),
            pltpu.SemaphoreType.DMA,
            pltpu.VMEM((2, GROUP, TILE, TILE), BF16),
            pltpu.SemaphoreType.DMA((2,)),
        ],
        flops=slots * TILE * TILE * edges * 4,
        moved=slots * TILE * TILE * 2,
        limit=LARGE,
    )(where, lists)

    zh_here = zh.astype(I32)[None]
    pair = call(pair_body, shape((PLANE, N_ZH, TILE, width), BF16), [smem, vmem, vmem])(
        zh_here, own, other
    )
    pair, up = lax.optimization_barrier((pair, upstream[0]))
    mine = exchange(pair, ("x", "y")).reshape(column_tiles, TILE, width)
    mine, total, other_up = lax.optimization_barrier((mine, total, swap(up, "z2")))
    theirs = swap(mine, "core")

    work = dict(flops=slots * TILE * TILE * width, moved=slots * TILE * TILE, limit=LARGE)
    sums = (N_ZL, TILE, width)
    partial = call(
        functools.partial(forward_body, 0),
        shape(sums, F32),
        [smem] * 2 + [hbm, vmem],
        scratch=[pltpu.VMEM(sums, F32)] + tile_room,
        **work,
    )(total, codes, tiles, mine)
    partial = call(
        functools.partial(forward_body, 1),
        shape(sums, BF16),
        [smem] * 2 + [hbm, vmem, vmem],
        scratch=[pltpu.VMEM(sums, F32)] + tile_room,
        **work,
    )(total, codes, tiles, theirs, partial)

    got = exchange(partial, "z4").reshape((N_Z4, N_Z2, TILE, width))
    partial = jnp.sum(got.astype(F32), axis=0).astype(BF16)

    node_total = features.shape[1] * N_X * N_ZH * N_Y * N_ZL * N_CORE
    out_act, send = call(
        functools.partial(dense_body, scale=1.0 / math.sqrt(node_total)),
        (shape((TILE, hidden), BF16), shape((N_Z4, N_Z2 * TILE + W_ROWS, TILE), BF16)),
        [smem] + [vmem] * 5,
    )(
        lax.axis_index("z2").astype(I32)[None],
        partial,
        swap(partial, "z2"),
        weight,
        up,
        other_up,
    )

    got = exchange(send, "z4")
    sums = (column_tiles, width, TILE)
    send = call(
        backward_other_body,
        shape((column_tiles + 1, width, TILE), BF16),
        [smem] * 3 + [hbm, vmem],
        scratch=[pltpu.VMEM(sums, F32)] + tile_room,
        **work,
    )(where[1:], total, codes, tiles, got)
    keep, keep_weight = call(
        backward_own_body,
        (shape(sums, F32), shape((W_HALF, TILE), F32)),
        [smem] * 3 + [hbm, vmem],
        scratch=tile_room,
        **work,
    )(where[1:], total, codes, tiles, got)

    send = call(merge_body, shape((PLANE, N_ZH * TILE + W_HALF, TILE), BF16), [vmem] * 3)(
        swap(send, "core"), keep, keep_weight
    )
    got = exchange(send, ("x", "y"))
    send, keep = call(
        halfway_body,
        (shape((TILE + 2 * W_HALF, TILE), BF16), shape((TILE, TILE), F32)),
        [smem, vmem],
    )(zh_here, got)
    got = swap(send, "zh")
    send_weight = call(last_sum_body, shape((N_Z4 * N_CORE, W_HALF, TILE), F32), [vmem] * 2)(
        got, send
    )
    got_weight = exchange(send_weight, ("z4", "core"))
    grad_features = call(finish_body, shape((TILE, width), BF16), [vmem] * 2)(got, keep)
    grad_weight = call(place_body, shape((width, hidden), F32), [vmem])(got_weight)
    return (out_act[None], grad_features[None], grad_weight)


def solution(mesh):
    fine = Mesh(mesh.devices.reshape([size for _, size in FINE]), [name for name, _ in FINE])
    in_specs = (
        P(COL, ROW, None),
        P(),
        P(COL, ROW, None),
        P(ROW, COL, None),
        P(ROW, COL, None),
        P(ROW, COL),
        P(ROW, COL, None, None),
        P(ROW, COL, None, None),
        P(ROW, COL, None, None),
    )
    out_specs = (P(COL, ROW, None), P(COL, ROW, None), P())
    return jax.shard_map(local, mesh=fine, in_specs=in_specs, out_specs=out_specs, check_vma=False)
```

```python
import functools
import math

import jax
import jax.numpy as jnp
from jax import lax
from jax.experimental import pallas as pl
from jax.experimental.pallas import tpu as pltpu
from jax.sharding import Mesh
from jax.sharding import PartitionSpec as P

TILE = 128
GROUP = 16
BLOCK = 8
SRC_AT, ZL_AT, FLAG_AT = 10, 15, 18
EXTRA = 8
FINE = (("x", 4), ("zh", 2), ("y", 4), ("z2", 2), ("z4", 4), ("core", 2))
N_X, N_ZH, N_Y, N_Z2, N_Z4, N_CORE = (size for _, size in FINE)
N_ZL = N_Z2 * N_Z4
ROW = ("x", "zh")
COL = ("y", "z2", "z4", "core")
LISTS = N_Y * N_CORE
PLANE = N_X * N_Y
PACK = 62
LARGE = 50
W_ROWS = 64
W_HALF = W_ROWS // N_CORE
BF16 = jnp.bfloat16
F32 = jnp.float32
I32 = jnp.int32

vmem = pl.BlockSpec(memory_space=pltpu.VMEM)
smem = pl.BlockSpec(memory_space=pltpu.SMEM)
hbm = pl.BlockSpec(memory_space=pltpu.HBM)
shape = jax.ShapeDtypeStruct


def call(body, outs, in_specs, out_specs=None, scratch=(), flops=0, moved=0, limit=24):
    return pl.pallas_call(
        body,
        out_shape=outs,
        in_specs=in_specs,
        out_specs=jax.tree.map(lambda _: vmem, outs) if out_specs is None else out_specs,
        scratch_shapes=list(scratch),
        compiler_params=pltpu.CompilerParams(vmem_limit_bytes=limit * 1024 * 1024),
        cost_estimate=pl.CostEstimate(flops=flops, bytes_accessed=moved, transcendentals=0),
    )


def halves(value):
    high = value.astype(BF16)
    return high, (value - high.astype(F32)).astype(BF16)


def pair_body(zh_ref, own_ref, other_ref, send_ref):
    mine = zh_ref[0] == 0
    own, other = own_ref[...], other_ref[...]
    first, second = jnp.where(mine, own, other), jnp.where(mine, other, own)
    for peer in range(PLANE):
        send_ref[peer, 0] = first
        send_ref[peer, 1] = second


def pack_body(
    rows_hbm, cols_hbm, weight_hbm, row_hbm, col_hbm, count_ref, send_ref,
    rows_ref, cols_ref, weight_ref, row_ref, col_ref, sems,
):
    copies = [
        pltpu.make_async_copy(source, target, sems.at[k])
        for k, (source, target) in enumerate(
            (
                (rows_hbm, rows_ref),
                (cols_hbm, cols_ref),
                (weight_hbm, weight_ref),
                (row_hbm, row_ref),
                (col_hbm, col_ref),
            )
        )
    ]
    for copy in copies:
        copy.start()
    for copy in copies:
        copy.wait()
    slots, edges = rows_ref.shape
    rows = rows_ref[...].astype(F32)
    cols = cols_ref[...].astype(F32)
    weight = weight_ref[...].astype(F32)
    line = lax.broadcasted_iota(I32, (slots, slots), 0)
    meta = jnp.where(line == 0, row_ref[...], jnp.where(line == 1, col_ref[...], count_ref[0, 0]))
    blocks = (
        rows[:, :TILE],
        cols[:, :TILE],
        weight[:, :TILE],
        jnp.concatenate([rows[:, TILE:], cols[:, TILE:]], axis=1),
        jnp.concatenate([weight[:, TILE:], meta.astype(F32)], axis=1),
    )
    for k, block in enumerate(blocks):
        block = block.astype(BF16)
        for peer in range(send_ref.shape[0]):
            send_ref[peer, k * slots : (k + 1) * slots, :] = block


def field(code, at, until):
    return (code >> at) & ((1 << (until - at)) - 1)


def fetch(tiles_hbm, tiles_ref, sems, group):
    here = pl.ds(group * GROUP, GROUP)
    return pltpu.make_async_copy(tiles_hbm.at[here], tiles_ref.at[here], sems.at[group])


def part_groups(code_ref, part):
    ends = code_ref.shape[0] - EXTRA
    first = 0 if part == 0 else code_ref[ends] // GROUP
    return first, code_ref[ends + part] // GROUP


def fetch_part(code_ref, part, tiles_hbm, tiles_ref, sems):
    def start(group, carry):
        fetch(tiles_hbm, tiles_ref, sems, group).start()
        return carry

    lax.fori_loop(*part_groups(code_ref, part), start, 0)


def build_body(
    where_ref, got_ref, tiles_hbm, code_ref,
    edge_rows_ref, edge_cols_ref, weight_ref, meta_ref, slots_ref, sem, stage_ref, sems,
):
    y, core = where_ref[0], where_ref[1]
    slots = got_ref.shape[1] // 5
    edges = edge_rows_ref.shape[1]
    rest = edges - TILE
    dummy = LISTS * slots
    lane = lax.broadcasted_iota(I32, (1, TILE), 1) - rest
    for index in range(LISTS):
        meta = got_ref[index, 4 * slots : 4 * slots + 16, :].astype(F32).astype(I32)
        row, col, count = meta[0:1], meta[1:2], meta[2:3]
        near = row >> 1
        place = (near & (N_Z4 - 1)) * N_Z2 + (near >> 2 & 1)
        source = ((col >> 1) * N_Y + index // N_CORE) * N_ZH + (col & 1)
        mine = (near >> 3 == y) & (row & 1 == core) & (lane < count)
        code = (index * slots + lane) + (source << SRC_AT) + (place << ZL_AT)
        meta_ref[index * 8 : index * 8 + 1, :] = code + jnp.where(mine, 1 << FLAG_AT, 0)
        meta_ref[index * 8 + 1 : index * 8 + 2, :] = count
    copy = pltpu.make_async_copy(meta_ref, slots_ref, sem)
    copy.start()
    for index in range(LISTS):
        here = slice(index * slots, (index + 1) * slots)
        block = [got_ref[index, k * slots : (k + 1) * slots, :].astype(F32) for k in range(5)]
        edge_rows_ref[here, :TILE] = block[0]
        edge_cols_ref[here, :TILE] = block[1]
        weight_ref[here, :TILE] = block[2]
        edge_rows_ref[here, TILE:] = block[3][:, :rest]
        edge_cols_ref[here, TILE:] = block[3][:, rest:]
        weight_ref[here, TILE:] = block[4][:, :rest]
    for ref in (edge_rows_ref, edge_cols_ref, weight_ref):
        ref[dummy:, :] = jnp.zeros_like(ref[dummy:, :])
    copy.wait()

    code_ref[code_ref.shape[0] - EXTRA + N_CORE] = core
    used = jnp.int32(0)
    for part in range(N_CORE):
        column_core = core if part == 0 else 1 - core
        for column_y in range(N_Y):
            index = column_y * N_CORE + column_core

            count = slots_ref[index * 8 + 1, rest]

            def scan(block, used, index=index):
                for i in range(BLOCK):
                    code = slots_ref[index * 8, rest + block * BLOCK + i]
                    code_ref[used] = code
                    used = used + (code >> FLAG_AT)
                return used

            used = lax.fori_loop(0, (count + BLOCK - 1) // BLOCK, scan, used)
        for extra in range(GROUP - 1):
            code_ref[used + extra] = dummy
        used = (used + GROUP - 1) // GROUP * GROUP
        code_ref[code_ref.shape[0] - EXTRA + part] = used

    positions = lax.broadcasted_iota(I32, (TILE, edges), 0).astype(F32)

    def store(group):
        place = group % 2
        here = pl.ds(group * GROUP, GROUP)
        return pltpu.make_async_copy(stage_ref.at[place], tiles_hbm.at[here], sems.at[place])

    def step(group, carry):
        @pl.when(group >= 2)
        def _():
            store(group - 2).wait()

        for i in range(GROUP):
            entry = group * GROUP + i
            slot = field(code_ref[entry], 0, SRC_AT)
            row_hot = jnp.where(positions == edge_rows_ref[pl.ds(slot, 1), :], 1.0, 0.0)
            col_hot = jnp.where(
                positions == edge_cols_ref[pl.ds(slot, 1), :], weight_ref[pl.ds(slot, 1), :], 0.0
            )
            built = lax.dot_general(
                row_hot.astype(BF16),
                col_hot.astype(BF16),
                (((1,), (1,)), ((), ())),
                preferred_element_type=F32,
            )
            stage_ref[group % 2, i] = built.astype(BF16)
        store(group).start()
        return carry

    groups = used // GROUP
    lax.fori_loop(0, groups, step, 0)
    for back in (2, 1):

        @pl.when(groups >= back)
        def _(back=back):
            store(groups - back).wait()


def forward_body(part, code_ref, tiles_hbm, feats_ref, *refs):
    *start_refs, out_ref, acc_ref, tiles_ref, sems = refs
    fetch_part(code_ref, part, tiles_hbm, tiles_ref, sems)
    acc_ref[...] = start_refs[0][...] if start_refs else jnp.zeros_like(acc_ref)

    def step(group, carry):
        fetch(tiles_hbm, tiles_ref, sems, group).wait()
        products = []
        for i in range(GROUP):
            entry = group * GROUP + i
            source = field(code_ref[entry], SRC_AT, ZL_AT)
            products.append(
                jnp.dot(tiles_ref[entry], feats_ref[source], preferred_element_type=F32)
            )
        for i in range(GROUP):
            acc_ref[field(code_ref[group * GROUP + i], ZL_AT, FLAG_AT)] += products[i]
        return carry

    lax.fori_loop(*part_groups(code_ref, part), step, 0)
    out_ref[...] = acc_ref[...].astype(out_ref.dtype)


def dense_body(
    z2_ref, own_ref, other_ref, weight_ref, up_ref, other_up_ref, act_ref, send_ref, *, scale
):
    first = z2_ref[0] == 0
    total = own_ref[...].astype(F32) + other_ref[...].astype(F32)
    aggregated = total.reshape(N_Z2 * TILE, TILE).astype(BF16)
    weight = weight_ref[...]
    own_up, other_up = up_ref[...], other_up_ref[...]
    up = jnp.concatenate(
        [jnp.where(first, own_up, other_up), jnp.where(first, other_up, own_up)], axis=0
    )
    pre_act = jnp.dot(aggregated, weight, preferred_element_type=F32)
    gate = jax.nn.sigmoid(pre_act)
    act = (pre_act * gate).astype(BF16)
    act_ref[...] = jnp.where(first, act[:TILE], act[TILE:])
    grad_pre = (up.astype(F32) * gate * (1.0 + pre_act * (1.0 - gate))).astype(BF16)
    local_weight = (
        lax.dot_general(aggregated, grad_pre, (((0,), (0,)), ((), ())), preferred_element_type=F32)
        * scale
    ).astype(BF16)
    deep = TILE // N_Z4
    for z2 in range(N_Z2):
        grad_agg = lax.dot_general(
            weight,
            grad_pre[z2 * TILE : (z2 + 1) * TILE],
            (((1,), (1,)), ((), ())),
            preferred_element_type=F32,
        ).astype(BF16)
        for peer in range(N_Z4):
            send_ref[peer, z2 * TILE : (z2 + 1) * TILE, :] = grad_agg
    for peer in range(N_Z4):
        here = slice(peer * deep, (peer + 1) * deep)
        send_ref[peer, N_Z2 * TILE : N_Z2 * TILE + deep, :] = local_weight[here, :TILE]
        send_ref[peer, N_Z2 * TILE + deep :, :] = local_weight[here, TILE:]


def backward_tiles(part, code_ref, tiles_hbm, got_ref, acc_ref, tiles_ref, sems):
    fetch_part(code_ref, part, tiles_hbm, tiles_ref, sems)
    acc_ref[...] = jnp.zeros_like(acc_ref)

    def step(group, carry):
        fetch(tiles_hbm, tiles_ref, sems, group).wait()
        products = []
        for i in range(GROUP):
            entry = group * GROUP + i
            place = field(code_ref[entry], ZL_AT, FLAG_AT)
            start = pl.multiple_of(place % N_Z2 * TILE, TILE)
            grad = got_ref[place // N_Z2, pl.ds(start, TILE), :]
            products.append(jnp.dot(grad, tiles_ref[entry], preferred_element_type=F32))
        for i in range(GROUP):
            acc_ref[field(code_ref[group * GROUP + i], SRC_AT, ZL_AT)] += products[i]
        return carry

    lax.fori_loop(*part_groups(code_ref, part), step, 0)


def own_core(code_ref):
    return code_ref[code_ref.shape[0] - EXTRA + N_CORE]


def weight_half(got_ref, core):
    terms = jnp.sum(got_ref[:, N_Z2 * TILE :, :].astype(F32), axis=0)
    return jnp.where(core == 0, terms[:W_HALF], terms[W_HALF:])


def backward_other_body(
    code_ref, tiles_hbm, got_ref, send_ref, acc_ref, tiles_ref, sems
):
    backward_tiles(1, code_ref, tiles_hbm, got_ref, acc_ref, tiles_ref, sems)
    tiles = acc_ref.shape[0]
    send_ref[0:tiles] = acc_ref[...].astype(BF16)
    high, low = halves(weight_half(got_ref, 1 - own_core(code_ref)))
    send_ref[tiles, 0:W_HALF, :] = high
    send_ref[tiles, W_HALF : 2 * W_HALF, :] = low
    send_ref[tiles, 2 * W_HALF :, :] = jnp.zeros_like(send_ref[tiles, 2 * W_HALF :, :])


def backward_own_body(
    code_ref, tiles_hbm, got_ref, keep_ref, keep_weight_ref, tiles_ref, sems
):
    backward_tiles(0, code_ref, tiles_hbm, got_ref, keep_ref, tiles_ref, sems)
    keep_weight_ref[...] = weight_half(got_ref, own_core(code_ref))


def merge_body(zh_ref, got_ref, keep_ref, keep_weight_ref, send_ref, send_own_ref):
    zh = zh_ref[0]
    tiles = keep_ref.shape[0]
    terms = got_ref[tiles, 0 : 2 * W_HALF, :].astype(F32)
    part = (keep_weight_ref[...] + (terms[:W_HALF] + terms[W_HALF:])).astype(BF16)
    for peer in range(PLANE):
        own, other = peer * N_ZH + zh, peer * N_ZH + 1 - zh
        send_ref[peer, 0:TILE, :] = (keep_ref[other] + got_ref[other].astype(F32)).astype(BF16)
        send_ref[peer, TILE:, :] = part
        send_own_ref[peer] = (keep_ref[own] + got_ref[own].astype(F32)).astype(BF16)


def halfway_body(got_ref, send_ref):
    total = jnp.sum(got_ref[...].astype(F32), axis=0)
    send_ref[0:TILE, :] = total[:TILE].astype(BF16)
    high, low = halves(total[TILE:])
    send_ref[TILE : TILE + W_HALF, :] = high
    send_ref[TILE + W_HALF :, :] = low


def last_sum_body(got_ref, sent_ref, send_ref):
    terms = got_ref[TILE:, :].astype(F32), sent_ref[TILE:, :].astype(F32)
    total = (terms[0][:W_HALF] + terms[0][W_HALF:]) + (terms[1][:W_HALF] + terms[1][W_HALF:])
    for peer in range(N_Z4 * N_CORE):
        send_ref[peer] = total


def finish_body(got_ref, got_own_ref, grad_ref):
    total = jnp.sum(got_own_ref[...].astype(F32), axis=0)
    grad_ref[...] = (total + got_ref[0:TILE, :].astype(F32)).T.astype(BF16)


def place_body(got_ref, grad_weight_ref):
    for z4 in range(N_Z4):
        for core in range(N_CORE):
            grad_weight_ref[
                z4 * W_HALF : (z4 + 1) * W_HALF, core * TILE : (core + 1) * TILE
            ] = got_ref[z4 * N_CORE + core]


def swap(value, axis):
    return lax.ppermute(value, axis, [(0, 1), (1, 0)])


def exchange(value, axis):
    return lax.all_to_all(value, axis, 0, 0, tiled=True)


def local(
    features, weight, upstream, tile_rows, tile_cols, tile_count, edge_rows, edge_cols, edge_weight
):
    width = features.shape[2]
    hidden = weight.shape[1]
    slots, edges = edge_rows.shape[2:]
    column_tiles = PLANE * N_ZH
    most = slots + (LISTS - 1) * slots // 2 + 2 * GROUP
    tile_room = [pltpu.VMEM((most, TILE, TILE), BF16), pltpu.SemaphoreType.DMA((most // GROUP,))]
    zh = lax.axis_index("zh")
    where = jnp.stack([lax.axis_index("y"), lax.axis_index("core")]).astype(I32)

    own = features[0]
    other = swap(own, "zh")

    send = call(
        pack_body,
        shape((LISTS, 5 * slots, TILE), BF16),
        [hbm] * 5 + [smem],
        scratch=[
            pltpu.VMEM((slots, edges), I32),
            pltpu.VMEM((slots, edges), I32),
            pltpu.VMEM((slots, edges), BF16),
            pltpu.VMEM((1, slots), I32),
            pltpu.VMEM((1, slots), I32),
            pltpu.SemaphoreType.DMA((5,)),
        ],
        limit=PACK,
    )(edge_rows[0, 0], edge_cols[0, 0], edge_weight[0, 0], tile_rows[0], tile_cols[0], tile_count)
    lists = exchange(send, ("y", "core"))
    other, lists = lax.optimization_barrier((other, lists))
    tiles, codes = call(
        build_body,
        (shape((most, TILE, TILE), BF16), shape((most + EXTRA,), I32)),
        [smem, vmem],
        (hbm, smem),
        [pltpu.VMEM((LISTS * slots + 8, edges), F32)] * 3
        + [
            pltpu.VMEM((LISTS * 8, TILE), I32),
            pltpu.SMEM((LISTS * 8, TILE), I32),
            pltpu.SemaphoreType.DMA,
            pltpu.VMEM((2, GROUP, TILE, TILE), BF16),
            pltpu.SemaphoreType.DMA((2,)),
        ],
        flops=slots * TILE * TILE * edges * 4,
        moved=slots * TILE * TILE * 2,
        limit=LARGE,
    )(where, lists)

    zh_here = zh.astype(I32)[None]
    pair = call(pair_body, shape((PLANE, N_ZH, TILE, width), BF16), [smem, vmem, vmem])(
        zh_here, own, other
    )
    pair, up = lax.optimization_barrier((pair, upstream[0]))
    mine = exchange(pair, ("x", "y")).reshape(column_tiles, TILE, width)
    mine, codes, other_up = lax.optimization_barrier((mine, codes, swap(up, "z2")))
    theirs = swap(mine, "core")

    work = dict(flops=slots * TILE * TILE * width, moved=slots * TILE * TILE, limit=LARGE)
    sums = (N_ZL, TILE, width)
    partial = call(
        functools.partial(forward_body, 0),
        shape(sums, F32),
        [smem, hbm, vmem],
        scratch=[pltpu.VMEM(sums, F32)] + tile_room,
        **work,
    )(codes, tiles, mine)
    partial = call(
        functools.partial(forward_body, 1),
        shape(sums, BF16),
        [smem, hbm, vmem, vmem],
        scratch=[pltpu.VMEM(sums, F32)] + tile_room,
        **work,
    )(codes, tiles, theirs, partial)

    got = exchange(partial, "z4").reshape((N_Z4, N_Z2, TILE, width))
    partial = jnp.sum(got.astype(F32), axis=0).astype(BF16)

    node_total = features.shape[1] * N_X * N_ZH * N_Y * N_ZL * N_CORE
    out_act, send = call(
        functools.partial(dense_body, scale=1.0 / math.sqrt(node_total)),
        (shape((TILE, hidden), BF16), shape((N_Z4, N_Z2 * TILE + W_ROWS, TILE), BF16)),
        [smem] + [vmem] * 5,
    )(
        lax.axis_index("z2").astype(I32)[None],
        partial,
        swap(partial, "z2"),
        weight,
        up,
        other_up,
    )

    got = exchange(send, "z4")
    sums = (column_tiles, width, TILE)
    send = call(
        backward_other_body,
        shape((column_tiles + 1, width, TILE), BF16),
        [smem, hbm, vmem],
        scratch=[pltpu.VMEM(sums, F32)] + tile_room,
        **work,
    )(codes, tiles, got)
    keep, keep_weight = call(
        backward_own_body,
        (shape(sums, F32), shape((W_HALF, TILE), F32)),
        [smem, hbm, vmem],
        scratch=tile_room,
        **work,
    )(codes, tiles, got)

    send, send_own = call(
        merge_body,
        (shape((PLANE, TILE + W_HALF, TILE), BF16), shape((PLANE, TILE, TILE), BF16)),
        [smem] + [vmem] * 3,
    )(zh_here, swap(send, "core"), keep, keep_weight)
    got = exchange(send, ("x", "y"))
    got, send_own = lax.optimization_barrier((got, send_own))
    got_own = exchange(send_own, ("x", "y"))
    send = call(halfway_body, shape((TILE + 2 * W_HALF, TILE), BF16), [vmem])(got)
    got = swap(send, "zh")
    send_weight = call(last_sum_body, shape((N_Z4 * N_CORE, W_HALF, TILE), F32), [vmem] * 2)(
        got, send
    )
    got_weight = exchange(send_weight, ("z4", "core"))
    grad_features = call(finish_body, shape((TILE, width), BF16), [vmem] * 2)(got, got_own)
    grad_weight = call(place_body, shape((width, hidden), F32), [vmem])(got_weight)
    return (out_act[None], grad_features[None], grad_weight)


def solution(mesh):
    fine = Mesh(mesh.devices.reshape([size for _, size in FINE]), [name for name, _ in FINE])
    in_specs = (
        P(COL, ROW, None),
        P(),
        P(COL, ROW, None),
        P(ROW, COL, None),
        P(ROW, COL, None),
        P(ROW, COL),
        P(ROW, COL, None, None),
        P(ROW, COL, None, None),
        P(ROW, COL, None, None),
    )
    out_specs = (P(COL, ROW, None), P(COL, ROW, None), P())
    return jax.shard_map(local, mesh=fine, in_specs=in_specs, out_specs=out_specs, check_vma=False)
```

```python
import functools
import math

import jax
import jax.numpy as jnp
from jax import lax
from jax.experimental import pallas as pl
from jax.experimental.pallas import tpu as pltpu
from jax.sharding import Mesh
from jax.sharding import PartitionSpec as P

TILE = 128
GROUP = 16
BLOCK = 8
SRC_AT, ZL_AT, FLAG_AT = 10, 15, 18
NEAR = 4
EXTRA = 8
FINE = (("x", 4), ("zh", 2), ("y", 4), ("z2", 2), ("z4", 4), ("core", 2))
N_X, N_ZH, N_Y, N_Z2, N_Z4, N_CORE = (size for _, size in FINE)
N_ZL = N_Z2 * N_Z4
ROW = ("x", "zh")
COL = ("y", "z2", "z4", "core")
LISTS = N_Y * N_CORE
PLANE = N_X * N_Y
PACK = 62
LARGE = 46
W_ROWS = 64
W_HALF = W_ROWS // N_CORE
BF16 = jnp.bfloat16
F32 = jnp.float32
I32 = jnp.int32

vmem = pl.BlockSpec(memory_space=pltpu.VMEM)
smem = pl.BlockSpec(memory_space=pltpu.SMEM)
hbm = pl.BlockSpec(memory_space=pltpu.HBM)
shape = jax.ShapeDtypeStruct


def call(body, outs, in_specs, out_specs=None, scratch=(), flops=0, moved=0, limit=24):
    return pl.pallas_call(
        body,
        out_shape=outs,
        in_specs=in_specs,
        out_specs=jax.tree.map(lambda _: vmem, outs) if out_specs is None else out_specs,
        scratch_shapes=list(scratch),
        compiler_params=pltpu.CompilerParams(vmem_limit_bytes=limit * 1024 * 1024),
        cost_estimate=pl.CostEstimate(flops=flops, bytes_accessed=moved, transcendentals=0),
    )


def halves(value):
    high = value.astype(BF16)
    return high, (value - high.astype(F32)).astype(BF16)


def pair_body(zh_ref, own_ref, other_ref, send_ref):
    mine = zh_ref[0] == 0
    own, other = own_ref[...], other_ref[...]
    first, second = jnp.where(mine, own, other), jnp.where(mine, other, own)
    for peer in range(PLANE):
        send_ref[peer, 0] = first
        send_ref[peer, 1] = second


def pack_body(
    rows_hbm, cols_hbm, weight_hbm, row_hbm, col_hbm, count_ref, send_ref,
    rows_ref, cols_ref, weight_ref, row_ref, col_ref, sems,
):
    copies = [
        pltpu.make_async_copy(source, target, sems.at[k])
        for k, (source, target) in enumerate(
            (
                (rows_hbm, rows_ref),
                (cols_hbm, cols_ref),
                (weight_hbm, weight_ref),
                (row_hbm, row_ref),
                (col_hbm, col_ref),
            )
        )
    ]
    for copy in copies:
        copy.start()
    for copy in copies:
        copy.wait()
    slots, edges = rows_ref.shape
    rows = rows_ref[...].astype(F32)
    cols = cols_ref[...].astype(F32)
    weight = weight_ref[...].astype(F32)
    line = lax.broadcasted_iota(I32, (slots, slots), 0)
    meta = jnp.where(line == 0, row_ref[...], jnp.where(line == 1, col_ref[...], count_ref[0, 0]))
    blocks = (
        rows[:, :TILE],
        cols[:, :TILE],
        weight[:, :TILE],
        jnp.concatenate([rows[:, TILE:], cols[:, TILE:]], axis=1),
        jnp.concatenate([weight[:, TILE:], meta.astype(F32)], axis=1),
    )
    for k, block in enumerate(blocks):
        block = block.astype(BF16)
        for peer in range(send_ref.shape[0]):
            send_ref[peer, k * slots : (k + 1) * slots, :] = block


def field(code, at, until):
    return (code >> at) & ((1 << (until - at)) - 1)


def fetch(tiles_hbm, tiles_ref, sems, group):
    here = pl.ds(group * GROUP, GROUP)
    return pltpu.make_async_copy(tiles_hbm.at[here], tiles_ref.at[here], sems.at[group])


def part_groups(code_ref, part):
    ends = code_ref.shape[0] - EXTRA
    first = 0 if part == 0 else code_ref[ends] // GROUP
    return first, code_ref[ends + part] // GROUP


def split_loops(first, last, near_step, far_step):
    lax.fori_loop(jnp.minimum(first, NEAR), jnp.minimum(last, NEAR), near_step, 0)
    lax.fori_loop(jnp.maximum(first, NEAR), jnp.maximum(last, NEAR), far_step, 0)


def part_loops(code_ref, part, near_ref, tiles_hbm, tiles_ref, sems, prepare, step):
    first, last = part_groups(code_ref, part)

    def start(group, carry):
        fetch(tiles_hbm, tiles_ref, sems, group).start()
        return carry

    def far_step(group, carry):
        fetch(tiles_hbm, tiles_ref, sems, group).wait()
        return step(tiles_ref, group, carry)

    lax.fori_loop(jnp.maximum(first, NEAR), jnp.maximum(last, NEAR), start, 0)
    prepare()
    split_loops(first, last, functools.partial(step, near_ref), far_step)


def build_body(
    where_ref, got_ref, near_ref, tiles_hbm, code_ref,
    edge_rows_ref, edge_cols_ref, weight_ref, meta_ref, slots_ref, sem, stage_ref, sems,
):
    y, core = where_ref[0], where_ref[1]
    slots = got_ref.shape[1] // 5
    edges = edge_rows_ref.shape[1]
    rest = edges - TILE
    dummy = LISTS * slots
    lane = lax.broadcasted_iota(I32, (1, TILE), 1) - rest
    for index in range(LISTS):
        meta = got_ref[index, 4 * slots : 4 * slots + 16, :].astype(F32).astype(I32)
        row, col, count = meta[0:1], meta[1:2], meta[2:3]
        near = row >> 1
        place = (near & (N_Z4 - 1)) * N_Z2 + (near >> 2 & 1)
        source = ((col >> 1) * N_Y + index // N_CORE) * N_ZH + (col & 1)
        mine = (near >> 3 == y) & (row & 1 == core) & (lane < count)
        code = (index * slots + lane) + (source << SRC_AT) + (place << ZL_AT)
        meta_ref[index * 8 : index * 8 + 1, :] = code + jnp.where(mine, 1 << FLAG_AT, 0)
        meta_ref[index * 8 + 1 : index * 8 + 2, :] = count
    copy = pltpu.make_async_copy(meta_ref, slots_ref, sem)
    copy.start()
    for index in range(LISTS):
        here = slice(index * slots, (index + 1) * slots)
        block = [got_ref[index, k * slots : (k + 1) * slots, :].astype(F32) for k in range(5)]
        edge_rows_ref[here, :TILE] = block[0]
        edge_cols_ref[here, :TILE] = block[1]
        weight_ref[here, :TILE] = block[2]
        edge_rows_ref[here, TILE:] = block[3][:, :rest]
        edge_cols_ref[here, TILE:] = block[3][:, rest:]
        weight_ref[here, TILE:] = block[4][:, :rest]
    for ref in (edge_rows_ref, edge_cols_ref, weight_ref):
        ref[dummy:, :] = jnp.zeros_like(ref[dummy:, :])
    copy.wait()

    code_ref[code_ref.shape[0] - EXTRA + N_CORE] = core
    used = jnp.int32(0)
    for part in range(N_CORE):
        column_core = core if part == 0 else 1 - core
        for column_y in range(N_Y):
            index = column_y * N_CORE + column_core

            count = slots_ref[index * 8 + 1, rest]

            def scan(block, used, index=index):
                for i in range(BLOCK):
                    code = slots_ref[index * 8, rest + block * BLOCK + i]
                    code_ref[used] = code
                    used = used + (code >> FLAG_AT)
                return used

            used = lax.fori_loop(0, (count + BLOCK - 1) // BLOCK, scan, used)
        for extra in range(GROUP - 1):
            code_ref[used + extra] = dummy
        used = (used + GROUP - 1) // GROUP * GROUP
        code_ref[code_ref.shape[0] - EXTRA + part] = used

    positions = lax.broadcasted_iota(I32, (TILE, edges), 0).astype(F32)

    def store(group):
        place = group % 2
        here = pl.ds(group * GROUP, GROUP)
        return pltpu.make_async_copy(stage_ref.at[place], tiles_hbm.at[here], sems.at[place])

    def make(entry):
        slot = field(code_ref[entry], 0, SRC_AT)
        row_hot = jnp.where(positions == edge_rows_ref[pl.ds(slot, 1), :], 1.0, 0.0)
        col_hot = jnp.where(
            positions == edge_cols_ref[pl.ds(slot, 1), :], weight_ref[pl.ds(slot, 1), :], 0.0
        )
        built = lax.dot_general(
            row_hot.astype(BF16),
            col_hot.astype(BF16),
            (((1,), (1,)), ((), ())),
            preferred_element_type=F32,
        )
        return built.astype(BF16)

    def near_step(group, carry):
        for i in range(GROUP):
            near_ref[group * GROUP + i] = make(group * GROUP + i)
        return carry

    def far_step(group, carry):
        @pl.when(group >= NEAR + 2)
        def _():
            store(group - 2).wait()

        for i in range(GROUP):
            stage_ref[group % 2, i] = make(group * GROUP + i)
        store(group).start()
        return carry

    groups = used // GROUP
    split_loops(0, groups, near_step, far_step)
    for back in (2, 1):

        @pl.when(groups >= NEAR + back)
        def _(back=back):
            store(groups - back).wait()


def forward_body(part, code_ref, near_ref, tiles_hbm, feats_ref, *refs):
    *start_refs, out_ref, acc_ref, tiles_ref, sems = refs

    def prepare():
        acc_ref[...] = start_refs[0][...] if start_refs else jnp.zeros_like(acc_ref)

    def step(from_ref, group, carry):
        products = []
        for i in range(GROUP):
            entry = group * GROUP + i
            source = field(code_ref[entry], SRC_AT, ZL_AT)
            products.append(jnp.dot(from_ref[entry], feats_ref[source], preferred_element_type=F32))
        for i in range(GROUP):
            acc_ref[field(code_ref[group * GROUP + i], ZL_AT, FLAG_AT)] += products[i]
        return carry

    part_loops(code_ref, part, near_ref, tiles_hbm, tiles_ref, sems, prepare, step)
    out_ref[...] = acc_ref[...].astype(out_ref.dtype)


def dense_body(
    z2_ref, own_ref, other_ref, weight_ref, up_ref, other_up_ref, act_ref, send_ref, *, scale
):
    first = z2_ref[0] == 0
    total = own_ref[...].astype(F32) + other_ref[...].astype(F32)
    aggregated = total.reshape(N_Z2 * TILE, TILE).astype(BF16)
    weight = weight_ref[...]
    own_up, other_up = up_ref[...], other_up_ref[...]
    up = jnp.concatenate(
        [jnp.where(first, own_up, other_up), jnp.where(first, other_up, own_up)], axis=0
    )
    pre_act = jnp.dot(aggregated, weight, preferred_element_type=F32)
    gate = jax.nn.sigmoid(pre_act)
    act = (pre_act * gate).astype(BF16)
    act_ref[...] = jnp.where(first, act[:TILE], act[TILE:])
    grad_pre = (up.astype(F32) * gate * (1.0 + pre_act * (1.0 - gate))).astype(BF16)
    local_weight = (
        lax.dot_general(aggregated, grad_pre, (((0,), (0,)), ((), ())), preferred_element_type=F32)
        * scale
    ).astype(BF16)
    deep = TILE // N_Z4
    for z2 in range(N_Z2):
        grad_agg = lax.dot_general(
            weight,
            grad_pre[z2 * TILE : (z2 + 1) * TILE],
            (((1,), (1,)), ((), ())),
            preferred_element_type=F32,
        ).astype(BF16)
        for peer in range(N_Z4):
            send_ref[peer, z2 * TILE : (z2 + 1) * TILE, :] = grad_agg
    for peer in range(N_Z4):
        here = slice(peer * deep, (peer + 1) * deep)
        send_ref[peer, N_Z2 * TILE : N_Z2 * TILE + deep, :] = local_weight[here, :TILE]
        send_ref[peer, N_Z2 * TILE + deep :, :] = local_weight[here, TILE:]


def backward_tiles(part, code_ref, near_ref, tiles_hbm, got_ref, acc_ref, tiles_ref, sems):
    def prepare():
        acc_ref[...] = jnp.zeros_like(acc_ref)

    def step(from_ref, group, carry):
        products = []
        for i in range(GROUP):
            entry = group * GROUP + i
            place = field(code_ref[entry], ZL_AT, FLAG_AT)
            start = pl.multiple_of(place % N_Z2 * TILE, TILE)
            grad = got_ref[place // N_Z2, pl.ds(start, TILE), :]
            products.append(jnp.dot(grad, from_ref[entry], preferred_element_type=F32))
        for i in range(GROUP):
            acc_ref[field(code_ref[group * GROUP + i], SRC_AT, ZL_AT)] += products[i]
        return carry

    part_loops(code_ref, part, near_ref, tiles_hbm, tiles_ref, sems, prepare, step)


def own_core(code_ref):
    return code_ref[code_ref.shape[0] - EXTRA + N_CORE]


def weight_half(got_ref, core):
    terms = jnp.sum(got_ref[:, N_Z2 * TILE :, :].astype(F32), axis=0)
    return jnp.where(core == 0, terms[:W_HALF], terms[W_HALF:])


def backward_other_body(
    code_ref, near_ref, tiles_hbm, got_ref, send_ref, acc_ref, tiles_ref, sems
):
    backward_tiles(1, code_ref, near_ref, tiles_hbm, got_ref, acc_ref, tiles_ref, sems)
    tiles = acc_ref.shape[0]
    send_ref[0:tiles] = acc_ref[...].astype(BF16)
    high, low = halves(weight_half(got_ref, 1 - own_core(code_ref)))
    send_ref[tiles, 0:W_HALF, :] = high
    send_ref[tiles, W_HALF : 2 * W_HALF, :] = low
    send_ref[tiles, 2 * W_HALF :, :] = jnp.zeros_like(send_ref[tiles, 2 * W_HALF :, :])


def backward_own_body(
    code_ref, near_ref, tiles_hbm, got_ref, keep_ref, keep_weight_ref, tiles_ref, sems
):
    backward_tiles(0, code_ref, near_ref, tiles_hbm, got_ref, keep_ref, tiles_ref, sems)
    keep_weight_ref[...] = weight_half(got_ref, own_core(code_ref))


def merge_body(zh_ref, got_ref, keep_ref, keep_weight_ref, send_ref, send_own_ref):
    zh = zh_ref[0]
    tiles = keep_ref.shape[0]
    terms = got_ref[tiles, 0 : 2 * W_HALF, :].astype(F32)
    part = (keep_weight_ref[...] + (terms[:W_HALF] + terms[W_HALF:])).astype(BF16)
    for peer in range(PLANE):
        own, other = peer * N_ZH + zh, peer * N_ZH + 1 - zh
        send_ref[peer, 0:TILE, :] = (keep_ref[other] + got_ref[other].astype(F32)).astype(BF16)
        send_ref[peer, TILE:, :] = part
        send_own_ref[peer] = (keep_ref[own] + got_ref[own].astype(F32)).astype(BF16)


def halfway_body(got_ref, send_ref):
    total = jnp.sum(got_ref[...].astype(F32), axis=0)
    send_ref[0:TILE, :] = total[:TILE].astype(BF16)
    high, low = halves(total[TILE:])
    send_ref[TILE : TILE + W_HALF, :] = high
    send_ref[TILE + W_HALF :, :] = low


def last_sum_body(got_ref, sent_ref, send_ref):
    terms = got_ref[TILE:, :].astype(F32), sent_ref[TILE:, :].astype(F32)
    total = (terms[0][:W_HALF] + terms[0][W_HALF:]) + (terms[1][:W_HALF] + terms[1][W_HALF:])
    for peer in range(N_Z4 * N_CORE):
        send_ref[peer] = total


def finish_body(got_ref, got_own_ref, grad_ref):
    total = jnp.sum(got_own_ref[...].astype(F32), axis=0)
    grad_ref[...] = (total + got_ref[0:TILE, :].astype(F32)).T.astype(BF16)


def place_body(got_ref, grad_weight_ref):
    for z4 in range(N_Z4):
        for core in range(N_CORE):
            grad_weight_ref[
                z4 * W_HALF : (z4 + 1) * W_HALF, core * TILE : (core + 1) * TILE
            ] = got_ref[z4 * N_CORE + core]


def swap(value, axis):
    return lax.ppermute(value, axis, [(0, 1), (1, 0)])


def exchange(value, axis):
    return lax.all_to_all(value, axis, 0, 0, tiled=True)


def local(
    features, weight, upstream, tile_rows, tile_cols, tile_count, edge_rows, edge_cols, edge_weight
):
    width = features.shape[2]
    hidden = weight.shape[1]
    slots, edges = edge_rows.shape[2:]
    column_tiles = PLANE * N_ZH
    most = slots + (LISTS - 1) * slots // 2 + 2 * GROUP
    tile_room = [pltpu.VMEM((most, TILE, TILE), BF16), pltpu.SemaphoreType.DMA((most // GROUP,))]
    zh = lax.axis_index("zh")
    where = jnp.stack([lax.axis_index("y"), lax.axis_index("core")]).astype(I32)

    own = features[0]
    other = swap(own, "zh")

    send = call(
        pack_body,
        shape((LISTS, 5 * slots, TILE), BF16),
        [hbm] * 5 + [smem],
        scratch=[
            pltpu.VMEM((slots, edges), I32),
            pltpu.VMEM((slots, edges), I32),
            pltpu.VMEM((slots, edges), BF16),
            pltpu.VMEM((1, slots), I32),
            pltpu.VMEM((1, slots), I32),
            pltpu.SemaphoreType.DMA((5,)),
        ],
        limit=PACK,
    )(edge_rows[0, 0], edge_cols[0, 0], edge_weight[0, 0], tile_rows[0], tile_cols[0], tile_count)
    lists = exchange(send, ("y", "core"))
    other, lists = lax.optimization_barrier((other, lists))
    near, tiles, codes = call(
        build_body,
        (
            shape((NEAR * GROUP, TILE, TILE), BF16),
            shape((2 * most, TILE, TILE), BF16),
            shape((most + EXTRA,), I32),
        ),
        [smem, vmem],
        (vmem, hbm, smem),
        [pltpu.VMEM((LISTS * slots + 8, edges), F32)] * 3
        + [
            pltpu.VMEM((LISTS * 8, TILE), I32),
            pltpu.SMEM((LISTS * 8, TILE), I32),
            pltpu.SemaphoreType.DMA,
            pltpu.VMEM((2, GROUP, TILE, TILE), BF16),
            pltpu.SemaphoreType.DMA((2,)),
        ],
        flops=slots * TILE * TILE * edges * 4,
        moved=slots * TILE * TILE * 2,
        limit=LARGE,
    )(where, lists)

    zh_here = zh.astype(I32)[None]
    pair = call(pair_body, shape((PLANE, N_ZH, TILE, width), BF16), [smem, vmem, vmem])(
        zh_here, own, other
    )
    pair, up = lax.optimization_barrier((pair, upstream[0]))
    mine = exchange(pair, ("x", "y")).reshape(column_tiles, TILE, width)
    mine, codes, other_up = lax.optimization_barrier((mine, codes, swap(up, "z2")))
    theirs = swap(mine, "core")

    work = dict(flops=slots * TILE * TILE * width, moved=slots * TILE * TILE, limit=LARGE)
    sums = (N_ZL, TILE, width)
    partial = call(
        functools.partial(forward_body, 0),
        shape(sums, F32),
        [smem, vmem, hbm, vmem],
        scratch=[pltpu.VMEM(sums, F32)] + tile_room,
        **work,
    )(codes, near, tiles, mine)
    partial = call(
        functools.partial(forward_body, 1),
        shape(sums, BF16),
        [smem, vmem, hbm, vmem, vmem],
        scratch=[pltpu.VMEM(sums, F32)] + tile_room,
        **work,
    )(codes, near, tiles, theirs, partial)

    got = exchange(partial, "z4").reshape((N_Z4, N_Z2, TILE, width))
    partial = jnp.sum(got.astype(F32), axis=0).astype(BF16)

    node_total = features.shape[1] * N_X * N_ZH * N_Y * N_ZL * N_CORE
    out_act, send = call(
        functools.partial(dense_body, scale=1.0 / math.sqrt(node_total)),
        (shape((TILE, hidden), BF16), shape((N_Z4, N_Z2 * TILE + W_ROWS, TILE), BF16)),
        [smem] + [vmem] * 5,
    )(
        lax.axis_index("z2").astype(I32)[None],
        partial,
        swap(partial, "z2"),
        weight,
        up,
        other_up,
    )

    got = exchange(send, "z4")
    sums = (column_tiles, width, TILE)
    send = call(
        backward_other_body,
        shape((column_tiles + 1, width, TILE), BF16),
        [smem, vmem, hbm, vmem],
        scratch=[pltpu.VMEM(sums, F32)] + tile_room,
        **work,
    )(codes, near, tiles, got)
    keep, keep_weight = call(
        backward_own_body,
        (shape(sums, F32), shape((W_HALF, TILE), F32)),
        [smem, vmem, hbm, vmem],
        scratch=tile_room,
        **work,
    )(codes, near, tiles, got)

    send, send_own = call(
        merge_body,
        (shape((PLANE, TILE + W_HALF, TILE), BF16), shape((PLANE, TILE, TILE), BF16)),
        [smem] + [vmem] * 3,
    )(zh_here, swap(send, "core"), keep, keep_weight)
    got = exchange(send, ("x", "y"))
    got, send_own = lax.optimization_barrier((got, send_own))
    got_own = exchange(send_own, ("x", "y"))
    send = call(halfway_body, shape((TILE + 2 * W_HALF, TILE), BF16), [vmem])(got)
    got = swap(send, "zh")
    send_weight = call(last_sum_body, shape((N_Z4 * N_CORE, W_HALF, TILE), F32), [vmem] * 2)(
        got, send
    )
    got_weight = exchange(send_weight, ("z4", "core"))
    grad_features = call(finish_body, shape((TILE, width), BF16), [vmem] * 2)(got, got_own)
    grad_weight = call(place_body, shape((width, hidden), F32), [vmem])(got_weight)
    return (out_act[None], grad_features[None], grad_weight)


def solution(mesh):
    fine = Mesh(mesh.devices.reshape([size for _, size in FINE]), [name for name, _ in FINE])
    in_specs = (
        P(COL, ROW, None),
        P(),
        P(COL, ROW, None),
        P(ROW, COL, None),
        P(ROW, COL, None),
        P(ROW, COL),
        P(ROW, COL, None, None),
        P(ROW, COL, None, None),
        P(ROW, COL, None, None),
    )
    out_specs = (P(COL, ROW, None), P(COL, ROW, None), P())
    return jax.shard_map(local, mesh=fine, in_specs=in_specs, out_specs=out_specs, check_vma=False)
```

```python
import functools
import math

import jax
import jax.numpy as jnp
from jax import lax
from jax.experimental import pallas as pl
from jax.experimental.pallas import tpu as pltpu
from jax.sharding import Mesh
from jax.sharding import PartitionSpec as P

TILE = 128
GROUP = 16
BLOCK = 8
SRC_AT, ZL_AT, FLAG_AT = 10, 15, 18
NEAR = 4
EXTRA = 8
FINE = (("x", 4), ("zh", 2), ("y", 4), ("z2", 2), ("z4", 4), ("core", 2))
N_X, N_ZH, N_Y, N_Z2, N_Z4, N_CORE = (size for _, size in FINE)
N_ZL = N_Z2 * N_Z4
ROW = ("x", "zh")
COL = ("y", "z2", "z4", "core")
LISTS = N_Y * N_CORE
PLANE = N_X * N_Y
PACK = 62
LARGE = 46
W_ROWS = 64
W_HALF = W_ROWS // N_CORE
BF16 = jnp.bfloat16
F32 = jnp.float32
I32 = jnp.int32

vmem = pl.BlockSpec(memory_space=pltpu.VMEM)
smem = pl.BlockSpec(memory_space=pltpu.SMEM)
hbm = pl.BlockSpec(memory_space=pltpu.HBM)
shape = jax.ShapeDtypeStruct


def call(body, outs, in_specs, out_specs=None, scratch=(), flops=0, moved=0, limit=24):
    return pl.pallas_call(
        body,
        out_shape=outs,
        in_specs=in_specs,
        out_specs=jax.tree.map(lambda _: vmem, outs) if out_specs is None else out_specs,
        scratch_shapes=list(scratch),
        compiler_params=pltpu.CompilerParams(vmem_limit_bytes=limit * 1024 * 1024),
        cost_estimate=pl.CostEstimate(flops=flops, bytes_accessed=moved, transcendentals=0),
    )


def halves(value):
    high = value.astype(BF16)
    return high, (value - high.astype(F32)).astype(BF16)


def pair_body(zh_ref, own_ref, other_ref, send_ref):
    mine = zh_ref[0] == 0
    own, other = own_ref[...], other_ref[...]
    first, second = jnp.where(mine, own, other), jnp.where(mine, other, own)
    for peer in range(PLANE):
        send_ref[peer, 0] = first
        send_ref[peer, 1] = second


def pack_body(
    rows_hbm, cols_hbm, weight_hbm, row_hbm, col_hbm, count_ref, send_ref,
    rows_ref, cols_ref, weight_ref, row_ref, col_ref, sems,
):
    copies = [
        pltpu.make_async_copy(source, target, sems.at[k])
        for k, (source, target) in enumerate(
            (
                (rows_hbm, rows_ref),
                (cols_hbm, cols_ref),
                (weight_hbm, weight_ref),
                (row_hbm, row_ref),
                (col_hbm, col_ref),
            )
        )
    ]
    for copy in copies:
        copy.start()
    for copy in copies:
        copy.wait()
    slots, edges = rows_ref.shape
    rows = rows_ref[...].astype(F32)
    cols = cols_ref[...].astype(F32)
    weight = weight_ref[...].astype(F32)
    line = lax.broadcasted_iota(I32, (slots, slots), 0)
    meta = jnp.where(line == 0, row_ref[...], jnp.where(line == 1, col_ref[...], count_ref[0, 0]))
    blocks = (
        rows[:, :TILE],
        cols[:, :TILE],
        weight[:, :TILE],
        jnp.concatenate([rows[:, TILE:], cols[:, TILE:]], axis=1),
        jnp.concatenate([weight[:, TILE:], meta.astype(F32)], axis=1),
    )
    for k, block in enumerate(blocks):
        block = block.astype(BF16)
        for peer in range(send_ref.shape[0]):
            send_ref[peer, k * slots : (k + 1) * slots, :] = block


def field(code, at, until):
    return (code >> at) & ((1 << (until - at)) - 1)


def fetch(tiles_hbm, tiles_ref, sems, group):
    here = pl.ds(group * GROUP, GROUP)
    return pltpu.make_async_copy(tiles_hbm.at[here], tiles_ref.at[here], sems.at[group])


def part_groups(code_ref, part):
    ends = code_ref.shape[0] - EXTRA
    first = 0 if part == 0 else code_ref[ends] // GROUP
    return first, code_ref[ends + part] // GROUP


def split_loops(first, last, near_step, far_step):
    lax.fori_loop(jnp.minimum(first, NEAR), jnp.minimum(last, NEAR), near_step, 0)
    lax.fori_loop(jnp.maximum(first, NEAR), jnp.maximum(last, NEAR), far_step, 0)


def part_loops(code_ref, part, near_ref, tiles_hbm, tiles_ref, sems, prepare, step):
    first, last = part_groups(code_ref, part)

    def start(group, carry):
        fetch(tiles_hbm, tiles_ref, sems, group).start()
        return carry

    def far_step(group, carry):
        fetch(tiles_hbm, tiles_ref, sems, group).wait()
        return step(tiles_ref, group, carry)

    lax.fori_loop(jnp.maximum(first, NEAR), jnp.maximum(last, NEAR), start, 0)
    prepare()
    split_loops(first, last, functools.partial(step, near_ref), far_step)


def build_body(
    where_ref, got_ref, near_ref, tiles_hbm, code_ref,
    edge_rows_ref, edge_cols_ref, weight_ref, meta_ref, slots_ref, sem, stage_ref, sems,
):
    y, core = where_ref[0], where_ref[1]
    slots = got_ref.shape[1] // 5
    edges = edge_rows_ref.shape[1]
    rest = edges - TILE
    dummy = LISTS * slots
    lane = lax.broadcasted_iota(I32, (1, TILE), 1) - rest
    for index in range(LISTS):
        meta = got_ref[index, 4 * slots : 4 * slots + 16, :].astype(F32).astype(I32)
        row, col, count = meta[0:1], meta[1:2], meta[2:3]
        near = row >> 1
        place = (near & (N_Z4 - 1)) * N_Z2 + (near >> 2 & 1)
        source = ((col >> 1) * N_Y + index // N_CORE) * N_ZH + (col & 1)
        mine = (near >> 3 == y) & (row & 1 == core) & (lane < count)
        code = (index * slots + lane) + (source << SRC_AT) + (place << ZL_AT)
        meta_ref[index * 8 : index * 8 + 1, :] = code + jnp.where(mine, 1 << FLAG_AT, 0)
        meta_ref[index * 8 + 1 : index * 8 + 2, :] = count
    copy = pltpu.make_async_copy(meta_ref, slots_ref, sem)
    copy.start()
    for index in range(LISTS):
        here = slice(index * slots, (index + 1) * slots)
        block = [got_ref[index, k * slots : (k + 1) * slots, :].astype(F32) for k in range(5)]
        edge_rows_ref[here, :TILE] = block[0]
        edge_cols_ref[here, :TILE] = block[1]
        weight_ref[here, :TILE] = block[2]
        edge_rows_ref[here, TILE:] = block[3][:, :rest]
        edge_cols_ref[here, TILE:] = block[3][:, rest:]
        weight_ref[here, TILE:] = block[4][:, :rest]
    for ref in (edge_rows_ref, edge_cols_ref, weight_ref):
        ref[dummy:, :] = jnp.zeros_like(ref[dummy:, :])
    copy.wait()

    code_ref[code_ref.shape[0] - EXTRA + N_CORE] = core
    used = jnp.int32(0)
    for part in range(N_CORE):
        column_core = core if part == 0 else 1 - core
        for column_y in range(N_Y):
            index = column_y * N_CORE + column_core

            count = slots_ref[index * 8 + 1, rest]

            def scan(block, used, index=index):
                for i in range(BLOCK):
                    code = slots_ref[index * 8, rest + block * BLOCK + i]
                    code_ref[used] = code
                    used = used + (code >> FLAG_AT)
                return used

            used = lax.fori_loop(0, (count + BLOCK - 1) // BLOCK, scan, used)
        for extra in range(GROUP - 1):
            code_ref[used + extra] = dummy
        used = (used + GROUP - 1) // GROUP * GROUP
        code_ref[code_ref.shape[0] - EXTRA + part] = used

    positions = lax.broadcasted_iota(I32, (TILE, edges), 0).astype(F32)

    def store(group):
        place = group % 2
        here = pl.ds(group * GROUP, GROUP)
        return pltpu.make_async_copy(stage_ref.at[place], tiles_hbm.at[here], sems.at[place])

    def make(entry):
        slot = field(code_ref[entry], 0, SRC_AT)
        row_hot = jnp.where(positions == edge_rows_ref[pl.ds(slot, 1), :], 1.0, 0.0)
        col_hot = jnp.where(
            positions == edge_cols_ref[pl.ds(slot, 1), :], weight_ref[pl.ds(slot, 1), :], 0.0
        )
        built = lax.dot_general(
            row_hot.astype(BF16),
            col_hot.astype(BF16),
            (((1,), (1,)), ((), ())),
            preferred_element_type=F32,
        )
        return built.astype(BF16)

    def near_step(group, carry):
        for i in range(GROUP):
            near_ref[group * GROUP + i] = make(group * GROUP + i)
        return carry

    def far_step(group, carry):
        @pl.when(group >= NEAR + 2)
        def _():
            store(group - 2).wait()

        for i in range(GROUP):
            stage_ref[group % 2, i] = make(group * GROUP + i)
        store(group).start()
        return carry

    groups = used // GROUP
    split_loops(0, groups, near_step, far_step)
    for back in (2, 1):

        @pl.when(groups >= NEAR + back)
        def _(back=back):
            store(groups - back).wait()


def forward_body(part, code_ref, near_ref, tiles_hbm, feats_ref, *refs):
    *start_refs, out_ref, acc_ref, tiles_ref, sems = refs

    def prepare():
        acc_ref[...] = start_refs[0][...] if start_refs else jnp.zeros_like(acc_ref)

    def step(from_ref, group, carry):
        products = []
        for i in range(GROUP):
            entry = group * GROUP + i
            source = field(code_ref[entry], SRC_AT, ZL_AT)
            products.append(jnp.dot(from_ref[entry], feats_ref[source], preferred_element_type=F32))
        for i in range(GROUP):
            acc_ref[field(code_ref[group * GROUP + i], ZL_AT, FLAG_AT)] += products[i]
        return carry

    part_loops(code_ref, part, near_ref, tiles_hbm, tiles_ref, sems, prepare, step)
    out_ref[...] = acc_ref[...].astype(out_ref.dtype)


def dense_body(
    z2_ref, own_ref, other_ref, weight_ref, up_ref, other_up_ref, act_ref, send_ref, *, scale
):
    first = z2_ref[0] == 0
    total = own_ref[...].astype(F32) + other_ref[...].astype(F32)
    aggregated = total.reshape(N_Z2 * TILE, TILE).astype(BF16)
    weight = weight_ref[...]
    own_up, other_up = up_ref[...], other_up_ref[...]
    up = jnp.concatenate(
        [jnp.where(first, own_up, other_up), jnp.where(first, other_up, own_up)], axis=0
    )
    pre_act = jnp.dot(aggregated, weight, preferred_element_type=F32)
    gate = jax.nn.sigmoid(pre_act)
    act = (pre_act * gate).astype(BF16)
    act_ref[...] = jnp.where(first, act[:TILE], act[TILE:])
    grad_pre = (up.astype(F32) * gate * (1.0 + pre_act * (1.0 - gate))).astype(BF16)
    local_weight = (
        lax.dot_general(aggregated, grad_pre, (((0,), (0,)), ((), ())), preferred_element_type=F32)
        * scale
    ).astype(BF16)
    deep = TILE // N_Z4
    for z2 in range(N_Z2):
        grad_agg = lax.dot_general(
            weight,
            grad_pre[z2 * TILE : (z2 + 1) * TILE],
            (((1,), (1,)), ((), ())),
            preferred_element_type=F32,
        ).astype(BF16)
        for peer in range(N_Z4):
            send_ref[peer, z2 * TILE : (z2 + 1) * TILE, :] = grad_agg
    for peer in range(N_Z4):
        here = slice(peer * deep, (peer + 1) * deep)
        send_ref[peer, N_Z2 * TILE : N_Z2 * TILE + deep, :] = local_weight[here, :TILE]
        send_ref[peer, N_Z2 * TILE + deep :, :] = local_weight[here, TILE:]


def backward_tiles(part, code_ref, near_ref, tiles_hbm, got_ref, acc_ref, tiles_ref, sems):
    def prepare():
        acc_ref[...] = jnp.zeros_like(acc_ref)

    def step(from_ref, group, carry):
        products = []
        for i in range(GROUP):
            entry = group * GROUP + i
            place = field(code_ref[entry], ZL_AT, FLAG_AT)
            start = pl.multiple_of(place % N_Z2 * TILE, TILE)
            grad = got_ref[place // N_Z2, pl.ds(start, TILE), :]
            products.append(jnp.dot(grad, from_ref[entry], preferred_element_type=F32))
        for i in range(GROUP):
            acc_ref[field(code_ref[group * GROUP + i], SRC_AT, ZL_AT)] += products[i]
        return carry

    part_loops(code_ref, part, near_ref, tiles_hbm, tiles_ref, sems, prepare, step)


def own_core(code_ref):
    return code_ref[code_ref.shape[0] - EXTRA + N_CORE]


def weight_half(got_ref, core):
    terms = jnp.sum(got_ref[:, N_Z2 * TILE :, :].astype(F32), axis=0)
    return jnp.where(core == 0, terms[:W_HALF], terms[W_HALF:])


def backward_other_body(
    code_ref, near_ref, tiles_hbm, got_ref, send_ref, acc_ref, tiles_ref, sems
):
    backward_tiles(1, code_ref, near_ref, tiles_hbm, got_ref, acc_ref, tiles_ref, sems)
    tiles = acc_ref.shape[0]
    send_ref[0:tiles] = acc_ref[...].astype(BF16)
    high, low = halves(weight_half(got_ref, 1 - own_core(code_ref)))
    send_ref[tiles, 0:W_HALF, :] = high
    send_ref[tiles, W_HALF : 2 * W_HALF, :] = low
    send_ref[tiles, 2 * W_HALF :, :] = jnp.zeros_like(send_ref[tiles, 2 * W_HALF :, :])


def backward_own_body(
    code_ref, near_ref, tiles_hbm, got_ref, keep_ref, keep_weight_ref, tiles_ref, sems
):
    backward_tiles(0, code_ref, near_ref, tiles_hbm, got_ref, keep_ref, tiles_ref, sems)
    keep_weight_ref[...] = weight_half(got_ref, own_core(code_ref))


def merge_body(zh_ref, got_ref, keep_ref, keep_weight_ref, send_ref, send_own_ref):
    zh = zh_ref[0]
    tiles = keep_ref.shape[0]
    terms = got_ref[tiles, 0 : 2 * W_HALF, :].astype(F32)
    part = (keep_weight_ref[...] + (terms[:W_HALF] + terms[W_HALF:])).astype(BF16)
    for peer in range(PLANE):
        own, other = peer * N_ZH + zh, peer * N_ZH + 1 - zh
        send_ref[peer, 0:TILE, :] = (keep_ref[other] + got_ref[other].astype(F32)).astype(BF16)
        send_ref[peer, TILE:, :] = part
        send_own_ref[peer] = (keep_ref[own] + got_ref[own].astype(F32)).astype(BF16)


def halfway_body(got_ref, send_ref):
    send_ref[...] = jnp.sum(got_ref[...].astype(F32), axis=0)


def last_sum_body(got_ref, sent_ref, send_ref):
    total = got_ref[TILE:, :] + sent_ref[TILE:, :]
    for peer in range(N_Z4 * N_CORE):
        send_ref[peer] = total


def finish_body(got_ref, got_own_ref, grad_ref):
    total = jnp.sum(got_own_ref[...].astype(F32), axis=0)
    grad_ref[...] = (total + got_ref[0:TILE, :]).T.astype(BF16)


def place_body(got_ref, grad_weight_ref):
    for z4 in range(N_Z4):
        for core in range(N_CORE):
            grad_weight_ref[
                z4 * W_HALF : (z4 + 1) * W_HALF, core * TILE : (core + 1) * TILE
            ] = got_ref[z4 * N_CORE + core]


def swap(value, axis):
    return lax.ppermute(value, axis, [(0, 1), (1, 0)])


def exchange(value, axis):
    return lax.all_to_all(value, axis, 0, 0, tiled=True)


def local(
    features, weight, upstream, tile_rows, tile_cols, tile_count, edge_rows, edge_cols, edge_weight
):
    width = features.shape[2]
    hidden = weight.shape[1]
    slots, edges = edge_rows.shape[2:]
    column_tiles = PLANE * N_ZH
    most = slots + (LISTS - 1) * slots // 2 + 2 * GROUP
    tile_room = [pltpu.VMEM((most, TILE, TILE), BF16), pltpu.SemaphoreType.DMA((most // GROUP,))]
    zh = lax.axis_index("zh")
    where = jnp.stack([lax.axis_index("y"), lax.axis_index("core")]).astype(I32)

    own = features[0]
    other = swap(own, "zh")

    send = call(
        pack_body,
        shape((LISTS, 5 * slots, TILE), BF16),
        [hbm] * 5 + [smem],
        scratch=[
            pltpu.VMEM((slots, edges), I32),
            pltpu.VMEM((slots, edges), I32),
            pltpu.VMEM((slots, edges), BF16),
            pltpu.VMEM((1, slots), I32),
            pltpu.VMEM((1, slots), I32),
            pltpu.SemaphoreType.DMA((5,)),
        ],
        limit=PACK,
    )(edge_rows[0, 0], edge_cols[0, 0], edge_weight[0, 0], tile_rows[0], tile_cols[0], tile_count)
    lists = exchange(send, ("y", "core"))
    other, lists = lax.optimization_barrier((other, lists))
    near, tiles, codes = call(
        build_body,
        (
            shape((NEAR * GROUP, TILE, TILE), BF16),
            shape((2 * most, TILE, TILE), BF16),
            shape((most + EXTRA,), I32),
        ),
        [smem, vmem],
        (vmem, hbm, smem),
        [pltpu.VMEM((LISTS * slots + 8, edges), F32)] * 3
        + [
            pltpu.VMEM((LISTS * 8, TILE), I32),
            pltpu.SMEM((LISTS * 8, TILE), I32),
            pltpu.SemaphoreType.DMA,
            pltpu.VMEM((2, GROUP, TILE, TILE), BF16),
            pltpu.SemaphoreType.DMA((2,)),
        ],
        flops=slots * TILE * TILE * edges * 4,
        moved=slots * TILE * TILE * 2,
        limit=LARGE,
    )(where, lists)

    zh_here = zh.astype(I32)[None]
    pair = call(pair_body, shape((PLANE, N_ZH, TILE, width), BF16), [smem, vmem, vmem])(
        zh_here, own, other
    )
    pair, up = lax.optimization_barrier((pair, upstream[0]))
    mine = exchange(pair, ("x", "y")).reshape(column_tiles, TILE, width)
    mine, codes, other_up = lax.optimization_barrier((mine, codes, swap(up, "z2")))
    theirs = swap(mine, "core")

    work = dict(flops=slots * TILE * TILE * width, moved=slots * TILE * TILE, limit=LARGE)
    sums = (N_ZL, TILE, width)
    partial = call(
        functools.partial(forward_body, 0),
        shape(sums, F32),
        [smem, vmem, hbm, vmem],
        scratch=[pltpu.VMEM(sums, F32)] + tile_room,
        **work,
    )(codes, near, tiles, mine)
    partial = call(
        functools.partial(forward_body, 1),
        shape(sums, BF16),
        [smem, vmem, hbm, vmem, vmem],
        scratch=[pltpu.VMEM(sums, F32)] + tile_room,
        **work,
    )(codes, near, tiles, theirs, partial)

    got = exchange(partial, "z4").reshape((N_Z4, N_Z2, TILE, width))
    partial = jnp.sum(got.astype(F32), axis=0).astype(BF16)

    node_total = features.shape[1] * N_X * N_ZH * N_Y * N_ZL * N_CORE
    out_act, send = call(
        functools.partial(dense_body, scale=1.0 / math.sqrt(node_total)),
        (shape((TILE, hidden), BF16), shape((N_Z4, N_Z2 * TILE + W_ROWS, TILE), BF16)),
        [smem] + [vmem] * 5,
    )(
        lax.axis_index("z2").astype(I32)[None],
        partial,
        swap(partial, "z2"),
        weight,
        up,
        other_up,
    )

    got = exchange(send, "z4")
    sums = (column_tiles, width, TILE)
    send = call(
        backward_other_body,
        shape((column_tiles + 1, width, TILE), BF16),
        [smem, vmem, hbm, vmem],
        scratch=[pltpu.VMEM(sums, F32)] + tile_room,
        **work,
    )(codes, near, tiles, got)
    keep, keep_weight = call(
        backward_own_body,
        (shape(sums, F32), shape((W_HALF, TILE), F32)),
        [smem, vmem, hbm, vmem],
        scratch=tile_room,
        **work,
    )(codes, near, tiles, got)

    send, send_own = call(
        merge_body,
        (shape((PLANE, TILE + W_HALF, TILE), BF16), shape((PLANE, TILE, TILE), BF16)),
        [smem] + [vmem] * 3,
    )(zh_here, swap(send, "core"), keep, keep_weight)
    got = exchange(send, ("x", "y"))
    got, send_own = lax.optimization_barrier((got, send_own))
    got_own = exchange(send_own, ("x", "y"))
    send = call(halfway_body, shape((TILE + W_HALF, TILE), F32), [vmem])(got)
    got = swap(send, "zh")
    send_weight = call(last_sum_body, shape((N_Z4 * N_CORE, W_HALF, TILE), F32), [vmem] * 2)(
        got, send
    )
    got_weight = exchange(send_weight, ("z4", "core"))
    grad_features = call(finish_body, shape((TILE, width), BF16), [vmem] * 2)(got, got_own)
    grad_weight = call(place_body, shape((width, hidden), F32), [vmem])(got_weight)
    return (out_act[None], grad_features[None], grad_weight)


def solution(mesh):
    fine = Mesh(mesh.devices.reshape([size for _, size in FINE]), [name for name, _ in FINE])
    in_specs = (
        P(COL, ROW, None),
        P(),
        P(COL, ROW, None),
        P(ROW, COL, None),
        P(ROW, COL, None),
        P(ROW, COL),
        P(ROW, COL, None, None),
        P(ROW, COL, None, None),
        P(ROW, COL, None, None),
    )
    out_specs = (P(COL, ROW, None), P(COL, ROW, None), P())
    return jax.shard_map(local, mesh=fine, in_specs=in_specs, out_specs=out_specs, check_vma=False)
```
